512 devices in a mesh: grp: 4 (over x), blk: 128 (over z, y, core).
Axes of the slice: x: 4, y: 8, z: 8, core: 2. Of those that a mesh axis runs over, the one named last changes fastest.
Arguments:
- queries: bfloat16 [65536, 4096], P(('blk', 'grp')), may hold values from -150 to 150
- keys: bfloat16 [65536, 4096], P(('blk', 'grp')), may hold values from -4 to 4
- values: bfloat16 [65536, 4096], P(('blk', 'grp')), may hold values from -6 to 6
Outputs:
- attended: bfloat16 [65536, 4096], P(('blk', 'grp'))
The draws below stay inside these ranges and needn't reach their ends.
All inputs are finite; a program needn't handle non-finite values.
Results may differ from the reference program's by a relative error of at most 0.0033.
Values may be sent and summed in bfloat16 or wider, within the bound.
No kernel may reach another device: no remote copies, remote signals or barrier semaphores. Data moves between devices by JAX's collectives and lax.ppermute only.
A program may use at most 64 MiB of HBM per device.

```python
import math
import jax
import jax.numpy as jnp
from jax import lax

HD = 128
STRIDE = 32
D = 4096
SEG = 512
LENGTH = 65536


def shared_keys(key):
    return jnp.clip(jax.random.normal(key, (LENGTH, D), jnp.float32), -4.0, 4.0)


def draw_keys(key, part):
    return shared_keys(key).astype(jnp.bfloat16)


def draw_queries(key, part):
    key = jax.random.fold_in(key, 11)
    noise = jnp.clip(jax.random.normal(key, (LENGTH, D), jnp.float32), -4.0, 4.0)
    return noise.astype(jnp.bfloat16)


def levels(own_key, dims, pieces, smallest, largest):
    def one(position, shards_of):
        heights = jax.random.uniform(jax.random.fold_in(jax.random.fold_in(own_key, 6), position), (shards_of,), jnp.float32, smallest / len(pieces), largest / len(pieces))
        return jnp.repeat(jnp.exp(heights), dims[position] // shards_of).reshape((-1,) + (1,) * (len(dims) - position - 1))

    level = one(*pieces[0])
    for cut in pieces[1:]:
        level = level * one(*cut)
    return level


def bell_draw(key, dims, scale, reach, pieces=(), held_as=jnp.bfloat16):
    array = scale * jax.random.normal(key, dims, jnp.float32)
    if pieces:
        array = array * levels(key, dims, pieces, -0.22, 0.18)
    return jnp.clip(array, -reach, reach).astype(held_as)


def setup_inputs(seed: int = 0) -> dict:
    streams_of = jax.random.split(jax.random.key(seed), 4)
    queries = draw_queries(jax.random.fold_in(streams_of[3], 71), 0)
    keys = draw_keys(jax.random.fold_in(streams_of[3], 71), 0)
    values = bell_draw(streams_of[2], (LENGTH, D), 1.0, 6.0, ((0, 512),))
    return dict(queries=queries, keys=keys, values=values)


def rounded(weights):
    return lax.optimization_barrier(weights.astype(jnp.bfloat16)).astype(jnp.float32)

def softmax_rows(scores, visible):
    scores = jnp.where(visible, scores, -1e+30)
    maxima = lax.optimization_barrier(jnp.max(scores, axis=-1, keepdims=True))
    weights = jnp.where(visible, jnp.exp(scores - maxima), 0.0)
    return (weights, lax.optimization_barrier(jnp.sum(weights, axis=-1, keepdims=True)))

def reference(queries, keys, values):
    length, width = queries.shape
    quad_count = width // (4 * HD)
    row_count = length // STRIDE
    seg_rows = SEG // STRIDE
    segments = length // SEG
    head_count = quad_count * 2
    scaling = 1.0 / math.sqrt(HD)
    query_all = queries.astype(jnp.float32).reshape(row_count, STRIDE, quad_count, 4, HD)
    key_all = keys.astype(jnp.float32).reshape(row_count, STRIDE, quad_count, 4, HD)
    value_all = values.astype(jnp.float32).reshape(row_count, STRIDE, quad_count, 4, HD)
    places = jnp.arange(STRIDE, dtype=jnp.int32)
    causal = places[:, None] >= places[None, :]
    scores = jnp.einsum('rqah,rkah->raqk', query_all[:, :, :, 0], key_all[:, :, :, 0]) * scaling
    weights, totals = softmax_rows(scores, causal)
    row_out = jnp.einsum('raqk,rkah->rqah', rounded(weights), value_all[:, :, :, 0]) / totals.transpose(0, 2, 1, 3)
    all_rows = jnp.arange(row_count, dtype=jnp.int32)
    row_causal = all_rows[:, None] >= all_rows[None, :]

    def one_column(element):
        col_query, col_key, col_value = element
        col_scores = jnp.einsum('iah,jah->aij', col_query, col_key) * scaling
        col_weights, col_totals = softmax_rows(col_scores, row_causal)
        col_out = jnp.einsum('aij,jah->iah', rounded(col_weights), col_value)
        return col_out / col_totals.transpose(1, 0, 2)
    column_out = lax.map(one_column, (query_all[:, :, :, 1].transpose(1, 0, 2, 3), key_all[:, :, :, 1].transpose(1, 0, 2, 3), value_all[:, :, :, 1].transpose(1, 0, 2, 3)))
    column_out = column_out.transpose(1, 0, 2, 3)
    seg_places = jnp.arange(seg_rows, dtype=jnp.int32)
    fixed_query = query_all[:, :, :, 2:].reshape(segments, seg_rows, STRIDE, head_count, HD)
    fixed_key = key_all[:, :, :, 2:].reshape(segments, seg_rows, STRIDE, head_count, HD)
    fixed_value = value_all[:, :, :, 2:].reshape(segments, seg_rows, STRIDE, head_count, HD)
    summary_key = key_all[:, STRIDE - 1, :, 2:].reshape(row_count, head_count, HD)
    summary_value = value_all[:, STRIDE - 1, :, 2:].reshape(row_count, head_count, HD)
    key_rows = jnp.arange(row_count, dtype=jnp.int32)

    def one_segment(element):
        seg_query, seg_key, seg_value, seg_index = element
        own_scores = jnp.einsum('rqfh,rkfh->rfqk', seg_query, seg_key) * scaling
        far_scores = jnp.einsum('rqfh,kfh->rfqk', seg_query, summary_key) * scaling
        query_rows = seg_index * seg_rows + seg_places
        visible = (key_rows[None, :] < query_rows[:, None])[:, None, None, :]
        own_scores = jnp.where(causal, own_scores, -1e+30)
        far_scores = jnp.where(visible, far_scores, -1e+30)
        maxima = jnp.maximum(lax.optimization_barrier(jnp.max(own_scores, axis=-1)), lax.optimization_barrier(jnp.max(far_scores, axis=-1)))[..., None]
        own_weights = jnp.where(causal, jnp.exp(own_scores - maxima), 0.0)
        far_weights = jnp.where(visible, jnp.exp(far_scores - maxima), 0.0)
        totals_here = lax.optimization_barrier(jnp.sum(own_weights, axis=-1)) + lax.optimization_barrier(jnp.sum(far_weights, axis=-1))
        weighted = jnp.einsum('rfqk,rkfh->rfqh', rounded(own_weights), seg_value)
        weighted = weighted + jnp.einsum('rfqk,kfh->rfqh', rounded(far_weights), summary_value)
        return (weighted / totals_here[..., None]).transpose(0, 2, 1, 3)
    fixed_out = lax.map(one_segment, (fixed_query, fixed_key, fixed_value, jnp.arange(segments, dtype=jnp.int32)))
    fixed_out = fixed_out.reshape(row_count, STRIDE, quad_count, 2, HD)
    merged = jnp.concatenate([row_out[:, :, :, None, :], column_out[:, :, :, None, :], fixed_out], axis=3)
    return merged.reshape(length, width).astype(jnp.bfloat16)
```

```python
import math

import jax
import jax.numpy as jnp
from jax import lax
from jax.experimental import pallas as pl
from jax.experimental.pallas import tpu as pltpu
from jax.sharding import Mesh
from jax.sharding import PartitionSpec as P

HD = 128
STRIDE = 32
QUADS = 8
POS = 128
ROWS = 4
LOW = -1e30
SCALE = math.log2(math.e) / math.sqrt(HD)
SUM_ROWS = 16
PAY = 2 * POS + SUM_ROWS

f32 = jnp.float32
bf16 = jnp.bfloat16


def dot_t(a, b):
    return lax.dot_general(a, b, (((1,), (1,)), ((), ())), preferred_element_type=f32)


def dot_tl(a, b):
    return lax.dot_general(a, b, (((0,), (0,)), ((), ())), preferred_element_type=f32)


def dot(a, b):
    return lax.dot_general(a, b, (((1,), (0,)), ((), ())), preferred_element_type=f32)


def iota(shape, dim):
    return lax.broadcasted_iota(jnp.int32, shape, dim)


def one_hot(rows, cols, source):
    row = iota((rows, cols), 0)
    col = iota((rows, cols), 1)
    return jnp.where(source(row) == col, 1.0, 0.0).astype(bf16)


def div12(o):
    return (o * 5462) >> 16


def head(ref, quad, kind):
    start = (quad * 4 + kind) * HD
    return ref[:, start : start + HD]


def pack_kernel(q_ref, k_ref, v_ref, item_ref, quad_ref):
    def source(o):
        col = div12(o)
        rest = o - 12 * col
        return (rest >> 2) * POS + (rest & 3) * STRIDE + col

    perm = one_hot(384, 384, source)
    pick = one_hot(
        SUM_ROWS, 512, lambda o: (o >> 2) * POS + (o & 3) * STRIDE + STRIDE - 1
    )
    for quad in range(QUADS):
        stack = jnp.concatenate(
            [head(q_ref, quad, 1), head(k_ref, quad, 1), head(v_ref, quad, 1)], axis=0
        )
        item_ref[quad] = dot(perm, stack).astype(bf16)
        for h in range(2):
            quad_ref[quad, h * POS : (h + 1) * POS, :] = head(q_ref, quad, 2 + h)
        summary = jnp.concatenate(
            [
                head(k_ref, quad, 2),
                head(k_ref, quad, 3),
                head(v_ref, quad, 2),
                head(v_ref, quad, 3),
            ],
            axis=0,
        )
        quad_ref[quad, 2 * POS :, :] = dot(pick, summary).astype(bf16)


def rows_kernel(q_ref, k_ref, v_ref, row_ref, part_ref, stat_ref):
    key = iota((POS, POS), 0)
    pos = iota((POS, POS), 1)
    visible = jnp.logical_and((key >> 5) == (pos >> 5), key <= pos)
    for quad in range(QUADS):
        for kind in (0, 2, 3):
            s = dot_t(head(k_ref, quad, kind), head(q_ref, quad, kind)) * SCALE
            s = jnp.where(visible, s, LOW)
            m = jnp.max(s, axis=0, keepdims=True)
            p = jnp.where(visible, jnp.exp2(s - m), 0.0)
            total = jnp.sum(p, axis=0, keepdims=True)
            acc = dot_tl(head(v_ref, quad, kind), p.astype(bf16))
            if kind == 0:
                row_ref[quad] = (acc / total).T.astype(bf16)
            else:
                slot = quad * 2 + kind - 2
                part_ref[slot] = acc
                row = iota((8, POS), 0)
                stat_ref[slot] = jnp.where(row == 0, m, total)


def column_kernel(core_ref, x_ref, out_ref, q_scr, k_scr, v_scr):
    core = core_ref[0]

    def source(o):
        within = o & 31
        return (within >> 2) * 12 + (o >> 5) * 4 + (within & 3)

    split = one_hot(96, 96, source)
    for c in range(2):
        for g in range(32):
            y = dot(split, x_ref[c, g * 96 : (g + 1) * 96, :]).astype(bf16)
            k_scr[c, g * 32 : (g + 1) * 32, :] = y[32:64]
            v_scr[c, g * 32 : (g + 1) * 32, :] = y[64:96]

            @pl.when(core == c)
            def _(y=y, g=g):
                q_scr[g * 32 : (g + 1) * 32, :] = y[0:32]

    block = 256
    for qb in range(1024 // block):
        q = q_scr[qb * block : (qb + 1) * block, :]
        jq = iota((block, block), 1)
        row_q = ((jq >> 4) << 5) + (jq & 15) + 16 * core
        jk = iota((block, block), 0)
        pieces = []
        m = jnp.full((1, block), LOW, f32)
        for kb in range(qb + 1):
            for c in range(2):
                s = dot_t(k_scr[c, kb * block : (kb + 1) * block, :], q) * SCALE
                if kb == qb:
                    row_k = ((jk >> 4) << 5) + (jk & 15) + 16 * c
                    s = jnp.where(row_k <= row_q, s, LOW)
                m = jnp.maximum(m, jnp.max(s, axis=0, keepdims=True))
                pieces.append((kb, c, s))
        total = jnp.zeros((1, block), f32)
        acc = jnp.zeros((HD, block), f32)
        for kb, c, s in pieces:
            p = jnp.exp2(s - m)
            total = total + jnp.sum(p, axis=0, keepdims=True)
            acc = acc + dot_tl(v_scr[c, kb * block : (kb + 1) * block, :], p.astype(bf16))
        out_ref[qb * block : (qb + 1) * block, :] = (acc / total).T.astype(bf16)


def far_kernel(seg_ref, q_ref, kv_ref, out_ref):
    seg = seg_ref[0]
    chunk = 8
    keys = chunk * 32
    lanes = QUADS * POS
    last = seg // chunk

    for h in range(2):
        q = jnp.concatenate(
            [q_ref[e, h * POS : (h + 1) * POS, :] for e in range(QUADS)], axis=0
        )

        def step(i, carried, masked):
            m, total, acc = carried
            k = jnp.concatenate(
                [kv_ref[i * chunk + t, h * 32 : h * 32 + 32, :] for t in range(chunk)], axis=0
            )
            v = jnp.concatenate(
                [kv_ref[i * chunk + t, 64 + h * 32 : 96 + h * 32, :] for t in range(chunk)],
                axis=0,
            )
            s = dot_t(k, q) * SCALE
            if masked:
                row_k = i * keys + iota((keys, lanes), 0)
                row_q = seg * 32 + (iota((keys, lanes), 1) >> 5)
                visible = row_k < row_q
                s = jnp.where(visible, s, LOW)
            m_next = jnp.maximum(m, jnp.max(s, axis=0, keepdims=True))
            p = jnp.exp2(s - m_next)
            if masked:
                p = jnp.where(visible, p, 0.0)
            rescale = jnp.exp2(m - m_next)
            total = total * rescale + jnp.sum(p, axis=0, keepdims=True)
            acc = acc * rescale + dot_tl(v, p.astype(bf16))
            return m_next, total, acc

        carried = (
            jnp.full((1, lanes), LOW, f32),
            jnp.zeros((1, lanes), f32),
            jnp.zeros((HD, lanes), f32),
        )
        carried = lax.fori_loop(0, last, lambda i, x: step(i, x, False), carried)
        m, total, acc = step(last, carried, True)
        seen = total > 0.0
        safe = jnp.where(seen, total, 1.0)
        out = (acc / safe).astype(bf16)
        lse = jnp.where(seen, m + jnp.log2(safe), LOW)
        high = lse.astype(bf16).astype(f32)
        left = lse - high
        mid = left.astype(bf16).astype(f32)
        low = left - mid
        row = iota((SUM_ROWS, POS), 0) - 3 * h
        for e in range(QUADS):
            at = slice(e * POS, (e + 1) * POS)
            out_ref[e, h * POS : (h + 1) * POS, :] = out[:, at]
            terms = jnp.where(
                row == 0,
                high[:, at],
                jnp.where(row == 1, mid[:, at], jnp.where(row == 2, low[:, at], 0.0)),
            )
            if h == 0:
                out_ref[e, 2 * POS :, :] = terms.astype(bf16)
            else:
                out_ref[e, 2 * POS :, :] = (
                    out_ref[e, 2 * POS :, :].astype(f32) + terms
                ).astype(bf16)


def final_kernel(far_ref, col_ref, row_ref, part_ref, stat_ref, out_ref):
    back = one_hot(POS, POS, lambda o: (o & 31) * 4 + (o >> 5))
    for quad in range(QUADS):
        base = quad * 4 * HD
        out_ref[:, base : base + HD] = row_ref[quad]
        out_ref[:, base + HD : base + 2 * HD] = dot(
            back, col_ref[quad * POS : (quad + 1) * POS, :]
        ).astype(bf16)
        terms = far_ref[quad, 2 * POS :, :].astype(f32)
        for h in range(2):
            lse = (terms[3 * h : 3 * h + 1] + terms[3 * h + 1 : 3 * h + 2]) + terms[
                3 * h + 2 : 3 * h + 3
            ]
            m = stat_ref[quad * 2 + h, 0:1, :]
            total = stat_ref[quad * 2 + h, 1:2, :]
            top = jnp.maximum(m, lse)
            own = jnp.exp2(m - top)
            far = jnp.exp2(lse - top)
            scale = 1.0 / (total * own + far)
            merged = (
                part_ref[quad * 2 + h] * (own * scale)
                + far_ref[quad, h * POS : (h + 1) * POS, :].astype(f32) * (far * scale)
            )
            start = base + (2 + h) * HD
            out_ref[:, start : start + HD] = merged.T.astype(bf16)


def call(kernel, outs, args, scalars=0, scratch=(), flops=0, moved=0, exps=0):
    vmem = pl.BlockSpec(memory_space=pltpu.VMEM)
    smem = pl.BlockSpec(memory_space=pltpu.SMEM)
    shapes = [jax.ShapeDtypeStruct(s, d) for s, d in outs]
    many = len(shapes) > 1
    return pl.pallas_call(
        kernel,
        out_shape=shapes if many else shapes[0],
        in_specs=[smem] * scalars + [vmem] * (len(args) - scalars),
        out_specs=[vmem] * len(shapes) if many else vmem,
        scratch_shapes=list(scratch),
        compiler_params=pltpu.CompilerParams(vmem_limit_bytes=40 * 1024 * 1024),
        cost_estimate=pl.CostEstimate(flops=flops, bytes_accessed=moved, transcendentals=exps),
    )(*args)


def exchange(array, axes):
    return lax.all_to_all(array, axes, split_axis=0, concat_axis=0, tiled=True)


def body(queries, keys, values):
    near = ("c", "x")
    wide = ("z", "u", "w", "x")
    mib = 1 << 20
    items, quads = call(
        pack_kernel,
        [((QUADS, 384, HD), bf16), ((QUADS, PAY, HD), bf16)],
        (queries, keys, values),
        flops=2 * 8 * 384 * 384 * 128,
        moved=5 * mib,
    )
    quads = exchange(quads, near)
    summary = (
        quads[:, 2 * POS :]
        .reshape(QUADS, 2, 2, ROWS, HD)
        .transpose(1, 2, 0, 3, 4)
        .reshape(1, POS, HD)
    )
    summary = lax.all_gather(summary, "w", axis=0, tiled=True)
    summary = lax.all_gather(summary, ("z", "u"), axis=0, tiled=True)

    items = exchange(items.reshape(768, ROWS, HD), wide).reshape(1, 3072, HD)
    row_out, part, stat = call(
        rows_kernel,
        [((QUADS, POS, HD), bf16), ((16, POS, POS), f32), ((16, 8, POS), f32)],
        (queries, keys, values),
        flops=24 * 4 * 128 * 128 * 128,
        moved=5 * mib,
        exps=24 * 128 * 128,
    )
    items = lax.all_gather(items, "c", axis=0, tiled=True)
    core = lax.axis_index("c").astype(jnp.int32).reshape(1)
    column = call(
        column_kernel,
        [((1024, HD), bf16)],
        (core, items),
        scalars=1,
        scratch=[
            pltpu.VMEM((1024, HD), bf16),
            pltpu.VMEM((2, 1024, HD), bf16),
            pltpu.VMEM((2, 1024, HD), bf16),
        ],
        flops=4 * 1024 * 1280 * 128,
        moved=2 * mib,
        exps=1024 * 1280,
    )
    column = exchange(column.reshape(256, ROWS, HD), wide).reshape(1024, HD)

    seg = lax.axis_index(("z", "u", "w")).astype(jnp.int32).reshape(1)
    far = call(
        far_kernel,
        [((QUADS, PAY, POS), bf16)],
        (seg, quads, summary),
        scalars=1,
        flops=8 * 1024 * 2048 * 128,
        moved=3 * mib,
        exps=2 * 1024 * 2048,
    )
    far = exchange(far, near)
    return call(
        final_kernel,
        [((POS, QUADS * 4 * HD), bf16)],
        (far, column, row_out, part, stat),
        flops=2 * 8 * 128 * 128 * 128,
        moved=4 * mib,
    )


def solution(mesh):
    fine = Mesh(mesh.devices.reshape(4, 8, 4, 2, 2), ("x", "z", "u", "w", "c"))
    spec = P(("z", "u", "w", "c", "x"), None)
    return jax.shard_map(
        body, mesh=fine, in_specs=(spec, spec, spec), out_specs=spec, check_vma=False
    )
```

```python
import math

import jax
import jax.numpy as jnp
from jax import lax
from jax.experimental import pallas as pl
from jax.experimental.pallas import tpu as pltpu
from jax.sharding import Mesh
from jax.sharding import PartitionSpec as P

HD = 128
STRIDE = 32
QUADS = 8
POS = 128
ROWS = 4
LOW = -1e30
SCALE = math.log2(math.e) / math.sqrt(HD)
SUM_ROWS = 16
PAY = POS + SUM_ROWS
HEADS = 16
PAIR = HEADS * POS

f32 = jnp.float32
bf16 = jnp.bfloat16


def dot_t(a, b):
    return lax.dot_general(a, b, (((1,), (1,)), ((), ())), preferred_element_type=f32)


def dot_tl(a, b):
    return lax.dot_general(a, b, (((0,), (0,)), ((), ())), preferred_element_type=f32)


def dot(a, b):
    return lax.dot_general(a, b, (((1,), (0,)), ((), ())), preferred_element_type=f32)


def iota(shape, dim):
    return lax.broadcasted_iota(jnp.int32, shape, dim)


def one_hot(rows, cols, source):
    row = iota((rows, cols), 0)
    col = iota((rows, cols), 1)
    return jnp.where(source(row) == col, 1.0, 0.0).astype(bf16)


def div12(o):
    return (o * 5462) >> 16


def head(ref, quad, kind):
    start = (quad * 4 + kind) * HD
    return ref[:, start : start + HD]


def pack_far_kernel(q_ref, k_ref, v_ref, query_ref, sum_ref):
    pick = one_hot(
        8, 2 * POS, lambda o: (o >> 2) * POS + (o & 3) * STRIDE + STRIDE - 1
    )
    for g in range(HEADS):
        quad, kind = g // 2, 2 + g % 2
        query_ref[g] = head(q_ref, quad, kind)
        stack = jnp.concatenate([head(k_ref, quad, kind), head(v_ref, quad, kind)], axis=0)
        rows = dot(pick, stack).astype(bf16)
        for t in range(sum_ref.shape[0] // HEADS):
            sum_ref[t * HEADS + g] = rows


def pack_column_kernel(after_ref, q_ref, k_ref, v_ref, item_ref):
    def source(o):
        col = div12(o)
        rest = o - 12 * col
        return (rest >> 2) * POS + (rest & 3) * STRIDE + col

    perm = one_hot(384, 384, source)
    for quad in range(QUADS):
        stack = jnp.concatenate(
            [head(q_ref, quad, 1), head(k_ref, quad, 1), head(v_ref, quad, 1)], axis=0
        )
        item_ref[quad] = dot(perm, stack).astype(bf16)


def rows_kernel(q_ref, k_ref, v_ref, row_ref, part_ref, max_ref, sum_ref):
    pos = iota((POS, POS), 0)
    key = iota((POS, POS), 1)
    visible = jnp.logical_and((key >> 5) == (pos >> 5), key <= pos)
    tops = jnp.zeros((POS, POS), f32)
    sums = jnp.ones((POS, POS), f32)
    for quad in range(QUADS):
        for kind in (0, 2, 3):
            s = dot_t(head(q_ref, quad, kind), head(k_ref, quad, kind)) * SCALE
            s = jnp.where(visible, s, LOW)
            m = jnp.max(s, axis=1, keepdims=True)
            p = jnp.where(visible, jnp.exp2(s - m), 0.0)
            total = jnp.sum(p, axis=1, keepdims=True)
            acc = dot(p.astype(bf16), head(v_ref, quad, kind))
            if kind == 0:
                row_ref[quad] = (acc / total).astype(bf16)
            else:
                slot = quad * 2 + kind - 2
                part_ref[slot] = acc
                tops = jnp.where(key == slot, m, tops)
                sums = jnp.where(key == slot, total, sums)
    max_ref[...] = tops
    sum_ref[...] = sums


def column_kernel(core_ref, own_ref, other_ref, out_ref, q_scr, k_scr, v_scr):
    core = core_ref[0]

    def source(o):
        within = o & 31
        return (within >> 2) * 12 + (o >> 5) * 4 + (within & 3)

    split = one_hot(96, 96, source)
    split_kv = one_hot(64, 96, lambda o: source(o + 32))
    for g in range(32):
        at = slice(g * 32, (g + 1) * 32)
        y = dot(split, own_ref[g * 96 : (g + 1) * 96, :]).astype(bf16)
        q_scr[at, :] = y[0:32]
        k_scr[0, at, :] = y[32:64]
        v_scr[0, at, :] = y[64:96]
        y = dot(split_kv, other_ref[g * 96 : (g + 1) * 96, :]).astype(bf16)
        k_scr[1, at, :] = y[0:32]
        v_scr[1, at, :] = y[32:64]

    block = 256
    jq = iota((block, block), 0)
    jk = iota((block, block), 1)
    visible = (jk <= jq, (jk >> 4) < (jq >> 4) + core)
    for qb in range(1024 // block):
        q = q_scr[qb * block : (qb + 1) * block, :]
        pieces = []
        top = None
        for kb in range(qb + 1):
            for c in range(2):
                s = dot_t(q, k_scr[c, kb * block : (kb + 1) * block, :]) * SCALE
                if kb == qb:
                    s = jnp.where(visible[c], s, LOW)
                fold = jnp.maximum(s[:, :128], s[:, 128:])
                top = fold if top is None else jnp.maximum(top, fold)
                pieces.append((kb, c, s))
        m = jnp.max(top, axis=1, keepdims=True)
        total = jnp.zeros((block, 128), f32)
        acc = jnp.zeros((block, HD), f32)
        for kb, c, s in pieces:
            p = jnp.exp2(s - m)
            total = total + (p[:, :128] + p[:, 128:])
            acc = acc + dot(p.astype(bf16), v_scr[c, kb * block : (kb + 1) * block, :])
        total = jnp.sum(total, axis=1, keepdims=True)
        out_ref[qb * block : (qb + 1) * block, :] = (acc / total).astype(bf16)


FAR_Q = 512
FAR_K = 1024


def far_kernel(pair_ref, q_ref, kv_ref, out_ref, s_scr):
    pair = pair_ref[0]
    row_ids = PAIR // STRIDE
    last = (pair * row_ids) // FAR_K
    lane = iota((POS, 128), 1)
    eye = one_hot(SUM_ROWS, 128, lambda o: o)
    per = FAR_Q // POS
    planes = FAR_K // 256

    def piece(i, j):
        return jnp.concatenate([kv_ref[i * planes + t, j] for t in range(planes)], axis=0)

    def fold(x, op):
        r = x[:, :128]
        for t in range(1, FAR_K // 128):
            r = op(r, x[:, t * 128 : (t + 1) * 128])
        return r

    def block(b, unused):
        q = q_ref[pl.ds(b * per, per)].reshape(FAR_Q, HD)

        def score(i, top):
            s = dot_t(q, piece(i, 0)) * SCALE
            s_scr[i] = s
            return jnp.maximum(top, fold(s, jnp.maximum))

        top = lax.fori_loop(0, last, score, jnp.full((FAR_Q, 128), LOW, f32))
        s = dot_t(q, piece(last, 0)) * SCALE
        row_k = last * FAR_K + iota((FAR_Q, FAR_K), 1)
        row_q = pair * row_ids + ((b * FAR_Q + iota((FAR_Q, FAR_K), 0)) >> 5)
        s = jnp.where(row_k < row_q, s, LOW)
        s_scr[last] = s
        top = jnp.maximum(top, fold(s, jnp.maximum))
        m = jnp.max(top, axis=1, keepdims=True)

        def weigh(i, carried):
            total, acc = carried
            p = jnp.exp2(s_scr[i] - m)
            return (
                total + fold(p, jnp.add),
                acc + dot(p.astype(bf16), piece(i, 1)),
            )

        total, acc = lax.fori_loop(
            0,
            last + 1,
            weigh,
            (jnp.zeros((FAR_Q, 128), f32), jnp.zeros((FAR_Q, HD), f32)),
        )
        total = jnp.sum(total, axis=1, keepdims=True)
        out = (acc / total).astype(bf16)
        lse = jnp.where(m > 0.5 * LOW, m + jnp.log2(total), LOW)
        high = lse.astype(bf16).astype(f32)
        left = lse - high
        mid = left.astype(bf16).astype(f32)
        low = left - mid
        for e in range(per):
            at = slice(e * POS, (e + 1) * POS)
            terms = jnp.where(
                lane == 0,
                high[at],
                jnp.where(lane == 1, mid[at], jnp.where(lane == 2, low[at], 0.0)),
            ).astype(bf16)
            out_ref[b * per + e, :POS, :] = out[at]
            out_ref[b * per + e, POS:, :] = dot_t(eye, terms).astype(bf16)
        return unused

    lax.fori_loop(0, PAIR // FAR_Q, block, 0)


def final_kernel(far_ref, col_ref, row_ref, part_ref, max_ref, sum_ref, out_ref):
    back = one_hot(POS, POS, lambda o: (o & 31) * 4 + (o >> 5))
    row = iota((HEADS * SUM_ROWS, 128), 0)
    lane = iota((HEADS * SUM_ROWS, 128), 1)
    pick = jnp.where(
        jnp.logical_and((row >> 4) == lane, (row & 15) < 3), 1.0, 0.0
    ).astype(bf16)
    terms = jnp.concatenate([far_ref[g, POS:, :] for g in range(HEADS)], axis=0)
    lse = dot_tl(terms, pick)
    top = jnp.maximum(max_ref[...], lse)
    own = jnp.exp2(max_ref[...] - top)
    far = jnp.exp2(lse - top)
    scale = 1.0 / (sum_ref[...] * own + far)
    own = own * scale
    far = far * scale
    for quad in range(QUADS):
        base = quad * 4 * HD
        out_ref[:, base : base + HD] = row_ref[quad]
        out_ref[:, base + HD : base + 2 * HD] = dot(
            back, col_ref[quad * POS : (quad + 1) * POS, :]
        ).astype(bf16)
        for h in range(2):
            g = quad * 2 + h
            merged = (
                part_ref[g] * own[:, g : g + 1]
                + far_ref[g, :POS, :].astype(f32) * far[:, g : g + 1]
            )
            start = base + (2 + h) * HD
            out_ref[:, start : start + HD] = merged.astype(bf16)


def call(kernel, outs, args, scalars=0, scratch=(), flops=0, moved=0, exps=0, mib=16, unread=0):
    vmem = pl.BlockSpec(memory_space=pltpu.VMEM)
    smem = pl.BlockSpec(memory_space=pltpu.SMEM)
    hbm = pl.BlockSpec(memory_space=pl.ANY)
    shapes = [jax.ShapeDtypeStruct(s, d) for s, d in outs]
    many = len(shapes) > 1
    specs = [smem] * scalars + [hbm] * unread
    return pl.pallas_call(
        kernel,
        out_shape=shapes if many else shapes[0],
        in_specs=specs + [vmem] * (len(args) - len(specs)),
        out_specs=[vmem] * len(shapes) if many else vmem,
        scratch_shapes=list(scratch),
        compiler_params=pltpu.CompilerParams(vmem_limit_bytes=mib * 1024 * 1024),
        cost_estimate=pl.CostEstimate(flops=flops, bytes_accessed=moved, transcendentals=exps),
    )(*args)


def exchange(array, axes):
    return lax.all_to_all(array, axes, split_axis=0, concat_axis=0, tiled=True)


def body(queries, keys, values):
    heads_at = ("w", "c", "x")
    plane = ("u", "v", "w", "c", "x")
    wide = ("z", "u", "v", "w", "x")
    mib = 1 << 20
    heads, summary = call(
        pack_far_kernel,
        [((HEADS, POS, HD), bf16), ((64, 8, HD), bf16)],
        (queries, keys, values),
        flops=2 * 16 * 16 * 256 * 128,
        moved=4 * mib,
    )
    summary = exchange(summary, plane)
    summary = summary.reshape(64, 2, ROWS, HD).transpose(1, 0, 2, 3).reshape(1, 2, 256, HD)
    items = call(
        pack_column_kernel,
        [((QUADS, 384, HD), bf16)],
        (summary, queries, keys, values),
        unread=1,
        flops=2 * 8 * 384 * 384 * 128,
        moved=4 * mib,
    )
    summary = lax.all_gather(summary, "z", axis=0, tiled=True)
    items = exchange(items.reshape(768, ROWS, HD), wide).reshape(3072, HD)
    heads = exchange(heads, heads_at)
    other = lax.ppermute(items, "c", [(0, 1), (1, 0)])
    core = lax.axis_index("c").astype(jnp.int32).reshape(1)
    column = call(
        column_kernel,
        [((1024, HD), bf16)],
        (core, items, other),
        scalars=1,
        scratch=[
            pltpu.VMEM((1024, HD), bf16),
            pltpu.VMEM((2, 1024, HD), bf16),
            pltpu.VMEM((2, 1024, HD), bf16),
        ],
        flops=4 * 1024 * 1280 * 128,
        moved=2 * mib,
        exps=1024 * 1280,
    )
    column = exchange(column.reshape(256, ROWS, HD), wide).reshape(1024, HD)
    row_out, part, tops, sums = call(
        rows_kernel,
        [
            ((QUADS, POS, HD), bf16),
            ((HEADS, POS, HD), f32),
            ((POS, 128), f32),
            ((POS, 128), f32),
        ],
        (queries, keys, values),
        flops=24 * 4 * 128 * 128 * 128,
        moved=5 * mib,
        exps=24 * 128 * 128,
    )

    pair = lax.axis_index(("z", "u", "v")).astype(jnp.int32).reshape(1)
    far = call(
        far_kernel,
        [((HEADS, PAY, HD), bf16)],
        (pair, heads, summary),
        scalars=1,
        scratch=[pltpu.VMEM((2048 // FAR_K, FAR_Q, FAR_K), f32)],
        flops=8 * 1024 * 2048 * 128,
        moved=3 * mib,
        exps=2 * 1024 * 2048,
        mib=24,
    )
    far = exchange(far, heads_at)
    return call(
        final_kernel,
        [((POS, QUADS * 4 * HD), bf16)],
        (far, column, row_out, part, tops, sums),
        flops=2 * 8 * 128 * 128 * 128,
        moved=4 * mib,
    )


def solution(mesh):
    fine = Mesh(mesh.devices.reshape(4, 8, 2, 2, 2, 2), ("x", "z", "u", "v", "w", "c"))
    spec = P(("z", "u", "v", "w", "c", "x"), None)
    return jax.shard_map(
        body, mesh=fine, in_specs=(spec, spec, spec), out_specs=spec, check_vma=False
    )
```

```python
import math

import jax
import jax.numpy as jnp
from jax import lax
from jax.experimental import pallas as pl
from jax.experimental.pallas import tpu as pltpu
from jax.sharding import Mesh
from jax.sharding import PartitionSpec as P

HD = 128
STRIDE = 32
QUADS = 8
POS = 128
ROWS = 4
LOW = -1e30
SCALE = math.log2(math.e) / math.sqrt(HD)
SUM_ROWS = 16
PAY = POS + SUM_ROWS
HEADS = 16
PAIR = HEADS * POS

f32 = jnp.float32
bf16 = jnp.bfloat16


def dot_t(a, b):
    return lax.dot_general(a, b, (((1,), (1,)), ((), ())), preferred_element_type=f32)


def dot_tl(a, b):
    return lax.dot_general(a, b, (((0,), (0,)), ((), ())), preferred_element_type=f32)


def dot(a, b):
    return lax.dot_general(a, b, (((1,), (0,)), ((), ())), preferred_element_type=f32)


def iota(shape, dim):
    return lax.broadcasted_iota(jnp.int32, shape, dim)


def one_hot(rows, cols, source):
    row = iota((rows, cols), 0)
    col = iota((rows, cols), 1)
    return jnp.where(source(row) == col, 1.0, 0.0).astype(bf16)


def div12(o):
    return (o * 5462) >> 16


def head(ref, quad, kind):
    start = (quad * 4 + kind) * HD
    return ref[:, start : start + HD]


def pack_summary_kernel(k_ref, v_ref, sum_ref, buf, sems):
    moves = []
    for a, ref in enumerate((k_ref, v_ref)):
        for r in range(ROWS):
            move = pltpu.make_async_copy(
                ref.at[pl.ds(r * STRIDE + 16, 16), :],
                buf.at[pl.ds((a * ROWS + r) * 16, 16), :],
                sems.at[a * ROWS + r],
            )
            move.start()
            moves.append(move)
    pick = one_hot(8, 128, lambda o: o * 16 + 15)
    for move in moves:
        move.wait()
    for g in range(HEADS):
        rows = dot(pick, head(buf, g // 2, 2 + g % 2)).astype(bf16)
        for t in range(sum_ref.shape[0] // HEADS):
            sum_ref[t * HEADS + g] = rows


def pack_kernel(after_ref, q_ref, k_ref, v_ref, item_ref, query_ref, items, heads, sems):
    def source(o):
        col = div12(o)
        rest = o - 12 * col
        return (rest >> 2) * POS + (rest & 3) * STRIDE + col

    perm = one_hot(384, 384, source)
    moves = []
    for quad in range(QUADS):
        stack = jnp.concatenate(
            [head(q_ref, quad, 1), head(k_ref, quad, 1), head(v_ref, quad, 1)], axis=0
        )
        items[quad] = dot(perm, stack).astype(bf16)
        move = pltpu.make_async_copy(items.at[quad], item_ref.at[quad], sems.at[quad])
        move.start()
        moves.append(move)
    for g in range(HEADS):
        heads[g] = head(q_ref, g // 2, 2 + g % 2)
    move = pltpu.make_async_copy(heads, query_ref, sems.at[QUADS])
    move.start()
    moves.append(move)
    for move in moves:
        move.wait()


def rows_kernel(q_ref, k_ref, v_ref, row_ref, part_ref, max_ref, sum_ref):
    pos = iota((POS, POS), 0)
    key = iota((POS, POS), 1)
    visible = jnp.logical_and((key >> 5) == (pos >> 5), key <= pos)
    tops = jnp.zeros((POS, POS), f32)
    sums = jnp.ones((POS, POS), f32)
    for quad in range(QUADS):
        for kind in (0, 2, 3):
            s = dot_t(head(q_ref, quad, kind), head(k_ref, quad, kind)) * SCALE
            s = jnp.where(visible, s, LOW)
            m = jnp.max(s, axis=1, keepdims=True)
            p = jnp.where(visible, jnp.exp2(s - m), 0.0)
            total = jnp.sum(p, axis=1, keepdims=True)
            acc = dot(p.astype(bf16), head(v_ref, quad, kind))
            if kind == 0:
                row_ref[quad] = (acc / total).astype(bf16)
            else:
                slot = quad * 2 + kind - 2
                part_ref[slot] = acc
                tops = jnp.where(key == slot, m, tops)
                sums = jnp.where(key == slot, total, sums)
    max_ref[...] = tops
    sum_ref[...] = sums


def column_kernel(
    core_ref, own_hbm, other_hbm, out_hbm, own_ref, other_ref, out_scr, q_scr, k_scr, v_scr, sems
):
    core = core_ref[0]
    own_in = pltpu.make_async_copy(own_hbm, own_ref, sems.at[0])
    other_in = pltpu.make_async_copy(other_hbm, other_ref, sems.at[1])
    own_in.start()
    other_in.start()

    def source(o):
        within = o & 31
        return (within >> 2) * 12 + (o >> 5) * 4 + (within & 3)

    split = one_hot(96, 96, source)
    split_kv = one_hot(64, 96, lambda o: source(o + 32))
    by_x = one_hot(POS, POS, lambda o: ((o >> 2) & 7) * 16 + (o >> 5) * 4 + (o & 3))
    own_in.wait()
    for g in range(32):
        at = slice(g * 32, (g + 1) * 32)
        y = dot(split, own_ref[g * 96 : (g + 1) * 96, :]).astype(bf16)
        q_scr[at, :] = y[0:32]
        k_scr[0, at, :] = y[32:64]
        v_scr[0, at, :] = y[64:96]
    other_in.wait()
    for g in range(32):
        at = slice(g * 32, (g + 1) * 32)
        y = dot(split_kv, other_ref[g * 96 : (g + 1) * 96, :]).astype(bf16)
        k_scr[1, at, :] = y[0:32]
        v_scr[1, at, :] = y[32:64]

    block = 256
    jq = iota((block, block), 0)
    jk = iota((block, block), 1)
    visible = (jk <= jq, (jk >> 4) < (jq >> 4) + core)
    moves = []
    for qb in range(1024 // block):
        q = q_scr[qb * block : (qb + 1) * block, :]
        pieces = []
        top = None
        for kb in range(qb + 1):
            for c in range(2):
                s = dot_t(q, k_scr[c, kb * block : (kb + 1) * block, :]) * SCALE
                if kb == qb:
                    s = jnp.where(visible[c], s, LOW)
                fold = jnp.maximum(s[:, :128], s[:, 128:])
                top = fold if top is None else jnp.maximum(top, fold)
                pieces.append((kb, c, s))
        m = jnp.max(top, axis=1, keepdims=True)
        total = jnp.zeros((block, 128), f32)
        acc = jnp.zeros((block, HD), f32)
        for kb, c, s in pieces:
            p = jnp.exp2(s - m)
            total = total + (p[:, :128] + p[:, 128:])
            acc = acc + dot(p.astype(bf16), v_scr[c, kb * block : (kb + 1) * block, :])
        total = jnp.sum(total, axis=1, keepdims=True)
        out = (acc / total).astype(bf16)
        for t in range(block // POS):
            y = dot(by_x, out[t * POS : (t + 1) * POS]).astype(bf16)
            at = (qb * block // POS + t) * STRIDE
            for x in range(4):
                out_scr[x, at : at + STRIDE, :] = y[x * STRIDE : (x + 1) * STRIDE]
        at = pl.ds(qb * block // 4, block // 4)
        move = pltpu.make_async_copy(out_scr.at[:, at, :], out_hbm.at[:, at, :], sems.at[2 + qb])
        move.start()
        moves.append(move)
    for move in moves:
        move.wait()


FAR_Q = 512
FAR_K = 1024
FAR_BLOCKS = PAIR // FAR_Q


def far_kernel(pair_ref, q_hbm, kv_hbm, out_hbm, q_ref, kv_ref, out_ref, s_scr, sems):
    pair = pair_ref[0]
    ins = [
        pltpu.make_async_copy(q_hbm, q_ref, sems.at[0]),
        pltpu.make_async_copy(kv_hbm, kv_ref, sems.at[1]),
    ]
    for move in ins:
        move.start()
    row_ids = PAIR // STRIDE
    last = (pair * row_ids) // FAR_K
    lane = iota((POS, 128), 1)
    eye = one_hot(SUM_ROWS, 128, lambda o: o)
    per = FAR_Q // POS
    planes = FAR_K // 256

    for move in ins:
        move.wait()

    def send(b):
        at = pl.ds(b * per, per)
        return pltpu.make_async_copy(out_ref.at[at], out_hbm.at[at], sems.at[2 + b])

    def piece(i, j):
        return jnp.concatenate([kv_ref[i * planes + t, j] for t in range(planes)], axis=0)

    def fold(x, op):
        r = x[:, :128]
        for t in range(1, FAR_K // 128):
            r = op(r, x[:, t * 128 : (t + 1) * 128])
        return r

    def block(b, unused):
        q = q_ref[pl.ds(b * per, per)].reshape(FAR_Q, HD)

        def score(i, top):
            s = dot_t(q, piece(i, 0)) * SCALE
            s_scr[i] = s
            return jnp.maximum(top, fold(s, jnp.maximum))

        top = lax.fori_loop(0, last, score, jnp.full((FAR_Q, 128), LOW, f32))
        s = dot_t(q, piece(last, 0)) * SCALE
        row_k = last * FAR_K + iota((FAR_Q, FAR_K), 1)
        row_q = pair * row_ids + ((b * FAR_Q + iota((FAR_Q, FAR_K), 0)) >> 5)
        s = jnp.where(row_k < row_q, s, LOW)
        s_scr[last] = s
        top = jnp.maximum(top, fold(s, jnp.maximum))
        m = jnp.max(top, axis=1, keepdims=True)

        def weigh(i, carried):
            total, acc = carried
            p = jnp.exp2(s_scr[i] - m)
            return (
                total + fold(p, jnp.add),
                acc + dot(p.astype(bf16), piece(i, 1)),
            )

        total, acc = lax.fori_loop(
            0,
            last + 1,
            weigh,
            (jnp.zeros((FAR_Q, 128), f32), jnp.zeros((FAR_Q, HD), f32)),
        )
        total = jnp.sum(total, axis=1, keepdims=True)
        out = (acc / total).astype(bf16)
        lse = jnp.where(m > 0.5 * LOW, m + jnp.log2(total), LOW)
        high = lse.astype(bf16).astype(f32)
        left = lse - high
        mid = left.astype(bf16).astype(f32)
        low = left - mid
        for e in range(per):
            at = slice(e * POS, (e + 1) * POS)
            terms = jnp.where(
                lane == 0,
                high[at],
                jnp.where(lane == 1, mid[at], jnp.where(lane == 2, low[at], 0.0)),
            ).astype(bf16)
            out_ref[b * per + e, :POS, :] = out[at]
            out_ref[b * per + e, POS:, :] = dot_t(eye, terms).astype(bf16)
        send(b).start()
        return unused

    lax.fori_loop(0, FAR_BLOCKS, block, 0)
    for b in range(FAR_BLOCKS):
        send(b).wait()


def final_kernel(
    far_hbm, col_hbm, row_hbm, part_hbm, max_ref, sum_ref, out_hbm,
    far_ref, col_ref, row_ref, part_ref, out_ref, sems,
):
    ins = [
        pltpu.make_async_copy(far_hbm, far_ref, sems.at[0]),
        pltpu.make_async_copy(part_hbm, part_ref, sems.at[1]),
        pltpu.make_async_copy(col_hbm, col_ref, sems.at[2]),
        pltpu.make_async_copy(row_hbm, row_ref, sems.at[3]),
    ]
    for move in ins:
        move.start()
    back = one_hot(
        POS, POS, lambda o: (o & 3) * STRIDE + ((o >> 2) & 7) * 4 + (o >> 5)
    )
    row = iota((HEADS * SUM_ROWS, 128), 0)
    lane = iota((HEADS * SUM_ROWS, 128), 1)
    pick = jnp.where(
        jnp.logical_and((row >> 4) == lane, (row & 15) < 3), 1.0, 0.0
    ).astype(bf16)
    ins[0].wait()
    terms = jnp.concatenate([far_ref[g, POS:, :] for g in range(HEADS)], axis=0)
    lse = dot_tl(terms, pick)
    top = jnp.maximum(max_ref[...], lse)
    own = jnp.exp2(max_ref[...] - top)
    far = jnp.exp2(lse - top)
    scale = 1.0 / (sum_ref[...] * own + far)
    own = own * scale
    far = far * scale
    for move in ins[1:]:
        move.wait()
    moves = []
    for quad in range(QUADS):
        base = quad * 4 * HD
        out_ref[:, base : base + HD] = row_ref[quad]
        stack = jnp.concatenate(
            [col_ref[x, quad * STRIDE : (quad + 1) * STRIDE, :] for x in range(4)], axis=0
        )
        out_ref[:, base + HD : base + 2 * HD] = dot(back, stack).astype(bf16)
        for h in range(2):
            g = quad * 2 + h
            merged = (
                part_ref[g] * own[:, g : g + 1]
                + far_ref[g, :POS, :].astype(f32) * far[:, g : g + 1]
            )
            start = base + (2 + h) * HD
            out_ref[:, start : start + HD] = merged.astype(bf16)
        at = pl.ds(base, 4 * HD)
        move = pltpu.make_async_copy(out_ref.at[:, at], out_hbm.at[:, at], sems.at[4 + quad])
        move.start()
        moves.append(move)
    for move in moves:
        move.wait()


SPACES = {"v": pltpu.VMEM, "s": pltpu.SMEM, "h": pltpu.HBM, "a": pl.ANY}


def call(kernel, outs, args, ins, to="v", scratch=(), flops=0, moved=0, exps=0, mib=16):
    def spec(space):
        return pl.BlockSpec(memory_space=SPACES[space])

    shapes = [jax.ShapeDtypeStruct(s, d) for s, d in outs]
    many = len(shapes) > 1
    return pl.pallas_call(
        kernel,
        out_shape=shapes if many else shapes[0],
        in_specs=[spec(space) for space in ins],
        out_specs=[spec(to)] * len(shapes) if many else spec(to),
        scratch_shapes=list(scratch),
        compiler_params=pltpu.CompilerParams(vmem_limit_bytes=mib * 1024 * 1024),
        cost_estimate=pl.CostEstimate(flops=flops, bytes_accessed=moved, transcendentals=exps),
    )(*args)


def exchange(array, axes):
    return lax.all_to_all(array, axes, split_axis=0, concat_axis=0, tiled=True)


def dma(n):
    return pltpu.SemaphoreType.DMA((n,))


mib = 1 << 20


def pack_summary(keys, values):
    return call(
        pack_summary_kernel,
        [((64, 8, HD), bf16)],
        (keys, values),
        "hh",
        scratch=[pltpu.VMEM((128, QUADS * 4 * HD), bf16), dma(8)],
        flops=2 * 16 * 16 * 128 * 128,
        moved=mib,
    )


def pack(after, queries, keys, values):
    return call(
        pack_kernel,
        [((QUADS, 384, HD), bf16), ((HEADS, POS, HD), bf16)],
        (after, queries, keys, values),
        "avvv",
        to="h",
        scratch=[pltpu.VMEM((QUADS, 384, HD), bf16), pltpu.VMEM((HEADS, POS, HD), bf16), dma(9)],
        flops=2 * 8 * 384 * 384 * 128,
        moved=4 * mib,
    )


def rows(queries, keys, values):
    return call(
        rows_kernel,
        [
            ((QUADS, POS, HD), bf16),
            ((HEADS, POS, HD), f32),
            ((POS, 128), f32),
            ((POS, 128), f32),
        ],
        (queries, keys, values),
        "vvv",
        flops=24 * 4 * 128 * 128 * 128,
        moved=5 * mib,
        exps=24 * 128 * 128,
    )


def columns(core, items, other):
    return call(
        column_kernel,
        [((4, 256, HD), bf16)],
        (core, items, other),
        "shh",
        to="h",
        scratch=[
            pltpu.VMEM((3072, HD), bf16),
            pltpu.VMEM((3072, HD), bf16),
            pltpu.VMEM((4, 256, HD), bf16),
            pltpu.VMEM((1024, HD), bf16),
            pltpu.VMEM((2, 1024, HD), bf16),
            pltpu.VMEM((2, 1024, HD), bf16),
            dma(6),
        ],
        flops=4 * 1024 * 1280 * 128,
        moved=2 * mib,
        exps=1024 * 1280,
    )


def far_part(pair, heads, summary):
    return call(
        far_kernel,
        [((HEADS, PAY, HD), bf16)],
        (pair, heads, summary),
        "shh",
        to="h",
        scratch=[
            pltpu.VMEM((HEADS, POS, HD), bf16),
            pltpu.VMEM((8, 2, 256, HD), bf16),
            pltpu.VMEM((HEADS, PAY, HD), bf16),
            pltpu.VMEM((2048 // FAR_K, FAR_Q, FAR_K), f32),
            dma(2 + FAR_BLOCKS),
        ],
        flops=8 * 1024 * 2048 * 128,
        moved=3 * mib,
        exps=2 * 1024 * 2048,
        mib=24,
    )


def final(far, column, row_out, part, tops, sums):
    return call(
        final_kernel,
        [((POS, QUADS * 4 * HD), bf16)],
        (far, column, row_out, part, tops, sums),
        "hhhhvv",
        to="h",
        scratch=[
            pltpu.VMEM((HEADS, PAY, HD), bf16),
            pltpu.VMEM((4, 256, HD), bf16),
            pltpu.VMEM((QUADS, POS, HD), bf16),
            pltpu.VMEM((HEADS, POS, HD), f32),
            pltpu.VMEM((POS, QUADS * 4 * HD), bf16),
            dma(12),
        ],
        flops=2 * 8 * 128 * 128 * 128,
        moved=4 * mib,
    )


def body(queries, keys, values):
    heads_at = ("w", "c", "x")
    plane = ("u", "v", "w", "c", "x")
    wide = ("z", "u", "v", "w", "x")
    back = ("x", "z", "u", "v", "w")
    summary = exchange(pack_summary(keys, values), plane)
    summary = summary.reshape(64, 2, ROWS, HD).transpose(1, 0, 2, 3).reshape(1, 2, 256, HD)
    items, heads = pack(summary, queries, keys, values)
    summary = lax.all_gather(summary, "z", axis=0, tiled=True)
    items = exchange(items.reshape(768, ROWS, HD), wide).reshape(3072, HD)
    heads = exchange(heads, heads_at)
    other = lax.ppermute(items, "c", [(0, 1), (1, 0)])
    core = lax.axis_index("c").astype(jnp.int32).reshape(1)
    column = columns(core, items, other)
    column = exchange(column.reshape(256, ROWS, HD), back).reshape(4, 256, HD)
    row_out, part, tops, sums = rows(queries, keys, values)
    pair = lax.axis_index(("z", "u", "v")).astype(jnp.int32).reshape(1)
    far = exchange(far_part(pair, heads, summary), heads_at)
    return final(far, column, row_out, part, tops, sums)


def solution(mesh):
    fine = Mesh(mesh.devices.reshape(4, 8, 2, 2, 2, 2), ("x", "z", "u", "v", "w", "c"))
    spec = P(("z", "u", "v", "w", "c", "x"), None)
    return jax.shard_map(
        body, mesh=fine, in_specs=(spec, spec, spec), out_specs=spec, check_vma=False
    )
```

```python
import math

import jax
import jax.numpy as jnp
from jax import lax
from jax.experimental import pallas as pl
from jax.experimental.pallas import tpu as pltpu
from jax.sharding import Mesh
from jax.sharding import PartitionSpec as P

HD = 128
STRIDE = 32
QUADS = 8
POS = 128
ROWS = 4
LOW = -1e30
SCALE = math.log2(math.e) / math.sqrt(HD)
SUM_ROWS = 16
PAY = POS + SUM_ROWS
HEADS = 16
PAIR = HEADS * POS

f32 = jnp.float32
bf16 = jnp.bfloat16


def dot_t(a, b):
    return lax.dot_general(a, b, (((1,), (1,)), ((), ())), preferred_element_type=f32)


def dot_tl(a, b):
    return lax.dot_general(a, b, (((0,), (0,)), ((), ())), preferred_element_type=f32)


def dot(a, b):
    return lax.dot_general(a, b, (((1,), (0,)), ((), ())), preferred_element_type=f32)


def iota(shape, dim):
    return lax.broadcasted_iota(jnp.int32, shape, dim)


def one_hot(rows, cols, source):
    row = iota((rows, cols), 0)
    col = iota((rows, cols), 1)
    return jnp.where(source(row) == col, 1.0, 0.0).astype(bf16)


def div12(o):
    return (o * 5462) >> 16


def head(ref, quad, kind):
    start = (quad * 4 + kind) * HD
    return ref[:, start : start + HD]


def pack_summary_kernel(k_ref, v_ref, sum_hbm, buf, sum_ref, sems):
    moves = []
    for a, ref in enumerate((k_ref, v_ref)):
        for r in range(ROWS):
            move = pltpu.make_async_copy(
                ref.at[pl.ds(r * STRIDE + 16, 16), :],
                buf.at[pl.ds((a * ROWS + r) * 16, 16), :],
                sems.at[a * ROWS + r],
            )
            move.start()
            moves.append(move)
    pick = one_hot(8, 128, lambda o: o * 16 + 15)
    for move in moves:
        move.wait()
    for g in range(HEADS):
        rows = dot(pick, head(buf, g // 2, 2 + g % 2)).astype(bf16)
        sum_ref[g] = rows
    moves = []
    for t in range(sum_hbm.shape[0] // HEADS):
        move = pltpu.make_async_copy(
            sum_ref, sum_hbm.at[pl.ds(t * HEADS, HEADS)], sems.at[2 * ROWS + t]
        )
        move.start()
        moves.append(move)
    for move in moves:
        move.wait()


def pack_kernel(q_hbm, k_hbm, v_hbm, item_hbm, query_hbm, stack, items, sems, outs):
    def source(o):
        col = div12(o)
        rest = o - 12 * col
        return (rest >> 2) * POS + (rest & 3) * STRIDE + col

    ins = []
    for quad in range(QUADS):
        at = pl.ds((quad * 4 + 1) * HD, HD)
        for a, ref in enumerate((q_hbm, k_hbm, v_hbm)):
            move = pltpu.make_async_copy(
                ref.at[:, at], stack.at[quad, pl.ds(a * POS, POS), :], sems.at[quad * 3 + a]
            )
            move.start()
            ins.append(move)
    moves = []
    for g in range(HEADS):
        at = pl.ds(((g // 2) * 4 + 2 + g % 2) * HD, HD)
        moves.append(
            pltpu.make_async_copy(q_hbm.at[:, at], query_hbm.at[g], outs.at[QUADS + g])
        )
    perm = one_hot(384, 384, source)
    for quad in range(QUADS):
        for a in range(3):
            ins[quad * 3 + a].wait()
        items[quad] = dot(perm, stack[quad]).astype(bf16)
        move = pltpu.make_async_copy(items.at[quad], item_hbm.at[quad], outs.at[quad])
        move.start()
        if quad == 0:
            for copy in moves:
                copy.start()
        moves.append(move)
    for move in moves:
        move.wait()


def order_kernel(after_ref, item_ref, out_ref):
    pass


def rows_kernel(
    q_hbm, k_hbm, v_hbm, row_hbm, part_hbm, stat_hbm,
    q_ref, k_ref, v_ref, row_ref, part_ref, stat_ref, sems,
):
    ins = []
    for a, (hbm, ref) in enumerate(((q_hbm, q_ref), (k_hbm, k_ref), (v_hbm, v_ref))):
        move = pltpu.make_async_copy(hbm, ref, sems.at[a])
        move.start()
        ins.append(move)
    pos = iota((POS, POS), 0)
    key = iota((POS, POS), 1)
    visible = jnp.logical_and((key >> 5) == (pos >> 5), key <= pos)
    tops = jnp.zeros((POS, POS), f32)
    sums = jnp.ones((POS, POS), f32)
    for move in ins:
        move.wait()
    moves = []
    for quad in range(QUADS):
        for kind in (0, 2, 3):
            s = dot_t(head(q_ref, quad, kind), head(k_ref, quad, kind)) * SCALE
            s = jnp.where(visible, s, LOW)
            m = jnp.max(s, axis=1, keepdims=True)
            p = jnp.where(visible, jnp.exp2(s - m), 0.0)
            total = jnp.sum(p, axis=1, keepdims=True)
            acc = dot(p.astype(bf16), head(v_ref, quad, kind))
            if kind == 0:
                row_ref[quad] = (acc / total).astype(bf16)
            else:
                slot = quad * 2 + kind - 2
                part_ref[slot] = acc
                tops = jnp.where(key == slot, m, tops)
                sums = jnp.where(key == slot, total, sums)
        two = pl.ds(quad * 2, 2)
        moves.append(pltpu.make_async_copy(part_ref.at[two], part_hbm.at[two], sems.at[3 + quad]))
        moves[-1].start()
    stat_ref[0] = tops
    stat_ref[1] = sums
    moves.append(pltpu.make_async_copy(row_ref, row_hbm, sems.at[11]))
    moves.append(pltpu.make_async_copy(stat_ref, stat_hbm, sems.at[12]))
    moves[-1].start()
    moves[-2].start()
    for move in moves:
        move.wait()


def column_kernel(
    core_ref, own_hbm, other_hbm, out_hbm, own_ref, other_ref, out_scr, q_scr, k_scr, v_scr, sems
):
    core = core_ref[0]
    own_in = pltpu.make_async_copy(own_hbm, own_ref, sems.at[0])
    other_in = pltpu.make_async_copy(other_hbm, other_ref, sems.at[1])
    own_in.start()
    other_in.start()

    def source(o):
        within = o & 31
        return (within >> 2) * 12 + (o >> 5) * 4 + (within & 3)

    split = one_hot(96, 96, source)
    split_kv = one_hot(64, 96, lambda o: source(o + 32))
    by_x = one_hot(POS, POS, lambda o: ((o >> 2) & 7) * 16 + (o >> 5) * 4 + (o & 3))
    own_in.wait()
    for g in range(32):
        at = slice(g * 32, (g + 1) * 32)
        y = dot(split, own_ref[g * 96 : (g + 1) * 96, :]).astype(bf16)
        q_scr[at, :] = y[0:32]
        k_scr[0, at, :] = y[32:64]
        v_scr[0, at, :] = y[64:96]
    other_in.wait()
    for g in range(32):
        at = slice(g * 32, (g + 1) * 32)
        y = dot(split_kv, other_ref[g * 96 : (g + 1) * 96, :]).astype(bf16)
        k_scr[1, at, :] = y[0:32]
        v_scr[1, at, :] = y[32:64]

    block = 256
    jq = iota((block, block), 0)
    jk = iota((block, block), 1)
    visible = (jk <= jq, (jk >> 4) < (jq >> 4) + core)
    moves = []
    for qb in range(1024 // block):
        q = q_scr[qb * block : (qb + 1) * block, :]
        pieces = []
        top = None
        for kb in range(qb + 1):
            for c in range(2):
                s = dot_t(q, k_scr[c, kb * block : (kb + 1) * block, :]) * SCALE
                if kb == qb:
                    s = jnp.where(visible[c], s, LOW)
                fold = jnp.maximum(s[:, :128], s[:, 128:])
                top = fold if top is None else jnp.maximum(top, fold)
                pieces.append((kb, c, s))
        m = jnp.max(top, axis=1, keepdims=True)
        total = jnp.zeros((block, 128), f32)
        acc = jnp.zeros((block, HD), f32)
        for kb, c, s in pieces:
            p = jnp.exp2(s - m)
            total = total + (p[:, :128] + p[:, 128:])
            acc = acc + dot(p.astype(bf16), v_scr[c, kb * block : (kb + 1) * block, :])
        total = jnp.sum(total, axis=1, keepdims=True)
        out = (acc / total).astype(bf16)
        for t in range(block // POS):
            y = dot(by_x, out[t * POS : (t + 1) * POS]).astype(bf16)
            at = (qb * block // POS + t) * STRIDE
            for x in range(4):
                out_scr[x, at : at + STRIDE, :] = y[x * STRIDE : (x + 1) * STRIDE]
        at = pl.ds(qb * block // 4, block // 4)
        move = pltpu.make_async_copy(out_scr.at[:, at, :], out_hbm.at[:, at, :], sems.at[2 + qb])
        move.start()
        moves.append(move)
    for move in moves:
        move.wait()


FAR_Q = 512
FAR_K = 1024
FAR_BLOCKS = PAIR // FAR_Q


def far_kernel(pair_ref, q_hbm, kv_hbm, out_hbm, q_ref, kv_ref, out_ref, s_scr, sems):
    pair = pair_ref[0]
    ins = [
        pltpu.make_async_copy(q_hbm, q_ref, sems.at[0]),
        pltpu.make_async_copy(kv_hbm, kv_ref, sems.at[1]),
    ]
    for move in ins:
        move.start()
    row_ids = PAIR // STRIDE
    last = (pair * row_ids) // FAR_K
    lane = iota((POS, 128), 1)
    eye = one_hot(SUM_ROWS, 128, lambda o: o)
    per = FAR_Q // POS
    planes = FAR_K // 256

    for move in ins:
        move.wait()

    def send(b):
        at = pl.ds(b * per, per)
        return pltpu.make_async_copy(out_ref.at[at], out_hbm.at[at], sems.at[2 + b])

    def piece(i, j):
        return jnp.concatenate([kv_ref[i * planes + t, j] for t in range(planes)], axis=0)

    def fold(x, op):
        r = x[:, :128]
        for t in range(1, FAR_K // 128):
            r = op(r, x[:, t * 128 : (t + 1) * 128])
        return r

    def block(b, unused):
        q = q_ref[pl.ds(b * per, per)].reshape(FAR_Q, HD)

        def score(i, top):
            s = dot_t(q, piece(i, 0)) * SCALE
            s_scr[i] = s
            return jnp.maximum(top, fold(s, jnp.maximum))

        top = lax.fori_loop(0, last, score, jnp.full((FAR_Q, 128), LOW, f32))
        s = dot_t(q, piece(last, 0)) * SCALE
        row_k = last * FAR_K + iota((FAR_Q, FAR_K), 1)
        row_q = pair * row_ids + ((b * FAR_Q + iota((FAR_Q, FAR_K), 0)) >> 5)
        s = jnp.where(row_k < row_q, s, LOW)
        s_scr[last] = s
        top = jnp.maximum(top, fold(s, jnp.maximum))
        m = jnp.max(top, axis=1, keepdims=True)

        def weigh(i, carried):
            total, acc = carried
            p = jnp.exp2(s_scr[i] - m)
            return (
                total + fold(p, jnp.add),
                acc + dot(p.astype(bf16), piece(i, 1)),
            )

        total, acc = lax.fori_loop(
            0,
            last + 1,
            weigh,
            (jnp.zeros((FAR_Q, 128), f32), jnp.zeros((FAR_Q, HD), f32)),
        )
        total = jnp.sum(total, axis=1, keepdims=True)
        out = (acc / total).astype(bf16)
        lse = jnp.where(m > 0.5 * LOW, m + jnp.log2(total), LOW)
        high = lse.astype(bf16).astype(f32)
        left = lse - high
        mid = left.astype(bf16).astype(f32)
        low = left - mid
        for e in range(per):
            at = slice(e * POS, (e + 1) * POS)
            terms = jnp.where(
                lane == 0,
                high[at],
                jnp.where(lane == 1, mid[at], jnp.where(lane == 2, low[at], 0.0)),
            ).astype(bf16)
            out_ref[b * per + e, :POS, :] = out[at]
            out_ref[b * per + e, POS:, :] = dot_t(eye, terms).astype(bf16)
        send(b).start()
        return unused

    lax.fori_loop(0, FAR_BLOCKS, block, 0)
    for b in range(FAR_BLOCKS):
        send(b).wait()


def final_kernel(
    far_hbm, col_hbm, row_hbm, part_hbm, stat_hbm, out_hbm,
    far_ref, col_ref, row_ref, part_ref, stat_ref, out_ref, sems,
):
    ins = [
        pltpu.make_async_copy(far_hbm, far_ref, sems.at[0]),
        pltpu.make_async_copy(stat_hbm, stat_ref, sems.at[12]),
        pltpu.make_async_copy(part_hbm, part_ref, sems.at[1]),
        pltpu.make_async_copy(col_hbm, col_ref, sems.at[2]),
        pltpu.make_async_copy(row_hbm, row_ref, sems.at[3]),
    ]
    for move in ins:
        move.start()
    back = one_hot(
        POS, POS, lambda o: (o & 3) * STRIDE + ((o >> 2) & 7) * 4 + (o >> 5)
    )
    row = iota((HEADS * SUM_ROWS, 128), 0)
    lane = iota((HEADS * SUM_ROWS, 128), 1)
    pick = jnp.where(
        jnp.logical_and((row >> 4) == lane, (row & 15) < 3), 1.0, 0.0
    ).astype(bf16)
    ins[0].wait()
    ins[1].wait()
    terms = jnp.concatenate([far_ref[g, POS:, :] for g in range(HEADS)], axis=0)
    lse = dot_tl(terms, pick)
    top = jnp.maximum(stat_ref[0], lse)
    own = jnp.exp2(stat_ref[0] - top)
    far = jnp.exp2(lse - top)
    scale = 1.0 / (stat_ref[1] * own + far)
    own = own * scale
    far = far * scale
    for move in ins[2:]:
        move.wait()
    moves = []
    for quad in range(QUADS):
        base = quad * 4 * HD
        out_ref[:, base : base + HD] = row_ref[quad]
        stack = jnp.concatenate(
            [col_ref[x, quad * STRIDE : (quad + 1) * STRIDE, :] for x in range(4)], axis=0
        )
        out_ref[:, base + HD : base + 2 * HD] = dot(back, stack).astype(bf16)
        for h in range(2):
            g = quad * 2 + h
            merged = (
                part_ref[g] * own[:, g : g + 1]
                + far_ref[g, :POS, :].astype(f32) * far[:, g : g + 1]
            )
            start = base + (2 + h) * HD
            out_ref[:, start : start + HD] = merged.astype(bf16)
        at = pl.ds(base, 4 * HD)
        move = pltpu.make_async_copy(out_ref.at[:, at], out_hbm.at[:, at], sems.at[4 + quad])
        move.start()
        moves.append(move)
    for move in moves:
        move.wait()


SPACES = {"v": pltpu.VMEM, "s": pltpu.SMEM, "h": pltpu.HBM, "a": pl.ANY}


def call(kernel, outs, args, ins, to="v", scratch=(), flops=0, moved=0, exps=0, alias=None):
    def spec(space):
        return pl.BlockSpec(memory_space=SPACES[space])

    shapes = [jax.ShapeDtypeStruct(s, d) for s, d in outs]
    many = len(shapes) > 1
    return pl.pallas_call(
        kernel,
        out_shape=shapes if many else shapes[0],
        in_specs=[spec(space) for space in ins],
        out_specs=[spec(to)] * len(shapes) if many else spec(to),
        scratch_shapes=list(scratch),
        input_output_aliases=alias or {},
        compiler_params=pltpu.CompilerParams(vmem_limit_bytes=60 * 1024 * 1024),
        cost_estimate=pl.CostEstimate(flops=flops, bytes_accessed=moved, transcendentals=exps),
    )(*args)


def exchange(array, axes):
    return lax.all_to_all(array, axes, split_axis=0, concat_axis=0, tiled=True)


def dma(n):
    return pltpu.SemaphoreType.DMA((n,))


mib = 1 << 20


def pack_summary(keys, values):
    return call(
        pack_summary_kernel,
        [((64, 8, HD), bf16)],
        (keys, values),
        "hh",
        to="h",
        scratch=[
            pltpu.VMEM((128, QUADS * 4 * HD), bf16),
            pltpu.VMEM((HEADS, 8, HD), bf16),
            dma(12),
        ],
        flops=2 * 16 * 16 * 128 * 128,
        moved=mib,
    )


def pack(queries, keys, values):
    return call(
        pack_kernel,
        [((QUADS, 384, HD), bf16), ((HEADS, POS, HD), bf16)],
        (queries, keys, values),
        "hhh",
        to="h",
        scratch=[
            pltpu.VMEM((QUADS, 384, HD), bf16),
            pltpu.VMEM((QUADS, 384, HD), bf16),
            dma(24),
            dma(24),
        ],
        flops=2 * 8 * 384 * 384 * 128,
        moved=4 * mib,
    )


def ordered(after, items):
    return call(
        order_kernel, [((QUADS, 384, HD), bf16)], (after, items), "aa", to="a", alias={1: 0}
    )


def rows(queries, keys, values):
    outs = [((QUADS, POS, HD), bf16), ((HEADS, POS, HD), f32), ((2, POS, 128), f32)]
    return call(
        rows_kernel,
        outs,
        (queries, keys, values),
        "hhh",
        to="h",
        scratch=[pltpu.VMEM((POS, QUADS * 4 * HD), bf16)] * 3
        + [pltpu.VMEM(*out) for out in outs]
        + [dma(13)],
        flops=24 * 4 * 128 * 128 * 128,
        moved=5 * mib,
        exps=24 * 128 * 128,
    )


def columns(core, items, other):
    return call(
        column_kernel,
        [((4, 256, HD), bf16)],
        (core, items, other),
        "shh",
        to="h",
        scratch=[
            pltpu.VMEM((3072, HD), bf16),
            pltpu.VMEM((3072, HD), bf16),
            pltpu.VMEM((4, 256, HD), bf16),
            pltpu.VMEM((1024, HD), bf16),
            pltpu.VMEM((2, 1024, HD), bf16),
            pltpu.VMEM((2, 1024, HD), bf16),
            dma(6),
        ],
        flops=4 * 1024 * 1280 * 128,
        moved=2 * mib,
        exps=1024 * 1280,
    )


def far_part(pair, heads, summary):
    return call(
        far_kernel,
        [((HEADS, PAY, HD), bf16)],
        (pair, heads, summary),
        "shh",
        to="h",
        scratch=[
            pltpu.VMEM((HEADS, POS, HD), bf16),
            pltpu.VMEM((8, 2, 256, HD), bf16),
            pltpu.VMEM((HEADS, PAY, HD), bf16),
            pltpu.VMEM((2048 // FAR_K, FAR_Q, FAR_K), f32),
            dma(2 + FAR_BLOCKS),
        ],
        flops=8 * 1024 * 2048 * 128,
        moved=3 * mib,
        exps=2 * 1024 * 2048,
    )


def final(far, column, row_out, part, stat):
    return call(
        final_kernel,
        [((POS, QUADS * 4 * HD), bf16)],
        (far, column, row_out, part, stat),
        "hhhhh",
        to="h",
        scratch=[
            pltpu.VMEM((HEADS, PAY, HD), bf16),
            pltpu.VMEM((4, 256, HD), bf16),
            pltpu.VMEM((QUADS, POS, HD), bf16),
            pltpu.VMEM((HEADS, POS, HD), f32),
            pltpu.VMEM((2, POS, 128), f32),
            pltpu.VMEM((POS, QUADS * 4 * HD), bf16),
            dma(13),
        ],
        flops=2 * 8 * 128 * 128 * 128,
        moved=4 * mib,
    )


def body(queries, keys, values):
    heads_at = ("w", "c", "x")
    plane = ("u", "v", "w", "c", "x")
    wide = ("z", "u", "v", "w", "x")
    back = ("x", "z", "u", "v", "w")
    summary = exchange(pack_summary(keys, values), plane)
    summary = summary.reshape(64, 2, ROWS, HD).transpose(1, 0, 2, 3).reshape(1, 2, 256, HD)
    items, heads = pack(queries, keys, values)
    items = ordered(summary, items)
    summary = lax.all_gather(summary, "z", axis=0, tiled=True)
    items = exchange(items.reshape(768, ROWS, HD), wide).reshape(3072, HD)
    heads = exchange(heads, heads_at)
    other = lax.ppermute(items, "c", [(0, 1), (1, 0)])
    core = lax.axis_index("c").astype(jnp.int32).reshape(1)
    column = columns(core, items, other)
    column = exchange(column.reshape(256, ROWS, HD), back).reshape(4, 256, HD)
    row_out, part, stat = rows(queries, keys, values)
    pair = lax.axis_index(("z", "u", "v")).astype(jnp.int32).reshape(1)
    far = exchange(far_part(pair, heads, summary), heads_at)
    return final(far, column, row_out, part, stat)


def solution(mesh):
    fine = Mesh(mesh.devices.reshape(4, 8, 2, 2, 2, 2), ("x", "z", "u", "v", "w", "c"))
    spec = P(("z", "u", "v", "w", "c", "x"), None)
    return jax.shard_map(
        body, mesh=fine, in_specs=(spec, spec, spec), out_specs=spec, check_vma=False
    )
```

```python
import math

import jax
import jax.numpy as jnp
from jax import lax
from jax.experimental import pallas as pl
from jax.experimental.pallas import tpu as pltpu
from jax.sharding import Mesh
from jax.sharding import PartitionSpec as P

HD = 128
STRIDE = 32
QUADS = 8
POS = 128
ROWS = 4
LOW = -1e30
SCALE = math.log2(math.e) / math.sqrt(HD)
SUM_ROWS = 16
PAY = POS + SUM_ROWS
HEADS = 16
PAIR = HEADS * POS

f32 = jnp.float32
bf16 = jnp.bfloat16


def dot_t(a, b):
    return lax.dot_general(a, b, (((1,), (1,)), ((), ())), preferred_element_type=f32)


def dot_tl(a, b):
    return lax.dot_general(a, b, (((0,), (0,)), ((), ())), preferred_element_type=f32)


def dot(a, b):
    return lax.dot_general(a, b, (((1,), (0,)), ((), ())), preferred_element_type=f32)


def iota(shape, dim):
    return lax.broadcasted_iota(jnp.int32, shape, dim)


def one_hot(rows, cols, source):
    row = iota((rows, cols), 0)
    col = iota((rows, cols), 1)
    return jnp.where(source(row) == col, 1.0, 0.0).astype(bf16)


def div12(o):
    return (o * 5462) >> 16


def head(ref, quad, kind):
    start = (quad * 4 + kind) * HD
    return ref[:, start : start + HD]


def pack_summary_kernel(k_ref, v_ref, sum_hbm, buf, sum_ref, sems):
    moves = []
    for a, ref in enumerate((k_ref, v_ref)):
        for r in range(ROWS):
            move = pltpu.make_async_copy(
                ref.at[pl.ds(r * STRIDE + 16, 16), :],
                buf.at[pl.ds((a * ROWS + r) * 16, 16), :],
                sems.at[a * ROWS + r],
            )
            move.start()
            moves.append(move)
    pick = one_hot(8, 128, lambda o: o * 16 + 15)
    for move in moves:
        move.wait()
    for g in range(HEADS):
        rows = dot(pick, head(buf, g // 2, 2 + g % 2)).astype(bf16)
        sum_ref[g] = rows
    moves = []
    for t in range(sum_hbm.shape[0] // HEADS):
        move = pltpu.make_async_copy(
            sum_ref, sum_hbm.at[pl.ds(t * HEADS, HEADS)], sems.at[2 * ROWS + t]
        )
        move.start()
        moves.append(move)
    for move in moves:
        move.wait()


def pack_kernel(q_hbm, k_hbm, v_hbm, item_hbm, query_hbm, qs, ks, vs, items, heads, ins, outs):
    def source(o):
        col = div12(o)
        rest = o - 12 * col
        return (rest >> 2) * POS + (rest & 3) * STRIDE + col

    def fetch(quad):
        at = quad * 4 * HD
        return [
            pltpu.make_async_copy(
                q_hbm.at[:, pl.ds(at + HD, 3 * HD)], qs.at[quad], ins.at[quad * 3]
            ),
            pltpu.make_async_copy(
                k_hbm.at[:, pl.ds(at + HD, HD)], ks.at[quad], ins.at[quad * 3 + 1]
            ),
            pltpu.make_async_copy(
                v_hbm.at[:, pl.ds(at + HD, HD)], vs.at[quad], ins.at[quad * 3 + 2]
            ),
        ]

    for quad in range(QUADS):
        for move in fetch(quad):
            move.start()
    perm = one_hot(384, 384, source)
    moves = []
    for quad in range(QUADS):
        for move in fetch(quad):
            move.wait()
        stack = jnp.concatenate([qs[quad, :, :HD], ks[quad], vs[quad]], axis=0)
        items[quad] = dot(perm, stack).astype(bf16)
        heads[quad * 2] = qs[quad, :, HD : 2 * HD]
        heads[quad * 2 + 1] = qs[quad, :, 2 * HD :]
        two = pl.ds(quad * 2, 2)
        for move in (
            pltpu.make_async_copy(items.at[quad], item_hbm.at[quad], outs.at[quad * 2]),
            pltpu.make_async_copy(heads.at[two], query_hbm.at[two], outs.at[quad * 2 + 1]),
        ):
            move.start()
            moves.append(move)
    for move in moves:
        move.wait()


def order_kernel(after_ref, item_ref, out_ref):
    pass


def rows_kernel(
    q_hbm, k_hbm, v_hbm, row_hbm, part_hbm, stat_hbm,
    q_ref, k_ref, v_ref, row_ref, part_ref, stat_ref, sems,
):
    ins = []
    for a, (hbm, ref) in enumerate(((q_hbm, q_ref), (k_hbm, k_ref), (v_hbm, v_ref))):
        move = pltpu.make_async_copy(hbm, ref, sems.at[a])
        move.start()
        ins.append(move)
    pos = iota((POS, POS), 0)
    key = iota((POS, POS), 1)
    visible = jnp.logical_and((key >> 5) == (pos >> 5), key <= pos)
    tops = jnp.zeros((POS, POS), f32)
    sums = jnp.ones((POS, POS), f32)
    for move in ins:
        move.wait()
    moves = []
    for quad in range(QUADS):
        for kind in (0, 2, 3):
            s = dot_t(head(q_ref, quad, kind), head(k_ref, quad, kind)) * SCALE
            s = jnp.where(visible, s, LOW)
            m = jnp.max(s, axis=1, keepdims=True)
            p = jnp.where(visible, jnp.exp2(s - m), 0.0)
            total = jnp.sum(p, axis=1, keepdims=True)
            acc = dot(p.astype(bf16), head(v_ref, quad, kind))
            if kind == 0:
                row_ref[quad] = (acc / total).astype(bf16)
            else:
                slot = quad * 2 + kind - 2
                part_ref[slot] = acc
                tops = jnp.where(key == slot, m, tops)
                sums = jnp.where(key == slot, total, sums)
        two = pl.ds(quad * 2, 2)
        moves.append(pltpu.make_async_copy(part_ref.at[two], part_hbm.at[two], sems.at[3 + quad]))
        moves[-1].start()
    stat_ref[0] = tops
    stat_ref[1] = sums
    moves.append(pltpu.make_async_copy(row_ref, row_hbm, sems.at[11]))
    moves.append(pltpu.make_async_copy(stat_ref, stat_hbm, sems.at[12]))
    moves[-1].start()
    moves[-2].start()
    for move in moves:
        move.wait()


def column_kernel(
    core_ref, own_hbm, other_hbm, out_hbm, own_ref, other_ref, out_scr, q_scr, k_scr, v_scr, sems
):
    core = core_ref[0]
    own_in = pltpu.make_async_copy(own_hbm, own_ref, sems.at[0])
    other_in = pltpu.make_async_copy(other_hbm, other_ref, sems.at[1])
    own_in.start()
    other_in.start()

    def source(o):
        within = o & 31
        return (within >> 2) * 12 + (o >> 5) * 4 + (within & 3)

    split = one_hot(96, 96, source)
    split_kv = one_hot(64, 96, lambda o: source(o + 32))
    by_x = one_hot(POS, POS, lambda o: ((o >> 2) & 7) * 16 + (o >> 5) * 4 + (o & 3))
    own_in.wait()
    for g in range(32):
        at = slice(g * 32, (g + 1) * 32)
        y = dot(split, own_ref[g * 96 : (g + 1) * 96, :]).astype(bf16)
        q_scr[at, :] = y[0:32]
        k_scr[0, at, :] = y[32:64]
        v_scr[0, at, :] = y[64:96]
    other_in.wait()
    for g in range(32):
        at = slice(g * 32, (g + 1) * 32)
        y = dot(split_kv, other_ref[g * 96 : (g + 1) * 96, :]).astype(bf16)
        k_scr[1, at, :] = y[0:32]
        v_scr[1, at, :] = y[32:64]

    block = 256
    jq = iota((block, block), 0)
    jk = iota((block, block), 1)
    visible = (jk <= jq, (jk >> 4) < (jq >> 4) + core)
    moves = []
    for qb in range(1024 // block):
        q = q_scr[qb * block : (qb + 1) * block, :]
        pieces = []
        top = None
        for kb in range(qb + 1):
            for c in range(2):
                s = dot_t(q, k_scr[c, kb * block : (kb + 1) * block, :]) * SCALE
                if kb == qb:
                    s = jnp.where(visible[c], s, LOW)
                fold = jnp.maximum(s[:, :128], s[:, 128:])
                top = fold if top is None else jnp.maximum(top, fold)
                pieces.append((kb, c, s))
        m = jnp.max(top, axis=1, keepdims=True)
        total = jnp.zeros((block, 128), f32)
        acc = jnp.zeros((block, HD), f32)
        for kb, c, s in pieces:
            p = jnp.exp2(s - m)
            total = total + (p[:, :128] + p[:, 128:])
            acc = acc + dot(p.astype(bf16), v_scr[c, kb * block : (kb + 1) * block, :])
        total = jnp.sum(total, axis=1, keepdims=True)
        out = (acc / total).astype(bf16)
        for t in range(block // POS):
            y = dot(by_x, out[t * POS : (t + 1) * POS]).astype(bf16)
            at = (qb * block // POS + t) * STRIDE
            for x in range(4):
                out_scr[x, at : at + STRIDE, :] = y[x * STRIDE : (x + 1) * STRIDE]
        at = pl.ds(qb * block // 4, block // 4)
        move = pltpu.make_async_copy(out_scr.at[:, at, :], out_hbm.at[:, at, :], sems.at[2 + qb])
        move.start()
        moves.append(move)
    for move in moves:
        move.wait()


FAR_Q = 1024
FAR_K = 2048
FAR_BLOCKS = PAIR // FAR_Q


def far_kernel(pair_ref, q_hbm, kv_hbm, out_hbm, q_ref, kv_ref, out_ref, s_scr, sems):
    pair = pair_ref[0]
    ins = [
        pltpu.make_async_copy(q_hbm, q_ref, sems.at[0]),
        pltpu.make_async_copy(kv_hbm, kv_ref, sems.at[1]),
    ]
    for move in ins:
        move.start()
    row_ids = PAIR // STRIDE
    last = (pair * row_ids) // FAR_K
    lane = iota((POS, 128), 1)
    eye = one_hot(SUM_ROWS, 128, lambda o: o)
    per = FAR_Q // POS
    planes = FAR_K // 256

    for move in ins:
        move.wait()

    def send(b):
        at = pl.ds(b * per, per)
        return pltpu.make_async_copy(out_ref.at[at], out_hbm.at[at], sems.at[2 + b])

    def piece(i, j):
        return jnp.concatenate([kv_ref[i * planes + t, j] for t in range(planes)], axis=0)

    def fold(x, op):
        r = x[:, :128]
        for t in range(1, FAR_K // 128):
            r = op(r, x[:, t * 128 : (t + 1) * 128])
        return r

    def block(b, unused):
        q = q_ref[pl.ds(b * per, per)].reshape(FAR_Q, HD)

        def score(i, top):
            s = dot_t(q, piece(i, 0)) * SCALE
            s_scr[i] = s
            return jnp.maximum(top, fold(s, jnp.maximum))

        top = lax.fori_loop(0, last, score, jnp.full((FAR_Q, 128), LOW, f32))
        s = dot_t(q, piece(last, 0)) * SCALE
        row_k = last * FAR_K + iota((FAR_Q, FAR_K), 1)
        row_q = pair * row_ids + ((b * FAR_Q + iota((FAR_Q, FAR_K), 0)) >> 5)
        s = jnp.where(row_k < row_q, s, LOW)
        s_scr[last] = s
        top = jnp.maximum(top, fold(s, jnp.maximum))
        m = jnp.max(top, axis=1, keepdims=True)

        def weigh(i, carried):
            total, acc = carried
            p = jnp.exp2(s_scr[i] - m)
            return (
                total + fold(p, jnp.add),
                acc + dot(p.astype(bf16), piece(i, 1)),
            )

        total, acc = lax.fori_loop(
            0,
            last + 1,
            weigh,
            (jnp.zeros((FAR_Q, 128), f32), jnp.zeros((FAR_Q, HD), f32)),
        )
        total = jnp.sum(total, axis=1, keepdims=True)
        out = (acc / total).astype(bf16)
        lse = jnp.where(m > 0.5 * LOW, m + jnp.log2(total), LOW)
        high = lse.astype(bf16).astype(f32)
        left = lse - high
        mid = left.astype(bf16).astype(f32)
        low = left - mid
        for e in range(per):
            at = slice(e * POS, (e + 1) * POS)
            terms = jnp.where(
                lane == 0,
                high[at],
                jnp.where(lane == 1, mid[at], jnp.where(lane == 2, low[at], 0.0)),
            ).astype(bf16)
            out_ref[b * per + e, :POS, :] = out[at]
            out_ref[b * per + e, POS:, :] = dot_t(eye, terms).astype(bf16)
        send(b).start()
        return unused

    lax.fori_loop(0, FAR_BLOCKS, block, 0)
    for b in range(FAR_BLOCKS):
        send(b).wait()


def final_kernel(
    far_hbm, col_hbm, row_hbm, part_hbm, stat_hbm, out_hbm,
    far_ref, col_ref, row_ref, part_ref, stat_ref, out_ref, sems,
):
    ins = [
        pltpu.make_async_copy(far_hbm, far_ref, sems.at[0]),
        pltpu.make_async_copy(stat_hbm, stat_ref, sems.at[12]),
        pltpu.make_async_copy(part_hbm, part_ref, sems.at[1]),
        pltpu.make_async_copy(col_hbm, col_ref, sems.at[2]),
        pltpu.make_async_copy(row_hbm, row_ref, sems.at[3]),
    ]
    for move in ins:
        move.start()
    back = one_hot(
        POS, POS, lambda o: (o & 3) * STRIDE + ((o >> 2) & 7) * 4 + (o >> 5)
    )
    row = iota((HEADS * SUM_ROWS, 128), 0)
    lane = iota((HEADS * SUM_ROWS, 128), 1)
    pick = jnp.where(
        jnp.logical_and((row >> 4) == lane, (row & 15) < 3), 1.0, 0.0
    ).astype(bf16)
    ins[0].wait()
    ins[1].wait()
    terms = jnp.concatenate([far_ref[g, POS:, :] for g in range(HEADS)], axis=0)
    lse = dot_tl(terms, pick)
    top = jnp.maximum(stat_ref[0], lse)
    own = jnp.exp2(stat_ref[0] - top)
    far = jnp.exp2(lse - top)
    scale = 1.0 / (stat_ref[1] * own + far)
    own = own * scale
    far = far * scale
    for move in ins[2:]:
        move.wait()
    moves = []
    for quad in range(QUADS):
        base = quad * 4 * HD
        out_ref[:, base : base + HD] = row_ref[quad]
        stack = jnp.concatenate(
            [col_ref[x, quad * STRIDE : (quad + 1) * STRIDE, :] for x in range(4)], axis=0
        )
        out_ref[:, base + HD : base + 2 * HD] = dot(back, stack).astype(bf16)
        for h in range(2):
            g = quad * 2 + h
            merged = (
                part_ref[g] * own[:, g : g + 1]
                + far_ref[g, :POS, :].astype(f32) * far[:, g : g + 1]
            )
            start = base + (2 + h) * HD
            out_ref[:, start : start + HD] = merged.astype(bf16)
        at = pl.ds(base, 4 * HD)
        move = pltpu.make_async_copy(out_ref.at[:, at], out_hbm.at[:, at], sems.at[4 + quad])
        move.start()
        moves.append(move)
    for move in moves:
        move.wait()


SPACES = {"v": pltpu.VMEM, "s": pltpu.SMEM, "h": pl.ANY}


def call(kernel, outs, args, ins, to="v", scratch=(), flops=0, moved=0, exps=0, alias=None):
    def spec(space):
        return pl.BlockSpec(memory_space=SPACES[space])

    shapes = [jax.ShapeDtypeStruct(s, d) for s, d in outs]
    many = len(shapes) > 1
    return pl.pallas_call(
        kernel,
        out_shape=shapes if many else shapes[0],
        in_specs=[spec(space) for space in ins],
        out_specs=[spec(to)] * len(shapes) if many else spec(to),
        scratch_shapes=list(scratch),
        input_output_aliases=alias or {},
        compiler_params=pltpu.CompilerParams(vmem_limit_bytes=60 * 1024 * 1024),
        cost_estimate=pl.CostEstimate(flops=flops, bytes_accessed=moved, transcendentals=exps),
    )(*args)


def exchange(array, axes):
    return lax.all_to_all(array, axes, split_axis=0, concat_axis=0, tiled=True)


def dma(n):
    return pltpu.SemaphoreType.DMA((n,))


mib = 1 << 20


def pack_summary(keys, values):
    return call(
        pack_summary_kernel,
        [((64, 8, HD), bf16)],
        (keys, values),
        "hh",
        to="h",
        scratch=[
            pltpu.VMEM((128, QUADS * 4 * HD), bf16),
            pltpu.VMEM((HEADS, 8, HD), bf16),
            dma(12),
        ],
        flops=2 * 16 * 16 * 128 * 128,
        moved=mib,
    )


def pack(queries, keys, values):
    return call(
        pack_kernel,
        [((QUADS, 384, HD), bf16), ((HEADS, POS, HD), bf16)],
        (queries, keys, values),
        "hhh",
        to="h",
        scratch=[
            pltpu.VMEM((QUADS, POS, 3 * HD), bf16),
            pltpu.VMEM((QUADS, POS, HD), bf16),
            pltpu.VMEM((QUADS, POS, HD), bf16),
            pltpu.VMEM((QUADS, 384, HD), bf16),
            pltpu.VMEM((HEADS, POS, HD), bf16),
            dma(24),
            dma(16),
        ],
        flops=2 * 8 * 384 * 384 * 128,
        moved=4 * mib,
    )


def ordered(after, items):
    return call(
        order_kernel, [((QUADS, 384, HD), bf16)], (after, items), "hh", to="h", alias={1: 0}
    )


def rows(queries, keys, values):
    outs = [((QUADS, POS, HD), bf16), ((HEADS, POS, HD), f32), ((2, POS, 128), f32)]
    return call(
        rows_kernel,
        outs,
        (queries, keys, values),
        "hhh",
        to="h",
        scratch=[pltpu.VMEM((POS, QUADS * 4 * HD), bf16)] * 3
        + [pltpu.VMEM(*out) for out in outs]
        + [dma(13)],
        flops=24 * 4 * 128 * 128 * 128,
        moved=5 * mib,
        exps=24 * 128 * 128,
    )


def columns(core, items, other):
    return call(
        column_kernel,
        [((4, 256, HD), bf16)],
        (core, items, other),
        "shh",
        to="h",
        scratch=[
            pltpu.VMEM((3072, HD), bf16),
            pltpu.VMEM((3072, HD), bf16),
            pltpu.VMEM((4, 256, HD), bf16),
            pltpu.VMEM((1024, HD), bf16),
            pltpu.VMEM((2, 1024, HD), bf16),
            pltpu.VMEM((2, 1024, HD), bf16),
            dma(6),
        ],
        flops=4 * 1024 * 1280 * 128,
        moved=2 * mib,
        exps=1024 * 1280,
    )


def far_part(pair, heads, summary):
    return call(
        far_kernel,
        [((HEADS, PAY, HD), bf16)],
        (pair, heads, summary),
        "shh",
        to="h",
        scratch=[
            pltpu.VMEM((HEADS, POS, HD), bf16),
            pltpu.VMEM((8, 2, 256, HD), bf16),
            pltpu.VMEM((HEADS, PAY, HD), bf16),
            pltpu.VMEM((2048 // FAR_K, FAR_Q, FAR_K), f32),
            dma(2 + FAR_BLOCKS),
        ],
        flops=8 * 1024 * 2048 * 128,
        moved=3 * mib,
        exps=2 * 1024 * 2048,
    )


def final(far, column, row_out, part, stat):
    return call(
        final_kernel,
        [((POS, QUADS * 4 * HD), bf16)],
        (far, column, row_out, part, stat),
        "hhhhh",
        to="h",
        scratch=[
            pltpu.VMEM((HEADS, PAY, HD), bf16),
            pltpu.VMEM((4, 256, HD), bf16),
            pltpu.VMEM((QUADS, POS, HD), bf16),
            pltpu.VMEM((HEADS, POS, HD), f32),
            pltpu.VMEM((2, POS, 128), f32),
            pltpu.VMEM((POS, QUADS * 4 * HD), bf16),
            dma(13),
        ],
        flops=2 * 8 * 128 * 128 * 128,
        moved=4 * mib,
    )


def body(queries, keys, values):
    heads_at = ("w", "c", "x")
    plane = ("u", "v", "w", "c", "x")
    wide = ("z", "u", "v", "w", "x")
    back = ("x", "z", "u", "v", "w")
    summary = exchange(pack_summary(keys, values), plane)
    summary = summary.reshape(64, 2, ROWS, HD).transpose(1, 0, 2, 3).reshape(1, 2, 256, HD)
    items, heads = pack(queries, keys, values)
    items = ordered(summary, items)
    summary = lax.all_gather(summary, "z", axis=0, tiled=True)
    items = exchange(items.reshape(768, ROWS, HD), wide).reshape(3072, HD)
    heads = exchange(heads, heads_at)
    other = lax.ppermute(items, "c", [(0, 1), (1, 0)])
    core = lax.axis_index("c").astype(jnp.int32).reshape(1)
    column = columns(core, items, other)
    column = exchange(column.reshape(256, ROWS, HD), back).reshape(4, 256, HD)
    row_out, part, stat = rows(queries, keys, values)
    pair = lax.axis_index(("z", "u", "v")).astype(jnp.int32).reshape(1)
    far = exchange(far_part(pair, heads, summary), heads_at)
    return final(far, column, row_out, part, stat)


def solution(mesh):
    fine = Mesh(mesh.devices.reshape(4, 8, 2, 2, 2, 2), ("x", "z", "u", "v", "w", "c"))
    spec = P(("z", "u", "v", "w", "c", "x"), None)
    return jax.shard_map(
        body, mesh=fine, in_specs=(spec, spec, spec), out_specs=spec, check_vma=False
    )
```

```python
import math

import jax
import jax.numpy as jnp
from jax import lax
from jax.experimental import pallas as pl
from jax.experimental.pallas import tpu as pltpu
from jax.sharding import Mesh
from jax.sharding import PartitionSpec as P

HD = 128
STRIDE = 32
QUADS = 8
POS = 128
ROWS = 4
LOW = -1e30
SCALE = math.log2(math.e) / math.sqrt(HD)
SUM_ROWS = 16
PAY = POS + SUM_ROWS
HEADS = 16
PAIR = HEADS * POS

f32 = jnp.float32
bf16 = jnp.bfloat16


def dot_t(a, b):
    return lax.dot_general(a, b, (((1,), (1,)), ((), ())), preferred_element_type=f32)


def dot_tl(a, b):
    return lax.dot_general(a, b, (((0,), (0,)), ((), ())), preferred_element_type=f32)


def dot(a, b):
    return lax.dot_general(a, b, (((1,), (0,)), ((), ())), preferred_element_type=f32)


def iota(shape, dim):
    return lax.broadcasted_iota(jnp.int32, shape, dim)


def one_hot(rows, cols, source):
    row = iota((rows, cols), 0)
    col = iota((rows, cols), 1)
    return jnp.where(source(row) == col, 1.0, 0.0).astype(bf16)


def div12(o):
    return (o * 5462) >> 16


def head(ref, quad, kind):
    start = (quad * 4 + kind) * HD
    return ref[:, start : start + HD]


def pack_summary_kernel(k_ref, v_ref, sum_hbm, buf, sum_ref, sems):
    moves = []
    for a, ref in enumerate((k_ref, v_ref)):
        for r in range(ROWS):
            move = pltpu.make_async_copy(
                ref.at[pl.ds(r * STRIDE + 16, 16), :],
                buf.at[pl.ds((a * ROWS + r) * 16, 16), :],
                sems.at[a * ROWS + r],
            )
            move.start()
            moves.append(move)
    pick = one_hot(8, 128, lambda o: o * 16 + 15)
    for move in moves:
        move.wait()
    for g in range(HEADS):
        rows = dot(pick, head(buf, g // 2, 2 + g % 2)).astype(bf16)
        sum_ref[g] = rows
    moves = []
    for t in range(sum_hbm.shape[0] // HEADS):
        move = pltpu.make_async_copy(
            sum_ref, sum_hbm.at[pl.ds(t * HEADS, HEADS)], sems.at[2 * ROWS + t]
        )
        move.start()
        moves.append(move)
    for move in moves:
        move.wait()


def pack_kernel(q_hbm, k_hbm, v_hbm, item_hbm, query_hbm, qs, ks, vs, items, heads, ins, outs):
    def source(o):
        col = div12(o)
        rest = o - 12 * col
        return (rest >> 2) * POS + (rest & 3) * STRIDE + col

    def fetch(quad):
        at = quad * 4 * HD
        return [
            pltpu.make_async_copy(
                q_hbm.at[:, pl.ds(at + HD, 3 * HD)], qs.at[quad], ins.at[quad * 3]
            ),
            pltpu.make_async_copy(
                k_hbm.at[:, pl.ds(at + HD, HD)], ks.at[quad], ins.at[quad * 3 + 1]
            ),
            pltpu.make_async_copy(
                v_hbm.at[:, pl.ds(at + HD, HD)], vs.at[quad], ins.at[quad * 3 + 2]
            ),
        ]

    for quad in range(QUADS):
        for move in fetch(quad):
            move.start()
    perm = one_hot(384, 384, source)
    moves = []
    for quad in range(QUADS):
        for move in fetch(quad):
            move.wait()
        stack = jnp.concatenate([qs[quad, :, :HD], ks[quad], vs[quad]], axis=0)
        items[quad] = dot(perm, stack).astype(bf16)
        heads[quad * 2] = qs[quad, :, HD : 2 * HD]
        heads[quad * 2 + 1] = qs[quad, :, 2 * HD :]
        two = pl.ds(quad * 2, 2)
        for move in (
            pltpu.make_async_copy(items.at[quad], item_hbm.at[quad], outs.at[quad * 2]),
            pltpu.make_async_copy(heads.at[two], query_hbm.at[two], outs.at[quad * 2 + 1]),
        ):
            move.start()
            moves.append(move)
    for move in moves:
        move.wait()


def order_kernel(after_ref, item_ref, out_ref):
    pass


def rows_kernel(
    q_hbm, k_hbm, v_hbm, row_hbm, part_hbm, stat_hbm,
    q_ref, k_ref, v_ref, row_ref, part_ref, stat_ref, sems,
):
    ins = []
    for a, (hbm, ref) in enumerate(((q_hbm, q_ref), (k_hbm, k_ref), (v_hbm, v_ref))):
        move = pltpu.make_async_copy(hbm, ref, sems.at[a])
        move.start()
        ins.append(move)
    pos = iota((POS, POS), 0)
    key = iota((POS, POS), 1)
    visible = jnp.logical_and((key >> 5) == (pos >> 5), key <= pos)
    tops = jnp.zeros((POS, POS), f32)
    sums = jnp.ones((POS, POS), f32)
    for move in ins:
        move.wait()
    moves = []
    for quad in range(QUADS):
        for kind in (0, 2, 3):
            s = dot_t(head(q_ref, quad, kind), head(k_ref, quad, kind)) * SCALE
            s = jnp.where(visible, s, LOW)
            m = jnp.max(s, axis=1, keepdims=True)
            p = jnp.where(visible, jnp.exp2(s - m), 0.0)
            total = jnp.sum(p, axis=1, keepdims=True)
            acc = dot(p.astype(bf16), head(v_ref, quad, kind))
            if kind == 0:
                row_ref[quad] = (acc / total).astype(bf16)
            else:
                slot = quad * 2 + kind - 2
                part_ref[slot] = acc
                tops = jnp.where(key == slot, m, tops)
                sums = jnp.where(key == slot, total, sums)
        two = pl.ds(quad * 2, 2)
        moves.append(pltpu.make_async_copy(part_ref.at[two], part_hbm.at[two], sems.at[3 + quad]))
        moves[-1].start()
    stat_ref[0] = tops
    stat_ref[1] = sums
    moves.append(pltpu.make_async_copy(row_ref, row_hbm, sems.at[11]))
    moves.append(pltpu.make_async_copy(stat_ref, stat_hbm, sems.at[12]))
    moves[-1].start()
    moves[-2].start()
    for move in moves:
        move.wait()


def column_kernel(
    core_ref, after_ref, own_ref, other_ref, out_hbm, out_scr, q_scr, k_scr, v_scr, sems
):
    core = core_ref[0]

    def source(o):
        within = o & 31
        return (within >> 2) * 12 + (o >> 5) * 4 + (within & 3)

    split = one_hot(96, 96, source)
    split_kv = one_hot(64, 96, lambda o: source(o + 32))
    by_x = one_hot(POS, POS, lambda o: ((o >> 2) & 7) * 16 + (o >> 5) * 4 + (o & 3))
    for g in range(32):
        at = slice(g * 32, (g + 1) * 32)
        y = dot(split, own_ref[g * 96 : (g + 1) * 96, :]).astype(bf16)
        q_scr[at, :] = y[0:32]
        k_scr[0, at, :] = y[32:64]
        v_scr[0, at, :] = y[64:96]
        y = dot(split_kv, other_ref[g * 96 : (g + 1) * 96, :]).astype(bf16)
        k_scr[1, at, :] = y[0:32]
        v_scr[1, at, :] = y[32:64]

    block = 256
    jq = iota((block, block), 0)
    jk = iota((block, block), 1)
    visible = (jk <= jq, (jk >> 4) < (jq >> 4) + core)
    moves = []
    for qb in range(1024 // block):
        q = q_scr[qb * block : (qb + 1) * block, :]
        pieces = []
        top = None
        for kb in range(qb + 1):
            for c in range(2):
                s = dot_t(q, k_scr[c, kb * block : (kb + 1) * block, :]) * SCALE
                if kb == qb:
                    s = jnp.where(visible[c], s, LOW)
                fold = jnp.maximum(s[:, :128], s[:, 128:])
                top = fold if top is None else jnp.maximum(top, fold)
                pieces.append((kb, c, s))
        m = jnp.max(top, axis=1, keepdims=True)
        total = jnp.zeros((block, 128), f32)
        acc = jnp.zeros((block, HD), f32)
        for kb, c, s in pieces:
            p = jnp.exp2(s - m)
            total = total + (p[:, :128] + p[:, 128:])
            acc = acc + dot(p.astype(bf16), v_scr[c, kb * block : (kb + 1) * block, :])
        total = jnp.sum(total, axis=1, keepdims=True)
        out = (acc / total).astype(bf16)
        for t in range(block // POS):
            y = dot(by_x, out[t * POS : (t + 1) * POS]).astype(bf16)
            at = (qb * block // POS + t) * STRIDE
            for x in range(4):
                out_scr[x, at : at + STRIDE, :] = y[x * STRIDE : (x + 1) * STRIDE]
        at = pl.ds(qb * block // 4, block // 4)
        move = pltpu.make_async_copy(out_scr.at[:, at, :], out_hbm.at[:, at, :], sems.at[qb])
        move.start()
        moves.append(move)
    for move in moves:
        move.wait()


FAR_Q = 1024
FAR_K = 2048
FAR_BLOCKS = PAIR // FAR_Q


def far_kernel(pair_ref, q_hbm, kv_hbm, out_hbm, q_ref, kv_ref, out_ref, s_scr, sems):
    pair = pair_ref[0]
    ins = [
        pltpu.make_async_copy(q_hbm, q_ref, sems.at[0]),
        pltpu.make_async_copy(kv_hbm, kv_ref, sems.at[1]),
    ]
    for move in ins:
        move.start()
    row_ids = PAIR // STRIDE
    last = (pair * row_ids) // FAR_K
    lane = iota((POS, 128), 1)
    eye = one_hot(SUM_ROWS, 128, lambda o: o)
    per = FAR_Q // POS
    planes = FAR_K // 256

    for move in ins:
        move.wait()

    def send(b):
        at = pl.ds(b * per, per)
        return pltpu.make_async_copy(out_ref.at[at], out_hbm.at[at], sems.at[2 + b])

    def piece(i, j):
        return jnp.concatenate([kv_ref[i * planes + t, j] for t in range(planes)], axis=0)

    def fold(x, op):
        r = x[:, :128]
        for t in range(1, FAR_K // 128):
            r = op(r, x[:, t * 128 : (t + 1) * 128])
        return r

    def block(b, unused):
        q = q_ref[pl.ds(b * per, per)].reshape(FAR_Q, HD)

        def score(i, top):
            s = dot_t(q, piece(i, 0)) * SCALE
            s_scr[i] = s
            return jnp.maximum(top, fold(s, jnp.maximum))

        top = lax.fori_loop(0, last, score, jnp.full((FAR_Q, 128), LOW, f32))
        s = dot_t(q, piece(last, 0)) * SCALE
        row_k = last * FAR_K + iota((FAR_Q, FAR_K), 1)
        row_q = pair * row_ids + ((b * FAR_Q + iota((FAR_Q, FAR_K), 0)) >> 5)
        s = jnp.where(row_k < row_q, s, LOW)
        s_scr[last] = s
        top = jnp.maximum(top, fold(s, jnp.maximum))
        m = jnp.max(top, axis=1, keepdims=True)

        def weigh(i, carried):
            total, acc = carried
            p = jnp.exp2(s_scr[i] - m)
            return (
                total + fold(p, jnp.add),
                acc + dot(p.astype(bf16), piece(i, 1)),
            )

        total, acc = lax.fori_loop(
            0,
            last + 1,
            weigh,
            (jnp.zeros((FAR_Q, 128), f32), jnp.zeros((FAR_Q, HD), f32)),
        )
        total = jnp.sum(total, axis=1, keepdims=True)
        out = (acc / total).astype(bf16)
        lse = jnp.where(m > 0.5 * LOW, m + jnp.log2(total), LOW)
        high = lse.astype(bf16).astype(f32)
        left = lse - high
        mid = left.astype(bf16).astype(f32)
        low = left - mid
        for e in range(per):
            at = slice(e * POS, (e + 1) * POS)
            terms = jnp.where(
                lane == 0,
                high[at],
                jnp.where(lane == 1, mid[at], jnp.where(lane == 2, low[at], 0.0)),
            ).astype(bf16)
            out_ref[b * per + e, :POS, :] = out[at]
            out_ref[b * per + e, POS:, :] = dot_t(eye, terms).astype(bf16)
        send(b).start()
        return unused

    lax.fori_loop(0, FAR_BLOCKS, block, 0)
    for b in range(FAR_BLOCKS):
        send(b).wait()


def final_kernel(
    far_ref, col_ref, row_hbm, part_hbm, stat_hbm, out_hbm,
    row_ref, part_ref, stat_ref, out_ref, sems,
):
    ins = [
        pltpu.make_async_copy(stat_hbm, stat_ref, sems.at[0]),
        pltpu.make_async_copy(part_hbm, part_ref, sems.at[1]),
        pltpu.make_async_copy(row_hbm, row_ref, sems.at[2]),
    ]
    for move in ins:
        move.start()
    back = one_hot(
        POS, POS, lambda o: (o & 3) * STRIDE + ((o >> 2) & 7) * 4 + (o >> 5)
    )
    row = iota((HEADS * SUM_ROWS, 128), 0)
    lane = iota((HEADS * SUM_ROWS, 128), 1)
    pick = jnp.where(
        jnp.logical_and((row >> 4) == lane, (row & 15) < 3), 1.0, 0.0
    ).astype(bf16)
    ins[0].wait()
    terms = jnp.concatenate([far_ref[g, POS:, :] for g in range(HEADS)], axis=0)
    lse = dot_tl(terms, pick)
    top = jnp.maximum(stat_ref[0], lse)
    own = jnp.exp2(stat_ref[0] - top)
    far = jnp.exp2(lse - top)
    scale = 1.0 / (stat_ref[1] * own + far)
    own = own * scale
    far = far * scale
    for move in ins[1:]:
        move.wait()
    moves = []
    for quad in range(QUADS):
        base = quad * 4 * HD
        out_ref[:, base : base + HD] = row_ref[quad]
        stack = jnp.concatenate(
            [col_ref[x, quad * STRIDE : (quad + 1) * STRIDE, :] for x in range(4)], axis=0
        )
        out_ref[:, base + HD : base + 2 * HD] = dot(back, stack).astype(bf16)
        for h in range(2):
            g = quad * 2 + h
            merged = (
                part_ref[g] * own[:, g : g + 1]
                + far_ref[g, :POS, :].astype(f32) * far[:, g : g + 1]
            )
            start = base + (2 + h) * HD
            out_ref[:, start : start + HD] = merged.astype(bf16)
        at = pl.ds(base, 4 * HD)
        move = pltpu.make_async_copy(out_ref.at[:, at], out_hbm.at[:, at], sems.at[3 + quad])
        move.start()
        moves.append(move)
    for move in moves:
        move.wait()


VMEM_BYTES = 63_000_000
SPACES = {"v": pltpu.VMEM, "s": pltpu.SMEM, "h": pl.ANY}


def call(kernel, outs, args, ins, to="v", scratch=(), flops=0, moved=0, exps=0, alias=None, room=0):
    def spec(space):
        return pl.BlockSpec(memory_space=SPACES[space])

    shapes = [jax.ShapeDtypeStruct(s, d) for s, d in outs]
    many = len(shapes) > 1
    return pl.pallas_call(
        kernel,
        out_shape=shapes if many else shapes[0],
        in_specs=[spec(space) for space in ins],
        out_specs=[spec(to)] * len(shapes) if many else spec(to),
        scratch_shapes=list(scratch),
        input_output_aliases=alias or {},
        compiler_params=pltpu.CompilerParams(vmem_limit_bytes=VMEM_BYTES - room),
        cost_estimate=pl.CostEstimate(flops=flops, bytes_accessed=moved, transcendentals=exps),
    )(*args)


def exchange(array, axes):
    return lax.all_to_all(array, axes, split_axis=0, concat_axis=0, tiled=True)


def dma(n):
    return pltpu.SemaphoreType.DMA((n,))


mib = 1 << 20


def pack_summary(keys, values):
    return call(
        pack_summary_kernel,
        [((64, 8, HD), bf16)],
        (keys, values),
        "hh",
        to="h",
        scratch=[
            pltpu.VMEM((128, QUADS * 4 * HD), bf16),
            pltpu.VMEM((HEADS, 8, HD), bf16),
            dma(12),
        ],
        flops=2 * 16 * 16 * 128 * 128,
        moved=mib,
    )


def pack(queries, keys, values):
    return call(
        pack_kernel,
        [((QUADS, 384, HD), bf16), ((HEADS, POS, HD), bf16)],
        (queries, keys, values),
        "hhh",
        to="h",
        scratch=[
            pltpu.VMEM((QUADS, POS, 3 * HD), bf16),
            pltpu.VMEM((QUADS, POS, HD), bf16),
            pltpu.VMEM((QUADS, POS, HD), bf16),
            pltpu.VMEM((QUADS, 384, HD), bf16),
            pltpu.VMEM((HEADS, POS, HD), bf16),
            dma(24),
            dma(16),
        ],
        flops=2 * 8 * 384 * 384 * 128,
        moved=4 * mib,
    )


def ordered(after, items):
    return call(
        order_kernel, [((QUADS, 384, HD), bf16)], (after, items), "hh", to="h", alias={1: 0}
    )


def rows(queries, keys, values):
    outs = [((QUADS, POS, HD), bf16), ((HEADS, POS, HD), f32), ((2, POS, 128), f32)]
    return call(
        rows_kernel,
        outs,
        (queries, keys, values),
        "hhh",
        to="h",
        scratch=[pltpu.VMEM((POS, QUADS * 4 * HD), bf16)] * 3
        + [pltpu.VMEM(*out) for out in outs]
        + [dma(13)],
        room=1_250_000,
        flops=24 * 4 * 128 * 128 * 128,
        moved=5 * mib,
        exps=24 * 128 * 128,
    )


def columns(core, after, items, other):
    return call(
        column_kernel,
        [((4, 256, HD), bf16)],
        (core, after, items, other),
        "shvv",
        to="h",
        scratch=[
            pltpu.VMEM((4, 256, HD), bf16),
            pltpu.VMEM((1024, HD), bf16),
            pltpu.VMEM((2, 1024, HD), bf16),
            pltpu.VMEM((2, 1024, HD), bf16),
            dma(4),
        ],
        room=1_250_000,
        flops=4 * 1024 * 1280 * 128,
        moved=2 * mib,
        exps=1024 * 1280,
    )


def far_part(pair, heads, summary):
    return call(
        far_kernel,
        [((HEADS, PAY, HD), bf16)],
        (pair, heads, summary),
        "shh",
        to="h",
        scratch=[
            pltpu.VMEM((HEADS, POS, HD), bf16),
            pltpu.VMEM((8, 2, 256, HD), bf16),
            pltpu.VMEM((HEADS, PAY, HD), bf16),
            pltpu.VMEM((2048 // FAR_K, FAR_Q, FAR_K), f32),
            dma(2 + FAR_BLOCKS),
        ],
        flops=8 * 1024 * 2048 * 128,
        moved=3 * mib,
        exps=2 * 1024 * 2048,
    )


def final(far, column, row_out, part, stat):
    return call(
        final_kernel,
        [((POS, QUADS * 4 * HD), bf16)],
        (far, column, row_out, part, stat),
        "vvhhh",
        to="h",
        scratch=[
            pltpu.VMEM((QUADS, POS, HD), bf16),
            pltpu.VMEM((HEADS, POS, HD), f32),
            pltpu.VMEM((2, POS, 128), f32),
            pltpu.VMEM((POS, QUADS * 4 * HD), bf16),
            dma(11),
        ],
        room=500_000,
        flops=2 * 8 * 128 * 128 * 128,
        moved=4 * mib,
    )


def body(queries, keys, values):
    heads_at = ("w", "c", "x")
    plane = ("u", "v", "w", "c", "x")
    wide = ("z", "u", "v", "w", "x")
    back = ("x", "z", "u", "v", "w")
    summary = exchange(pack_summary(keys, values), plane)
    summary = summary.reshape(64, 2, ROWS, HD).transpose(1, 0, 2, 3).reshape(1, 2, 256, HD)
    items, heads = pack(queries, keys, values)
    items = ordered(summary, items)
    summary = lax.all_gather(summary, "z", axis=0, tiled=True)
    items = exchange(items.reshape(768, ROWS, HD), wide).reshape(3072, HD)
    heads = exchange(heads, heads_at)
    other = lax.ppermute(items, "c", [(0, 1), (1, 0)])
    core = lax.axis_index("c").astype(jnp.int32).reshape(1)
    row_out, part, stat = rows(queries, keys, values)
    column = columns(core, stat, items, other)
    column = exchange(column.reshape(256, ROWS, HD), back).reshape(4, 256, HD)
    pair = lax.axis_index(("z", "u", "v")).astype(jnp.int32).reshape(1)
    far = exchange(far_part(pair, heads, summary), heads_at)
    return final(far, column, row_out, part, stat)


def solution(mesh):
    fine = Mesh(mesh.devices.reshape(4, 8, 2, 2, 2, 2), ("x", "z", "u", "v", "w", "c"))
    spec = P(("z", "u", "v", "w", "c", "x"), None)
    return jax.shard_map(
        body, mesh=fine, in_specs=(spec, spec, spec), out_specs=spec, check_vma=False
    )
```

```python
import math

import jax
import jax.numpy as jnp
from jax import lax
from jax.experimental import pallas as pl
from jax.experimental.pallas import tpu as pltpu
from jax.sharding import Mesh
from jax.sharding import PartitionSpec as P

HD = 128
STRIDE = 32
QUADS = 8
POS = 128
ROWS = 4
LOW = -1e30
SCALE = math.log2(math.e) / math.sqrt(HD)
SUM_ROWS = 16
PAY = POS + SUM_ROWS
HEADS = 16
PAIR = HEADS * POS

f32 = jnp.float32
bf16 = jnp.bfloat16


def dot_t(a, b):
    return lax.dot_general(a, b, (((1,), (1,)), ((), ())), preferred_element_type=f32)


def dot_tl(a, b):
    return lax.dot_general(a, b, (((0,), (0,)), ((), ())), preferred_element_type=f32)


def dot(a, b):
    return lax.dot_general(a, b, (((1,), (0,)), ((), ())), preferred_element_type=f32)


def iota(shape, dim):
    return lax.broadcasted_iota(jnp.int32, shape, dim)


def one_hot(rows, cols, source):
    row = iota((rows, cols), 0)
    col = iota((rows, cols), 1)
    return jnp.where(source(row) == col, 1.0, 0.0).astype(bf16)


def div12(o):
    return (o * 5462) >> 16


def head(ref, quad, kind):
    start = (quad * 4 + kind) * HD
    return ref[:, start : start + HD]


def pack_summary_kernel(k_ref, v_ref, sum_hbm, buf, sum_ref, sems):
    moves = []
    for a, ref in enumerate((k_ref, v_ref)):
        for r in range(ROWS):
            move = pltpu.make_async_copy(
                ref.at[pl.ds(r * STRIDE + 16, 16), :],
                buf.at[pl.ds((a * ROWS + r) * 16, 16), :],
                sems.at[a * ROWS + r],
            )
            move.start()
            moves.append(move)
    pick = one_hot(8, 128, lambda o: o * 16 + 15)
    for move in moves:
        move.wait()
    for g in range(HEADS):
        rows = dot(pick, head(buf, g // 2, 2 + g % 2)).astype(bf16)
        sum_ref[g] = rows
    moves = []
    for t in range(sum_hbm.shape[0] // HEADS):
        move = pltpu.make_async_copy(
            sum_ref, sum_hbm.at[pl.ds(t * HEADS, HEADS)], sems.at[2 * ROWS + t]
        )
        move.start()
        moves.append(move)
    for move in moves:
        move.wait()


def pack_kernel(q_hbm, k_hbm, v_hbm, item_hbm, query_hbm, qs, ks, vs, items, heads, ins, outs):
    def source(o):
        col = div12(o)
        rest = o - 12 * col
        return (rest >> 2) * POS + (rest & 3) * STRIDE + col

    def fetch(quad):
        at = quad * 4 * HD
        return [
            pltpu.make_async_copy(
                q_hbm.at[:, pl.ds(at + HD, 3 * HD)], qs.at[quad], ins.at[quad * 3]
            ),
            pltpu.make_async_copy(
                k_hbm.at[:, pl.ds(at + HD, HD)], ks.at[quad], ins.at[quad * 3 + 1]
            ),
            pltpu.make_async_copy(
                v_hbm.at[:, pl.ds(at + HD, HD)], vs.at[quad], ins.at[quad * 3 + 2]
            ),
        ]

    for quad in range(QUADS):
        for move in fetch(quad):
            move.start()
    perm = one_hot(384, 384, source)
    moves = []
    for quad in range(QUADS):
        for move in fetch(quad):
            move.wait()
        stack = jnp.concatenate([qs[quad, :, :HD], ks[quad], vs[quad]], axis=0)
        items[quad] = dot(perm, stack).astype(bf16)
        heads[quad * 2] = qs[quad, :, HD : 2 * HD]
        heads[quad * 2 + 1] = qs[quad, :, 2 * HD :]
        two = pl.ds(quad * 2, 2)
        for move in (
            pltpu.make_async_copy(items.at[quad], item_hbm.at[quad], outs.at[quad * 2]),
            pltpu.make_async_copy(heads.at[two], query_hbm.at[two], outs.at[quad * 2 + 1]),
        ):
            move.start()
            moves.append(move)
    for move in moves:
        move.wait()


def order_kernel(after_ref, item_ref, out_ref):
    pass


def rows_kernel(
    q_hbm, k_hbm, v_hbm, row_hbm, part_hbm, stat_hbm,
    q_ref, k_ref, v_ref, row_ref, part_ref, stat_ref, sems,
):
    ins = []
    for a, (hbm, ref) in enumerate(((q_hbm, q_ref), (k_hbm, k_ref), (v_hbm, v_ref))):
        move = pltpu.make_async_copy(hbm, ref, sems.at[a])
        move.start()
        ins.append(move)
    pos = iota((POS, POS), 0)
    key = iota((POS, POS), 1)
    visible = jnp.logical_and((key >> 5) == (pos >> 5), key <= pos)
    tops = jnp.zeros((POS, POS), f32)
    sums = jnp.ones((POS, POS), f32)
    for move in ins:
        move.wait()
    moves = []
    for quad in range(QUADS):
        for kind in (0, 2, 3):
            s = dot_t(head(q_ref, quad, kind), head(k_ref, quad, kind)) * SCALE
            s = jnp.where(visible, s, LOW)
            m = jnp.max(s, axis=1, keepdims=True)
            p = jnp.where(visible, jnp.exp2(s - m), 0.0)
            total = jnp.sum(p, axis=1, keepdims=True)
            acc = dot(p.astype(bf16), head(v_ref, quad, kind))
            if kind == 0:
                row_ref[quad] = (acc / total).astype(bf16)
            else:
                slot = quad * 2 + kind - 2
                part_ref[slot] = acc
                tops = jnp.where(key == slot, m, tops)
                sums = jnp.where(key == slot, total, sums)
        two = pl.ds(quad * 2, 2)
        moves.append(pltpu.make_async_copy(part_ref.at[two], part_hbm.at[two], sems.at[3 + quad]))
        moves[-1].start()
    stat_ref[0] = tops
    stat_ref[1] = sums
    moves.append(pltpu.make_async_copy(row_ref, row_hbm, sems.at[11]))
    moves.append(pltpu.make_async_copy(stat_ref, stat_hbm, sems.at[12]))
    moves[-1].start()
    moves[-2].start()
    for move in moves:
        move.wait()


def column_kernel(
    core_ref, own_ref, other_ref, out_hbm, out_scr, q_scr, k_scr, v_scr, sems
):
    core = core_ref[0]

    def source(o):
        within = o & 31
        return (within >> 2) * 12 + (o >> 5) * 4 + (within & 3)

    split = one_hot(96, 96, source)
    split_kv = one_hot(64, 96, lambda o: source(o + 32))
    by_x = one_hot(POS, POS, lambda o: ((o >> 2) & 7) * 16 + (o >> 5) * 4 + (o & 3))
    for g in range(32):
        at = slice(g * 32, (g + 1) * 32)
        y = dot(split, own_ref[g * 96 : (g + 1) * 96, :]).astype(bf16)
        q_scr[at, :] = y[0:32]
        k_scr[0, at, :] = y[32:64]
        v_scr[0, at, :] = y[64:96]
        y = dot(split_kv, other_ref[g * 96 : (g + 1) * 96, :]).astype(bf16)
        k_scr[1, at, :] = y[0:32]
        v_scr[1, at, :] = y[32:64]

    block = 256
    jq = iota((block, block), 0)
    jk = iota((block, block), 1)
    visible = (jk <= jq, (jk >> 4) < (jq >> 4) + core)
    moves = []
    for qb in range(1024 // block):
        q = q_scr[qb * block : (qb + 1) * block, :]
        pieces = []
        top = None
        for kb in range(qb + 1):
            for c in range(2):
                s = dot_t(q, k_scr[c, kb * block : (kb + 1) * block, :]) * SCALE
                if kb == qb:
                    s = jnp.where(visible[c], s, LOW)
                fold = jnp.maximum(s[:, :128], s[:, 128:])
                top = fold if top is None else jnp.maximum(top, fold)
                pieces.append((kb, c, s))
        m = jnp.max(top, axis=1, keepdims=True)
        total = jnp.zeros((block, 128), f32)
        acc = jnp.zeros((block, HD), f32)
        for kb, c, s in pieces:
            p = jnp.exp2(s - m)
            total = total + (p[:, :128] + p[:, 128:])
            acc = acc + dot(p.astype(bf16), v_scr[c, kb * block : (kb + 1) * block, :])
        total = jnp.sum(total, axis=1, keepdims=True)
        out = (acc / total).astype(bf16)
        for t in range(block // POS):
            y = dot(by_x, out[t * POS : (t + 1) * POS]).astype(bf16)
            at = (qb * block // POS + t) * STRIDE
            for x in range(4):
                out_scr[x, at : at + STRIDE, :] = y[x * STRIDE : (x + 1) * STRIDE]
        at = pl.ds(qb * block // 4, block // 4)
        move = pltpu.make_async_copy(out_scr.at[:, at, :], out_hbm.at[:, at, :], sems.at[qb])
        move.start()
        moves.append(move)
    for move in moves:
        move.wait()


FAR_Q = 1024
FAR_K = 2048
FAR_BLOCKS = PAIR // FAR_Q


def far_kernel(pair_ref, q_hbm, kv_hbm, out_hbm, q_ref, kv_ref, out_ref, s_scr, sems):
    pair = pair_ref[0]
    ins = [
        pltpu.make_async_copy(q_hbm, q_ref, sems.at[0]),
        pltpu.make_async_copy(kv_hbm, kv_ref, sems.at[1]),
    ]
    for move in ins:
        move.start()
    row_ids = PAIR // STRIDE
    last = (pair * row_ids) // FAR_K
    lane = iota((POS, 128), 1)
    eye = one_hot(SUM_ROWS, 128, lambda o: o)
    per = FAR_Q // POS
    planes = FAR_K // 256

    for move in ins:
        move.wait()

    def send(b):
        at = pl.ds(b * per, per)
        return pltpu.make_async_copy(out_ref.at[at], out_hbm.at[at], sems.at[2 + b])

    def piece(i, j):
        return jnp.concatenate([kv_ref[i * planes + t, j] for t in range(planes)], axis=0)

    def fold(x, op):
        r = x[:, :128]
        for t in range(1, FAR_K // 128):
            r = op(r, x[:, t * 128 : (t + 1) * 128])
        return r

    def block(b, unused):
        q = q_ref[pl.ds(b * per, per)].reshape(FAR_Q, HD)

        def score(i, top):
            s = dot_t(q, piece(i, 0)) * SCALE
            s_scr[i] = s
            return jnp.maximum(top, fold(s, jnp.maximum))

        top = lax.fori_loop(0, last, score, jnp.full((FAR_Q, 128), LOW, f32))
        s = dot_t(q, piece(last, 0)) * SCALE
        row_k = last * FAR_K + iota((FAR_Q, FAR_K), 1)
        row_q = pair * row_ids + ((b * FAR_Q + iota((FAR_Q, FAR_K), 0)) >> 5)
        s = jnp.where(row_k < row_q, s, LOW)
        s_scr[last] = s
        top = jnp.maximum(top, fold(s, jnp.maximum))
        m = jnp.max(top, axis=1, keepdims=True)

        def weigh(i, carried):
            total, acc = carried
            p = jnp.exp2(s_scr[i] - m)
            return (
                total + fold(p, jnp.add),
                acc + dot(p.astype(bf16), piece(i, 1)),
            )

        total, acc = lax.fori_loop(
            0,
            last + 1,
            weigh,
            (jnp.zeros((FAR_Q, 128), f32), jnp.zeros((FAR_Q, HD), f32)),
        )
        total = jnp.sum(total, axis=1, keepdims=True)
        out = (acc / total).astype(bf16)
        lse = jnp.where(m > 0.5 * LOW, m + jnp.log2(total), LOW)
        high = lse.astype(bf16).astype(f32)
        left = lse - high
        mid = left.astype(bf16).astype(f32)
        low = left - mid
        for e in range(per):
            at = slice(e * POS, (e + 1) * POS)
            terms = jnp.where(
                lane == 0,
                high[at],
                jnp.where(lane == 1, mid[at], jnp.where(lane == 2, low[at], 0.0)),
            ).astype(bf16)
            out_ref[b * per + e, :POS, :] = out[at]
            out_ref[b * per + e, POS:, :] = dot_t(eye, terms).astype(bf16)
        send(b).start()
        return unused

    lax.fori_loop(0, FAR_BLOCKS, block, 0)
    for b in range(FAR_BLOCKS):
        send(b).wait()


def final_kernel(
    far_ref, col_ref, row_hbm, part_hbm, stat_hbm, out_hbm,
    row_ref, part_ref, stat_ref, out_ref, sems,
):
    ins = [
        pltpu.make_async_copy(stat_hbm, stat_ref, sems.at[0]),
        pltpu.make_async_copy(part_hbm, part_ref, sems.at[1]),
        pltpu.make_async_copy(row_hbm, row_ref, sems.at[2]),
    ]
    for move in ins:
        move.start()
    back = one_hot(
        POS, POS, lambda o: (o & 3) * STRIDE + ((o >> 2) & 7) * 4 + (o >> 5)
    )
    row = iota((HEADS * SUM_ROWS, 128), 0)
    lane = iota((HEADS * SUM_ROWS, 128), 1)
    pick = jnp.where(
        jnp.logical_and((row >> 4) == lane, (row & 15) < 3), 1.0, 0.0
    ).astype(bf16)
    ins[0].wait()
    terms = jnp.concatenate([far_ref[g, POS:, :] for g in range(HEADS)], axis=0)
    lse = dot_tl(terms, pick)
    top = jnp.maximum(stat_ref[0], lse)
    own = jnp.exp2(stat_ref[0] - top)
    far = jnp.exp2(lse - top)
    scale = 1.0 / (stat_ref[1] * own + far)
    own = own * scale
    far = far * scale
    for move in ins[1:]:
        move.wait()
    moves = []
    for quad in range(QUADS):
        base = quad * 4 * HD
        out_ref[:, base : base + HD] = row_ref[quad]
        stack = jnp.concatenate(
            [col_ref[x, quad * STRIDE : (quad + 1) * STRIDE, :] for x in range(4)], axis=0
        )
        out_ref[:, base + HD : base + 2 * HD] = dot(back, stack).astype(bf16)
        for h in range(2):
            g = quad * 2 + h
            merged = (
                part_ref[g] * own[:, g : g + 1]
                + far_ref[g, :POS, :].astype(f32) * far[:, g : g + 1]
            )
            start = base + (2 + h) * HD
            out_ref[:, start : start + HD] = merged.astype(bf16)
        at = pl.ds(base, 4 * HD)
        move = pltpu.make_async_copy(out_ref.at[:, at], out_hbm.at[:, at], sems.at[3 + quad])
        move.start()
        moves.append(move)
    for move in moves:
        move.wait()


VMEM_BYTES = 63_000_000
SPACES = {"v": pltpu.VMEM, "s": pltpu.SMEM, "h": pl.ANY}


def call(kernel, outs, args, ins, to="v", scratch=(), flops=0, moved=0, exps=0, alias=None, room=0):
    def spec(space):
        return pl.BlockSpec(memory_space=SPACES[space])

    shapes = [jax.ShapeDtypeStruct(s, d) for s, d in outs]
    many = len(shapes) > 1
    return pl.pallas_call(
        kernel,
        out_shape=shapes if many else shapes[0],
        in_specs=[spec(space) for space in ins],
        out_specs=[spec(to)] * len(shapes) if many else spec(to),
        scratch_shapes=list(scratch),
        input_output_aliases=alias or {},
        compiler_params=pltpu.CompilerParams(vmem_limit_bytes=VMEM_BYTES - room),
        cost_estimate=pl.CostEstimate(flops=flops, bytes_accessed=moved, transcendentals=exps),
    )(*args)


def exchange(array, axes):
    return lax.all_to_all(array, axes, split_axis=0, concat_axis=0, tiled=True)


def dma(n):
    return pltpu.SemaphoreType.DMA((n,))


mib = 1 << 20


def pack_summary(keys, values):
    return call(
        pack_summary_kernel,
        [((64, 8, HD), bf16)],
        (keys, values),
        "hh",
        to="h",
        scratch=[
            pltpu.VMEM((128, QUADS * 4 * HD), bf16),
            pltpu.VMEM((HEADS, 8, HD), bf16),
            dma(12),
        ],
        flops=2 * 16 * 16 * 128 * 128,
        moved=mib,
    )


def pack(queries, keys, values):
    return call(
        pack_kernel,
        [((QUADS, 384, HD), bf16), ((HEADS, POS, HD), bf16)],
        (queries, keys, values),
        "hhh",
        to="h",
        scratch=[
            pltpu.VMEM((QUADS, POS, 3 * HD), bf16),
            pltpu.VMEM((QUADS, POS, HD), bf16),
            pltpu.VMEM((QUADS, POS, HD), bf16),
            pltpu.VMEM((QUADS, 384, HD), bf16),
            pltpu.VMEM((HEADS, POS, HD), bf16),
            dma(24),
            dma(16),
        ],
        flops=2 * 8 * 384 * 384 * 128,
        moved=4 * mib,
    )


def ordered(after, items):
    return call(
        order_kernel, [((QUADS, 384, HD), bf16)], (after, items), "hh", to="h", alias={1: 0}
    )


def rows(queries, keys, values):
    outs = [((QUADS, POS, HD), bf16), ((HEADS, POS, HD), f32), ((2, POS, 128), f32)]
    return call(
        rows_kernel,
        outs,
        (queries, keys, values),
        "hhh",
        to="h",
        scratch=[pltpu.VMEM((POS, QUADS * 4 * HD), bf16)] * 3
        + [pltpu.VMEM(*out) for out in outs]
        + [dma(13)],
        room=1_250_000,
        flops=24 * 4 * 128 * 128 * 128,
        moved=5 * mib,
        exps=24 * 128 * 128,
    )


def columns(core, items, other):
    return call(
        column_kernel,
        [((4, 256, HD), bf16)],
        (core, items, other),
        "svv",
        to="h",
        scratch=[
            pltpu.VMEM((4, 256, HD), bf16),
            pltpu.VMEM((1024, HD), bf16),
            pltpu.VMEM((2, 1024, HD), bf16),
            pltpu.VMEM((2, 1024, HD), bf16),
            dma(4),
        ],
        room=2_600_000,
        flops=4 * 1024 * 1280 * 128,
        moved=2 * mib,
        exps=1024 * 1280,
    )


def far_part(pair, heads, summary):
    return call(
        far_kernel,
        [((HEADS, PAY, HD), bf16)],
        (pair, heads, summary),
        "shh",
        to="h",
        scratch=[
            pltpu.VMEM((HEADS, POS, HD), bf16),
            pltpu.VMEM((8, 2, 256, HD), bf16),
            pltpu.VMEM((HEADS, PAY, HD), bf16),
            pltpu.VMEM((2048 // FAR_K, FAR_Q, FAR_K), f32),
            dma(2 + FAR_BLOCKS),
        ],
        flops=8 * 1024 * 2048 * 128,
        moved=3 * mib,
        exps=2 * 1024 * 2048,
    )


def final(far, column, row_out, part, stat):
    return call(
        final_kernel,
        [((POS, QUADS * 4 * HD), bf16)],
        (far, column, row_out, part, stat),
        "vvhhh",
        to="h",
        scratch=[
            pltpu.VMEM((QUADS, POS, HD), bf16),
            pltpu.VMEM((HEADS, POS, HD), f32),
            pltpu.VMEM((2, POS, 128), f32),
            pltpu.VMEM((POS, QUADS * 4 * HD), bf16),
            dma(11),
        ],
        room=500_000,
        flops=2 * 8 * 128 * 128 * 128,
        moved=4 * mib,
    )


def body(queries, keys, values):
    heads_at = ("w", "c", "x")
    plane = ("u", "v", "w", "c", "x")
    wide = ("z", "u", "v", "w", "x")
    back = ("x", "z", "u", "v", "w")
    summary = exchange(pack_summary(keys, values), plane)
    summary = summary.reshape(64, 2, ROWS, HD).transpose(1, 0, 2, 3).reshape(1, 2, 256, HD)
    items, heads = pack(queries, keys, values)
    items = ordered(summary, items)
    summary = lax.all_gather(summary, "z", axis=0, tiled=True)
    items = exchange(items.reshape(768, ROWS, HD), wide).reshape(3072, HD)
    heads = exchange(heads, heads_at)
    other = lax.ppermute(items, "c", [(0, 1), (1, 0)])
    core = lax.axis_index("c").astype(jnp.int32).reshape(1)
    column = columns(core, items, other)
    column = exchange(column.reshape(256, ROWS, HD), back).reshape(4, 256, HD)
    pair = lax.axis_index(("z", "u", "v")).astype(jnp.int32).reshape(1)
    far = exchange(far_part(pair, heads, summary), heads_at)
    row_out, part, stat = rows(queries, keys, values)
    return final(far, column, row_out, part, stat)


def solution(mesh):
    fine = Mesh(mesh.devices.reshape(4, 8, 2, 2, 2, 2), ("x", "z", "u", "v", "w", "c"))
    spec = P(("z", "u", "v", "w", "c", "x"), None)
    return jax.shard_map(
        body, mesh=fine, in_specs=(spec, spec, spec), out_specs=spec, check_vma=False
    )
```

```python
import math

import jax
import jax.numpy as jnp
from jax import lax
from jax.experimental import pallas as pl
from jax.experimental.pallas import tpu as pltpu
from jax.sharding import Mesh
from jax.sharding import PartitionSpec as P

HD = 128
STRIDE = 32
QUADS = 8
POS = 128
ROWS = 4
LOW = -1e30
SCALE = math.log2(math.e) / math.sqrt(HD)
SUM_ROWS = 16
PAY = POS + SUM_ROWS
HEADS = 16
PAIR = HEADS * POS

f32 = jnp.float32
bf16 = jnp.bfloat16


def dot_t(a, b):
    return lax.dot_general(a, b, (((1,), (1,)), ((), ())), preferred_element_type=f32)


def dot_tl(a, b):
    return lax.dot_general(a, b, (((0,), (0,)), ((), ())), preferred_element_type=f32)


def dot(a, b):
    return lax.dot_general(a, b, (((1,), (0,)), ((), ())), preferred_element_type=f32)


def iota(shape, dim):
    return lax.broadcasted_iota(jnp.int32, shape, dim)


def one_hot(rows, cols, source):
    row = iota((rows, cols), 0)
    col = iota((rows, cols), 1)
    return jnp.where(source(row) == col, 1.0, 0.0).astype(bf16)


def div12(o):
    return (o * 5462) >> 16


def head(ref, quad, kind):
    start = (quad * 4 + kind) * HD
    return ref[:, start : start + HD]


def pack_summary_kernel(k_ref, v_ref, sum_hbm, buf, sum_ref, sems):
    moves = []
    for a, ref in enumerate((k_ref, v_ref)):
        for r in range(ROWS):
            move = pltpu.make_async_copy(
                ref.at[pl.ds(r * STRIDE + 16, 16), :],
                buf.at[pl.ds((a * ROWS + r) * 16, 16), :],
                sems.at[a * ROWS + r],
            )
            move.start()
            moves.append(move)
    pick = one_hot(8, 128, lambda o: o * 16 + 15)
    for move in moves:
        move.wait()
    for g in range(HEADS):
        rows = dot(pick, head(buf, g // 2, 2 + g % 2)).astype(bf16)
        sum_ref[g] = rows
    moves = []
    for t in range(sum_hbm.shape[0] // HEADS):
        move = pltpu.make_async_copy(
            sum_ref, sum_hbm.at[pl.ds(t * HEADS, HEADS)], sems.at[2 * ROWS + t]
        )
        move.start()
        moves.append(move)
    for move in moves:
        move.wait()


def pack_kernel(q_hbm, k_hbm, v_hbm, item_hbm, query_hbm, qs, ks, vs, items, heads, ins, outs):
    def source(o):
        col = div12(o)
        rest = o - 12 * col
        return (rest >> 2) * POS + (rest & 3) * STRIDE + col

    def fetch(quad):
        at = quad * 4 * HD
        return [
            pltpu.make_async_copy(
                q_hbm.at[:, pl.ds(at + HD, 3 * HD)], qs.at[quad], ins.at[quad * 3]
            ),
            pltpu.make_async_copy(
                k_hbm.at[:, pl.ds(at + HD, HD)], ks.at[quad], ins.at[quad * 3 + 1]
            ),
            pltpu.make_async_copy(
                v_hbm.at[:, pl.ds(at + HD, HD)], vs.at[quad], ins.at[quad * 3 + 2]
            ),
        ]

    for quad in range(QUADS):
        for move in fetch(quad):
            move.start()
    perm = one_hot(384, 384, source)
    moves = []
    for quad in range(QUADS):
        for move in fetch(quad):
            move.wait()
        stack = jnp.concatenate([qs[quad, :, :HD], ks[quad], vs[quad]], axis=0)
        items[quad] = dot(perm, stack).astype(bf16)
        heads[quad * 2] = qs[quad, :, HD : 2 * HD]
        heads[quad * 2 + 1] = qs[quad, :, 2 * HD :]
        two = pl.ds(quad * 2, 2)
        for move in (
            pltpu.make_async_copy(items.at[quad], item_hbm.at[quad], outs.at[quad * 2]),
            pltpu.make_async_copy(heads.at[two], query_hbm.at[two], outs.at[quad * 2 + 1]),
        ):
            move.start()
            moves.append(move)
    for move in moves:
        move.wait()


def order_kernel(after_ref, array_ref, out_ref):
    pass


def rows_kernel(
    q_hbm, k_hbm, v_hbm, row_hbm, part_hbm, stat_hbm,
    q_ref, k_ref, v_ref, row_ref, part_ref, stat_ref, sems,
):
    ins = []
    for a, (hbm, ref) in enumerate(((q_hbm, q_ref), (k_hbm, k_ref), (v_hbm, v_ref))):
        move = pltpu.make_async_copy(hbm, ref, sems.at[a])
        move.start()
        ins.append(move)
    pos = iota((POS, POS), 0)
    key = iota((POS, POS), 1)
    visible = jnp.logical_and((key >> 5) == (pos >> 5), key <= pos)
    tops = jnp.zeros((POS, POS), f32)
    sums = jnp.ones((POS, POS), f32)
    for move in ins:
        move.wait()
    moves = []
    for quad in range(QUADS):
        for kind in (0, 2, 3):
            s = dot_t(head(q_ref, quad, kind), head(k_ref, quad, kind)) * SCALE
            s = jnp.where(visible, s, LOW)
            m = jnp.max(s, axis=1, keepdims=True)
            p = jnp.where(visible, jnp.exp2(s - m), 0.0)
            total = jnp.sum(p, axis=1, keepdims=True)
            acc = dot(p.astype(bf16), head(v_ref, quad, kind))
            if kind == 0:
                row_ref[quad] = (acc / total).astype(bf16)
            else:
                slot = quad * 2 + kind - 2
                part_ref[slot] = acc
                tops = jnp.where(key == slot, m, tops)
                sums = jnp.where(key == slot, total, sums)
        two = pl.ds(quad * 2, 2)
        moves.append(pltpu.make_async_copy(part_ref.at[two], part_hbm.at[two], sems.at[3 + quad]))
        moves[-1].start()
    stat_ref[0] = tops
    stat_ref[1] = sums
    moves.append(pltpu.make_async_copy(row_ref, row_hbm, sems.at[11]))
    moves.append(pltpu.make_async_copy(stat_ref, stat_hbm, sems.at[12]))
    moves[-1].start()
    moves[-2].start()
    for move in moves:
        move.wait()


def column_kernel(
    core_ref, own_ref, other_ref, out_hbm, out_scr, q_scr, k_scr, v_scr, sems
):
    core = core_ref[0]

    def source(o):
        within = o & 31
        return (within >> 2) * 12 + (o >> 5) * 4 + (within & 3)

    split = one_hot(96, 96, source)
    split_kv = one_hot(64, 96, lambda o: source(o + 32))
    by_x = one_hot(POS, POS, lambda o: ((o >> 2) & 7) * 16 + (o >> 5) * 4 + (o & 3))
    for g in range(32):
        at = slice(g * 32, (g + 1) * 32)
        y = dot(split, own_ref[g * 96 : (g + 1) * 96, :]).astype(bf16)
        q_scr[at, :] = y[0:32]
        k_scr[0, at, :] = y[32:64]
        v_scr[0, at, :] = y[64:96]
        y = dot(split_kv, other_ref[g * 96 : (g + 1) * 96, :]).astype(bf16)
        k_scr[1, at, :] = y[0:32]
        v_scr[1, at, :] = y[32:64]

    block = 256
    jq = iota((block, block), 0)
    jk = iota((block, block), 1)
    visible = (jk <= jq, (jk >> 4) < (jq >> 4) + core)
    moves = []
    for qb in range(1024 // block):
        q = q_scr[qb * block : (qb + 1) * block, :]
        pieces = []
        top = None
        for kb in range(qb + 1):
            for c in range(2):
                s = dot_t(q, k_scr[c, kb * block : (kb + 1) * block, :]) * SCALE
                if kb == qb:
                    s = jnp.where(visible[c], s, LOW)
                fold = jnp.maximum(s[:, :128], s[:, 128:])
                top = fold if top is None else jnp.maximum(top, fold)
                pieces.append((kb, c, s))
        m = jnp.max(top, axis=1, keepdims=True)
        total = jnp.zeros((block, 128), f32)
        acc = jnp.zeros((block, HD), f32)
        for kb, c, s in pieces:
            p = jnp.exp2(s - m)
            total = total + (p[:, :128] + p[:, 128:])
            acc = acc + dot(p.astype(bf16), v_scr[c, kb * block : (kb + 1) * block, :])
        total = jnp.sum(total, axis=1, keepdims=True)
        out = (acc / total).astype(bf16)
        for t in range(block // POS):
            y = dot(by_x, out[t * POS : (t + 1) * POS]).astype(bf16)
            at = (qb * block // POS + t) * STRIDE
            for x in range(4):
                out_scr[x, at : at + STRIDE, :] = y[x * STRIDE : (x + 1) * STRIDE]
        at = pl.ds(qb * block // 4, block // 4)
        move = pltpu.make_async_copy(out_scr.at[:, at, :], out_hbm.at[:, at, :], sems.at[qb])
        move.start()
        moves.append(move)
    for move in moves:
        move.wait()


FAR_Q = 1024
FAR_K = 2048
FAR_BLOCKS = PAIR // FAR_Q


def far_kernel(pair_ref, q_hbm, kv_hbm, out_hbm, q_ref, kv_ref, out_ref, s_scr, sems):
    pair = pair_ref[0]
    ins = [
        pltpu.make_async_copy(q_hbm, q_ref, sems.at[0]),
        pltpu.make_async_copy(kv_hbm, kv_ref, sems.at[1]),
    ]
    for move in ins:
        move.start()
    row_ids = PAIR // STRIDE
    last = (pair * row_ids) // FAR_K
    lane = iota((POS, 128), 1)
    eye = one_hot(SUM_ROWS, 128, lambda o: o)
    per = FAR_Q // POS
    planes = FAR_K // 256

    for move in ins:
        move.wait()

    def send(b):
        at = pl.ds(b * per, per)
        return pltpu.make_async_copy(out_ref.at[at], out_hbm.at[at], sems.at[2 + b])

    def piece(i, j):
        return jnp.concatenate([kv_ref[i * planes + t, j] for t in range(planes)], axis=0)

    def fold(x, op):
        r = x[:, :128]
        for t in range(1, FAR_K // 128):
            r = op(r, x[:, t * 128 : (t + 1) * 128])
        return r

    def block(b, unused):
        q = q_ref[pl.ds(b * per, per)].reshape(FAR_Q, HD)

        def score(i, top):
            s = dot_t(q, piece(i, 0)) * SCALE
            s_scr[i] = s
            return jnp.maximum(top, fold(s, jnp.maximum))

        top = lax.fori_loop(0, last, score, jnp.full((FAR_Q, 128), LOW, f32))
        s = dot_t(q, piece(last, 0)) * SCALE
        row_k = last * FAR_K + iota((FAR_Q, FAR_K), 1)
        row_q = pair * row_ids + ((b * FAR_Q + iota((FAR_Q, FAR_K), 0)) >> 5)
        s = jnp.where(row_k < row_q, s, LOW)
        s_scr[last] = s
        top = jnp.maximum(top, fold(s, jnp.maximum))
        m = jnp.max(top, axis=1, keepdims=True)

        def weigh(i, carried):
            total, acc = carried
            p = jnp.exp2(s_scr[i] - m)
            return (
                total + fold(p, jnp.add),
                acc + dot(p.astype(bf16), piece(i, 1)),
            )

        total, acc = lax.fori_loop(
            0,
            last + 1,
            weigh,
            (jnp.zeros((FAR_Q, 128), f32), jnp.zeros((FAR_Q, HD), f32)),
        )
        total = jnp.sum(total, axis=1, keepdims=True)
        out = (acc / total).astype(bf16)
        lse = jnp.where(m > 0.5 * LOW, m + jnp.log2(total), LOW)
        high = lse.astype(bf16).astype(f32)
        left = lse - high
        mid = left.astype(bf16).astype(f32)
        low = left - mid
        for e in range(per):
            at = slice(e * POS, (e + 1) * POS)
            terms = jnp.where(
                lane == 0,
                high[at],
                jnp.where(lane == 1, mid[at], jnp.where(lane == 2, low[at], 0.0)),
            ).astype(bf16)
            out_ref[b * per + e, :POS, :] = out[at]
            out_ref[b * per + e, POS:, :] = dot_t(eye, terms).astype(bf16)
        send(b).start()
        return unused

    lax.fori_loop(0, FAR_BLOCKS, block, 0)
    for b in range(FAR_BLOCKS):
        send(b).wait()


def place_kernel(col_hbm, row_hbm, out_hbm, col_ref, row_ref, out_ref, sems):
    ins = [
        pltpu.make_async_copy(col_hbm, col_ref, sems.at[0]),
        pltpu.make_async_copy(row_hbm, row_ref, sems.at[1]),
    ]
    for move in ins:
        move.start()
    back = one_hot(
        POS, POS, lambda o: (o & 3) * STRIDE + ((o >> 2) & 7) * 4 + (o >> 5)
    )
    for move in ins:
        move.wait()
    moves = []
    for quad in range(QUADS):
        out_ref[quad, :, :HD] = row_ref[quad]
        stack = jnp.concatenate(
            [col_ref[x, quad * STRIDE : (quad + 1) * STRIDE, :] for x in range(4)], axis=0
        )
        out_ref[quad, :, HD:] = dot(back, stack).astype(bf16)
        move = pltpu.make_async_copy(
            out_ref.at[quad], out_hbm.at[:, pl.ds(quad * 4 * HD, 2 * HD)], sems.at[2 + quad]
        )
        move.start()
        moves.append(move)
    for move in moves:
        move.wait()


def merge_kernel(
    placed_hbm, far_hbm, part_hbm, stat_hbm, out_hbm, far_ref, part_ref, stat_ref, out_ref, sems
):
    ins = [
        pltpu.make_async_copy(far_hbm, far_ref, sems.at[0]),
        pltpu.make_async_copy(stat_hbm, stat_ref, sems.at[1]),
    ]
    for g in range(0, HEADS, 4):
        some = pl.ds(g, 4)
        ins.append(
            pltpu.make_async_copy(part_hbm.at[some], part_ref.at[some], sems.at[2 + g // 4])
        )
    for move in ins:
        move.start()
    row = iota((HEADS * SUM_ROWS, 128), 0)
    lane = iota((HEADS * SUM_ROWS, 128), 1)
    pick = jnp.where(
        jnp.logical_and((row >> 4) == lane, (row & 15) < 3), 1.0, 0.0
    ).astype(bf16)
    ins[0].wait()
    ins[1].wait()
    terms = jnp.concatenate([far_ref[g, POS:, :] for g in range(HEADS)], axis=0)
    lse = dot_tl(terms, pick)
    top = jnp.maximum(stat_ref[0], lse)
    own = jnp.exp2(stat_ref[0] - top)
    far = jnp.exp2(lse - top)
    scale = 1.0 / (stat_ref[1] * own + far)
    own = own * scale
    far = far * scale
    moves = []
    for g in range(HEADS):
        if g % 4 == 0:
            ins[2 + g // 4].wait()
        merged = (
            part_ref[g] * own[:, g : g + 1]
            + far_ref[g, :POS, :].astype(f32) * far[:, g : g + 1]
        )
        quad, h = g // 2, g % 2
        out_ref[quad, :, h * HD : (h + 1) * HD] = merged.astype(bf16)
        if h == 1:
            move = pltpu.make_async_copy(
                out_ref.at[quad],
                out_hbm.at[:, pl.ds((quad * 4 + 2) * HD, 2 * HD)],
                sems.at[6 + quad],
            )
            move.start()
            moves.append(move)
    for move in moves:
        move.wait()


VMEM_BYTES = 63_000_000
SPACES = {"v": pltpu.VMEM, "s": pltpu.SMEM, "h": pl.ANY}


def call(kernel, outs, args, ins, to="v", scratch=(), flops=0, moved=0, exps=0, alias=None, room=0):
    def spec(space):
        return pl.BlockSpec(memory_space=SPACES[space])

    shapes = [jax.ShapeDtypeStruct(s, d) for s, d in outs]
    many = len(shapes) > 1
    return pl.pallas_call(
        kernel,
        out_shape=shapes if many else shapes[0],
        in_specs=[spec(space) for space in ins],
        out_specs=[spec(to)] * len(shapes) if many else spec(to),
        scratch_shapes=list(scratch),
        input_output_aliases=alias or {},
        compiler_params=pltpu.CompilerParams(vmem_limit_bytes=VMEM_BYTES - room),
        cost_estimate=pl.CostEstimate(flops=flops, bytes_accessed=moved, transcendentals=exps),
    )(*args)


def exchange(array, axes):
    return lax.all_to_all(array, axes, split_axis=0, concat_axis=0, tiled=True)


def dma(n):
    return pltpu.SemaphoreType.DMA((n,))


mib = 1 << 20


def pack_summary(keys, values):
    return call(
        pack_summary_kernel,
        [((64, 8, HD), bf16)],
        (keys, values),
        "hh",
        to="h",
        scratch=[
            pltpu.VMEM((128, QUADS * 4 * HD), bf16),
            pltpu.VMEM((HEADS, 8, HD), bf16),
            dma(12),
        ],
        flops=2 * 16 * 16 * 128 * 128,
        moved=mib,
    )


def pack(queries, keys, values):
    return call(
        pack_kernel,
        [((QUADS, 384, HD), bf16), ((HEADS, POS, HD), bf16)],
        (queries, keys, values),
        "hhh",
        to="h",
        scratch=[
            pltpu.VMEM((QUADS, POS, 3 * HD), bf16),
            pltpu.VMEM((QUADS, POS, HD), bf16),
            pltpu.VMEM((QUADS, POS, HD), bf16),
            pltpu.VMEM((QUADS, 384, HD), bf16),
            pltpu.VMEM((HEADS, POS, HD), bf16),
            dma(24),
            dma(16),
        ],
        flops=2 * 8 * 384 * 384 * 128,
        moved=4 * mib,
    )


def ordered(after, array):
    return call(
        order_kernel,
        [(array.shape, array.dtype)],
        (after, array),
        "hh",
        to="h",
        alias={1: 0},
        room=46_000_000,
    )


def rows(queries, keys, values):
    outs = [((QUADS, POS, HD), bf16), ((HEADS, POS, HD), f32), ((2, POS, 128), f32)]
    return call(
        rows_kernel,
        outs,
        (queries, keys, values),
        "hhh",
        to="h",
        scratch=[pltpu.VMEM((POS, QUADS * 4 * HD), bf16)] * 3
        + [pltpu.VMEM(*out) for out in outs]
        + [dma(13)],
        flops=24 * 4 * 128 * 128 * 128,
        moved=5 * mib,
        exps=24 * 128 * 128,
    )


def columns(core, items, other):
    return call(
        column_kernel,
        [((4, 256, HD), bf16)],
        (core, items, other),
        "svv",
        to="h",
        scratch=[
            pltpu.VMEM((4, 256, HD), bf16),
            pltpu.VMEM((1024, HD), bf16),
            pltpu.VMEM((2, 1024, HD), bf16),
            pltpu.VMEM((2, 1024, HD), bf16),
            dma(4),
        ],
        room=46_000_000,
        flops=4 * 1024 * 1280 * 128,
        moved=2 * mib,
        exps=1024 * 1280,
    )


def far_part(pair, heads, summary):
    return call(
        far_kernel,
        [((HEADS, PAY, HD), bf16)],
        (pair, heads, summary),
        "shh",
        to="h",
        scratch=[
            pltpu.VMEM((HEADS, POS, HD), bf16),
            pltpu.VMEM((8, 2, 256, HD), bf16),
            pltpu.VMEM((HEADS, PAY, HD), bf16),
            pltpu.VMEM((2048 // FAR_K, FAR_Q, FAR_K), f32),
            dma(2 + FAR_BLOCKS),
        ],
        flops=8 * 1024 * 2048 * 128,
        moved=3 * mib,
        exps=2 * 1024 * 2048,
    )


def place(column, row_out):
    return call(
        place_kernel,
        [((POS, QUADS * 4 * HD), bf16)],
        (column, row_out),
        "hh",
        to="h",
        scratch=[
            pltpu.VMEM((4, 256, HD), bf16),
            pltpu.VMEM((QUADS, POS, HD), bf16),
            pltpu.VMEM((QUADS, POS, 2 * HD), bf16),
            dma(10),
        ],
        flops=2 * 8 * 128 * 128 * 128,
        moved=mib,
    )


def merge(placed, far, part, stat):
    return call(
        merge_kernel,
        [((POS, QUADS * 4 * HD), bf16)],
        (placed, far, part, stat),
        "hhhh",
        to="h",
        scratch=[
            pltpu.VMEM((HEADS, PAY, HD), bf16),
            pltpu.VMEM((HEADS, POS, HD), f32),
            pltpu.VMEM((2, POS, 128), f32),
            pltpu.VMEM((QUADS, POS, 2 * HD), bf16),
            dma(14),
        ],
        alias={0: 0},
        flops=2 * 8 * 128 * 128 * 128,
        moved=3 * mib,
    )


def body(queries, keys, values):
    heads_at = ("w", "c", "x")
    plane = ("u", "v", "w", "c", "x")
    wide = ("z", "u", "v", "w", "x")
    back = ("x", "z", "u", "v", "w")
    summary = exchange(pack_summary(keys, values), plane)
    summary = summary.reshape(64, 2, ROWS, HD).transpose(1, 0, 2, 3).reshape(1, 2, 256, HD)
    items, heads = pack(queries, keys, values)
    items = ordered(summary, items)
    summary = lax.all_gather(summary, "z", axis=0, tiled=True)
    items = exchange(items.reshape(768, ROWS, HD), wide).reshape(3072, HD)
    row_out, part, stat = rows(queries, keys, values)
    items = ordered(stat, items)
    heads = exchange(ordered(stat, heads), heads_at)
    other = lax.ppermute(items, "c", [(0, 1), (1, 0)])
    core = lax.axis_index("c").astype(jnp.int32).reshape(1)
    column = columns(core, items, other)
    column = exchange(column.reshape(256, ROWS, HD), back).reshape(4, 256, HD)
    pair = lax.axis_index(("z", "u", "v")).astype(jnp.int32).reshape(1)
    far = exchange(far_part(pair, heads, summary), heads_at)
    return merge(place(column, row_out), far, part, stat)


def solution(mesh):
    fine = Mesh(mesh.devices.reshape(4, 8, 2, 2, 2, 2), ("x", "z", "u", "v", "w", "c"))
    spec = P(("z", "u", "v", "w", "c", "x"), None)
    return jax.shard_map(
        body, mesh=fine, in_specs=(spec, spec, spec), out_specs=spec, check_vma=False
    )
```

```python
import math

import jax
import jax.numpy as jnp
from jax import lax
from jax.experimental import pallas as pl
from jax.experimental.pallas import tpu as pltpu
from jax.sharding import Mesh
from jax.sharding import PartitionSpec as P

HD = 128
STRIDE = 32
QUADS = 8
POS = 128
ROWS = 4
LOW = -1e30
SCALE = math.log2(math.e) / math.sqrt(HD)
SUM_ROWS = 16
PAY = POS + SUM_ROWS
HEADS = 16
PAIR = HEADS * POS

f32 = jnp.float32
bf16 = jnp.bfloat16


def dot_t(a, b):
    return lax.dot_general(a, b, (((1,), (1,)), ((), ())), preferred_element_type=f32)


def dot_tl(a, b):
    return lax.dot_general(a, b, (((0,), (0,)), ((), ())), preferred_element_type=f32)


def dot(a, b):
    return lax.dot_general(a, b, (((1,), (0,)), ((), ())), preferred_element_type=f32)


def iota(shape, dim):
    return lax.broadcasted_iota(jnp.int32, shape, dim)


def one_hot(rows, cols, source):
    row = iota((rows, cols), 0)
    col = iota((rows, cols), 1)
    return jnp.where(source(row) == col, 1.0, 0.0).astype(bf16)


def div12(o):
    return (o * 5462) >> 16


def head(ref, quad, kind):
    start = (quad * 4 + kind) * HD
    return ref[:, start : start + HD]


def pack_summary_kernel(k_ref, v_ref, sum_hbm, buf, sum_ref, sems):
    moves = []
    for a, ref in enumerate((k_ref, v_ref)):
        for r in range(ROWS):
            move = pltpu.make_async_copy(
                ref.at[pl.ds(r * STRIDE + 16, 16), :],
                buf.at[pl.ds((a * ROWS + r) * 16, 16), :],
                sems.at[a * ROWS + r],
            )
            move.start()
            moves.append(move)
    pick = one_hot(8, 128, lambda o: o * 16 + 15)
    for move in moves:
        move.wait()
    for g in range(HEADS):
        rows = dot(pick, head(buf, g // 2, 2 + g % 2)).astype(bf16)
        sum_ref[g] = rows
    moves = []
    for t in range(sum_hbm.shape[0] // HEADS):
        move = pltpu.make_async_copy(
            sum_ref, sum_hbm.at[pl.ds(t * HEADS, HEADS)], sems.at[2 * ROWS + t]
        )
        move.start()
        moves.append(move)
    for move in moves:
        move.wait()


def pack_kernel(q_hbm, k_hbm, v_hbm, item_hbm, query_hbm, qs, ks, vs, items, heads, ins, outs):
    def source(o):
        col = div12(o)
        rest = o - 12 * col
        return (rest >> 2) * POS + (rest & 3) * STRIDE + col

    def fetch(quad):
        at = quad * 4 * HD
        return [
            pltpu.make_async_copy(
                q_hbm.at[:, pl.ds(at + HD, 3 * HD)], qs.at[quad], ins.at[quad * 3]
            ),
            pltpu.make_async_copy(
                k_hbm.at[:, pl.ds(at + HD, HD)], ks.at[quad], ins.at[quad * 3 + 1]
            ),
            pltpu.make_async_copy(
                v_hbm.at[:, pl.ds(at + HD, HD)], vs.at[quad], ins.at[quad * 3 + 2]
            ),
        ]

    for quad in range(QUADS):
        for move in fetch(quad):
            move.start()
    perm = one_hot(384, 384, source)
    moves = []
    for quad in range(QUADS):
        for move in fetch(quad):
            move.wait()
        stack = jnp.concatenate([qs[quad, :, :HD], ks[quad], vs[quad]], axis=0)
        items[quad] = dot(perm, stack).astype(bf16)
        heads[quad * 2] = qs[quad, :, HD : 2 * HD]
        heads[quad * 2 + 1] = qs[quad, :, 2 * HD :]
        two = pl.ds(quad * 2, 2)
        for move in (
            pltpu.make_async_copy(items.at[quad], item_hbm.at[quad], outs.at[quad * 2]),
            pltpu.make_async_copy(heads.at[two], query_hbm.at[two], outs.at[quad * 2 + 1]),
        ):
            move.start()
            moves.append(move)
    for move in moves:
        move.wait()


def order_kernel(after_ref, array_ref, out_ref):
    pass


def rows_kernel(
    q_hbm, k_hbm, v_hbm, row_hbm, part_hbm, stat_hbm,
    q_ref, k_ref, v_ref, row_ref, part_ref, stat_ref, sems,
):
    ins = []
    for a, (hbm, ref) in enumerate(((q_hbm, q_ref), (k_hbm, k_ref), (v_hbm, v_ref))):
        move = pltpu.make_async_copy(hbm, ref, sems.at[a])
        move.start()
        ins.append(move)
    pos = iota((POS, POS), 0)
    key = iota((POS, POS), 1)
    visible = jnp.logical_and((key >> 5) == (pos >> 5), key <= pos)
    tops = jnp.zeros((POS, POS), f32)
    sums = jnp.ones((POS, POS), f32)
    for move in ins:
        move.wait()
    moves = []
    for quad in range(QUADS):
        for kind in (0, 2, 3):
            s = dot_t(head(q_ref, quad, kind), head(k_ref, quad, kind)) * SCALE
            s = jnp.where(visible, s, LOW)
            m = jnp.max(s, axis=1, keepdims=True)
            p = jnp.where(visible, jnp.exp2(s - m), 0.0)
            total = jnp.sum(p, axis=1, keepdims=True)
            acc = dot(p.astype(bf16), head(v_ref, quad, kind))
            if kind == 0:
                row_ref[quad] = (acc / total).astype(bf16)
            else:
                slot = quad * 2 + kind - 2
                part_ref[slot] = acc
                tops = jnp.where(key == slot, m, tops)
                sums = jnp.where(key == slot, total, sums)
        two = pl.ds(quad * 2, 2)
        moves.append(pltpu.make_async_copy(part_ref.at[two], part_hbm.at[two], sems.at[3 + quad]))
        moves[-1].start()
    stat_ref[0] = tops
    stat_ref[1] = sums
    moves.append(pltpu.make_async_copy(row_ref, row_hbm, sems.at[11]))
    moves.append(pltpu.make_async_copy(stat_ref, stat_hbm, sems.at[12]))
    moves[-1].start()
    moves[-2].start()
    for move in moves:
        move.wait()


def column_kernel(
    core_ref, own_ref, other_ref, out_hbm, out_scr, q_scr, k_scr, v_scr, sems
):
    core = core_ref[0]

    def source(o):
        within = o & 31
        return (within >> 2) * 12 + (o >> 5) * 4 + (within & 3)

    split = one_hot(96, 96, source)
    split_kv = one_hot(64, 96, lambda o: source(o + 32))
    by_x = one_hot(POS, POS, lambda o: ((o >> 2) & 7) * 16 + (o >> 5) * 4 + (o & 3))
    for g in range(32):
        at = slice(g * 32, (g + 1) * 32)
        y = dot(split, own_ref[g * 96 : (g + 1) * 96, :]).astype(bf16)
        q_scr[at, :] = y[0:32]
        k_scr[0, at, :] = y[32:64]
        v_scr[0, at, :] = y[64:96]
        y = dot(split_kv, other_ref[g * 96 : (g + 1) * 96, :]).astype(bf16)
        k_scr[1, at, :] = y[0:32]
        v_scr[1, at, :] = y[32:64]

    block = 256
    jq = iota((block, block), 0)
    jk = iota((block, block), 1)
    visible = (jk <= jq, (jk >> 4) < (jq >> 4) + core)
    moves = []
    for qb in range(1024 // block):
        q = q_scr[qb * block : (qb + 1) * block, :]
        pieces = []
        top = None
        for kb in range(qb + 1):
            for c in range(2):
                s = dot_t(q, k_scr[c, kb * block : (kb + 1) * block, :]) * SCALE
                if kb == qb:
                    s = jnp.where(visible[c], s, LOW)
                fold = jnp.maximum(s[:, :128], s[:, 128:])
                top = fold if top is None else jnp.maximum(top, fold)
                pieces.append((kb, c, s))
        m = jnp.max(top, axis=1, keepdims=True)
        total = jnp.zeros((block, 128), f32)
        acc = jnp.zeros((block, HD), f32)
        for kb, c, s in pieces:
            p = jnp.exp2(s - m)
            total = total + (p[:, :128] + p[:, 128:])
            acc = acc + dot(p.astype(bf16), v_scr[c, kb * block : (kb + 1) * block, :])
        total = jnp.sum(total, axis=1, keepdims=True)
        out = (acc / total).astype(bf16)
        for t in range(block // POS):
            y = dot(by_x, out[t * POS : (t + 1) * POS]).astype(bf16)
            at = (qb * block // POS + t) * STRIDE
            for x in range(4):
                out_scr[x, at : at + STRIDE, :] = y[x * STRIDE : (x + 1) * STRIDE]
        at = pl.ds(qb * block // 4, block // 4)
        move = pltpu.make_async_copy(out_scr.at[:, at, :], out_hbm.at[:, at, :], sems.at[qb])
        move.start()
        moves.append(move)
    for move in moves:
        move.wait()


FAR_Q = 1024
FAR_K = 2048
FAR_BLOCKS = PAIR // FAR_Q


def far_kernel(pair_ref, q_hbm, kv_hbm, out_hbm, q_ref, kv_ref, out_ref, s_scr, sems):
    pair = pair_ref[0]
    ins = [
        pltpu.make_async_copy(q_hbm, q_ref, sems.at[0]),
        pltpu.make_async_copy(kv_hbm, kv_ref, sems.at[1]),
    ]
    for move in ins:
        move.start()
    row_ids = PAIR // STRIDE
    last = (pair * row_ids) // FAR_K
    lane = iota((POS, 128), 1)
    eye = one_hot(SUM_ROWS, 128, lambda o: o)
    per = FAR_Q // POS
    planes = FAR_K // 256

    for move in ins:
        move.wait()

    def send(b):
        at = pl.ds(b * per, per)
        return pltpu.make_async_copy(out_ref.at[at], out_hbm.at[at], sems.at[2 + b])

    def piece(i, j):
        return jnp.concatenate([kv_ref[i * planes + t, j] for t in range(planes)], axis=0)

    def fold(x, op):
        r = x[:, :128]
        for t in range(1, FAR_K // 128):
            r = op(r, x[:, t * 128 : (t + 1) * 128])
        return r

    def block(b, unused):
        q = q_ref[pl.ds(b * per, per)].reshape(FAR_Q, HD)

        def score(i, top):
            s = dot_t(q, piece(i, 0)) * SCALE
            s_scr[i] = s
            return jnp.maximum(top, fold(s, jnp.maximum))

        top = lax.fori_loop(0, last, score, jnp.full((FAR_Q, 128), LOW, f32))
        s = dot_t(q, piece(last, 0)) * SCALE
        row_k = last * FAR_K + iota((FAR_Q, FAR_K), 1)
        row_q = pair * row_ids + ((b * FAR_Q + iota((FAR_Q, FAR_K), 0)) >> 5)
        s = jnp.where(row_k < row_q, s, LOW)
        s_scr[last] = s
        top = jnp.maximum(top, fold(s, jnp.maximum))
        m = jnp.max(top, axis=1, keepdims=True)

        def weigh(i, carried):
            total, acc = carried
            p = jnp.exp2(s_scr[i] - m)
            return (
                total + fold(p, jnp.add),
                acc + dot(p.astype(bf16), piece(i, 1)),
            )

        total, acc = lax.fori_loop(
            0,
            last + 1,
            weigh,
            (jnp.zeros((FAR_Q, 128), f32), jnp.zeros((FAR_Q, HD), f32)),
        )
        total = jnp.sum(total, axis=1, keepdims=True)
        out = (acc / total).astype(bf16)
        lse = jnp.where(m > 0.5 * LOW, m + jnp.log2(total), LOW)
        high = lse.astype(bf16).astype(f32)
        left = lse - high
        mid = left.astype(bf16).astype(f32)
        low = left - mid
        for e in range(per):
            at = slice(e * POS, (e + 1) * POS)
            terms = jnp.where(
                lane == 0,
                high[at],
                jnp.where(lane == 1, mid[at], jnp.where(lane == 2, low[at], 0.0)),
            ).astype(bf16)
            out_ref[b * per + e, :POS, :] = out[at]
            out_ref[b * per + e, POS:, :] = dot_t(eye, terms).astype(bf16)
        send(b).start()
        return unused

    lax.fori_loop(0, FAR_BLOCKS, block, 0)
    for b in range(FAR_BLOCKS):
        send(b).wait()


def place_kernel(col_hbm, row_hbm, out_hbm, col_ref, row_ref, out_ref, sems):
    ins = [
        pltpu.make_async_copy(col_hbm, col_ref, sems.at[0]),
        pltpu.make_async_copy(row_hbm, row_ref, sems.at[1]),
    ]
    for move in ins:
        move.start()
    back = one_hot(
        POS, POS, lambda o: (o & 3) * STRIDE + ((o >> 2) & 7) * 4 + (o >> 5)
    )
    for move in ins:
        move.wait()
    moves = []
    for quad in range(QUADS):
        out_ref[quad, :, :HD] = row_ref[quad]
        stack = jnp.concatenate(
            [col_ref[x, quad * STRIDE : (quad + 1) * STRIDE, :] for x in range(4)], axis=0
        )
        out_ref[quad, :, HD:] = dot(back, stack).astype(bf16)
        move = pltpu.make_async_copy(
            out_ref.at[quad], out_hbm.at[:, pl.ds(quad * 4 * HD, 2 * HD)], sems.at[2 + quad]
        )
        move.start()
        moves.append(move)
    for move in moves:
        move.wait()


def merge_kernel(
    placed_hbm, far_hbm, part_hbm, stat_hbm, out_hbm, far_ref, part_ref, stat_ref, out_ref, sems
):
    ins = [
        pltpu.make_async_copy(far_hbm, far_ref, sems.at[0]),
        pltpu.make_async_copy(stat_hbm, stat_ref, sems.at[1]),
    ]
    for g in range(0, HEADS, 4):
        some = pl.ds(g, 4)
        ins.append(
            pltpu.make_async_copy(part_hbm.at[some], part_ref.at[some], sems.at[2 + g // 4])
        )
    for move in ins:
        move.start()
    row = iota((HEADS * SUM_ROWS, 128), 0)
    lane = iota((HEADS * SUM_ROWS, 128), 1)
    pick = jnp.where(
        jnp.logical_and((row >> 4) == lane, (row & 15) < 3), 1.0, 0.0
    ).astype(bf16)
    ins[0].wait()
    ins[1].wait()
    terms = jnp.concatenate([far_ref[g, POS:, :] for g in range(HEADS)], axis=0)
    lse = dot_tl(terms, pick)
    top = jnp.maximum(stat_ref[0], lse)
    own = jnp.exp2(stat_ref[0] - top)
    far = jnp.exp2(lse - top)
    scale = 1.0 / (stat_ref[1] * own + far)
    own = own * scale
    far = far * scale
    moves = []
    for g in range(HEADS):
        if g % 4 == 0:
            ins[2 + g // 4].wait()
        merged = (
            part_ref[g] * own[:, g : g + 1]
            + far_ref[g, :POS, :].astype(f32) * far[:, g : g + 1]
        )
        quad, h = g // 2, g % 2
        out_ref[quad, :, h * HD : (h + 1) * HD] = merged.astype(bf16)
        if h == 1:
            move = pltpu.make_async_copy(
                out_ref.at[quad],
                out_hbm.at[:, pl.ds((quad * 4 + 2) * HD, 2 * HD)],
                sems.at[6 + quad],
            )
            move.start()
            moves.append(move)
    for move in moves:
        move.wait()


VMEM_BYTES = 63_000_000
SPACES = {"v": pltpu.VMEM, "s": pltpu.SMEM, "h": pl.ANY}


def call(kernel, outs, args, ins, to="v", scratch=(), flops=0, moved=0, exps=0, alias=None, room=0):
    def spec(space):
        return pl.BlockSpec(memory_space=SPACES[space])

    shapes = [jax.ShapeDtypeStruct(s, d) for s, d in outs]
    many = len(shapes) > 1
    return pl.pallas_call(
        kernel,
        out_shape=shapes if many else shapes[0],
        in_specs=[spec(space) for space in ins],
        out_specs=[spec(to)] * len(shapes) if many else spec(to),
        scratch_shapes=list(scratch),
        input_output_aliases=alias or {},
        compiler_params=pltpu.CompilerParams(vmem_limit_bytes=VMEM_BYTES - room),
        cost_estimate=pl.CostEstimate(flops=flops, bytes_accessed=moved, transcendentals=exps),
    )(*args)


def exchange(array, axes):
    return lax.all_to_all(array, axes, split_axis=0, concat_axis=0, tiled=True)


def dma(n):
    return pltpu.SemaphoreType.DMA((n,))


mib = 1 << 20


def pack_summary(keys, values):
    return call(
        pack_summary_kernel,
        [((64, 8, HD), bf16)],
        (keys, values),
        "hh",
        to="h",
        scratch=[
            pltpu.VMEM((128, QUADS * 4 * HD), bf16),
            pltpu.VMEM((HEADS, 8, HD), bf16),
            dma(12),
        ],
        flops=2 * 16 * 16 * 128 * 128,
        moved=mib,
    )


def pack(queries, keys, values):
    return call(
        pack_kernel,
        [((QUADS, 384, HD), bf16), ((HEADS, POS, HD), bf16)],
        (queries, keys, values),
        "hhh",
        to="h",
        scratch=[
            pltpu.VMEM((QUADS, POS, 3 * HD), bf16),
            pltpu.VMEM((QUADS, POS, HD), bf16),
            pltpu.VMEM((QUADS, POS, HD), bf16),
            pltpu.VMEM((QUADS, 384, HD), bf16),
            pltpu.VMEM((HEADS, POS, HD), bf16),
            dma(24),
            dma(16),
        ],
        flops=2 * 8 * 384 * 384 * 128,
        moved=4 * mib,
    )


def ordered(after, array, room=46_000_000):
    return call(
        order_kernel,
        [(array.shape, array.dtype)],
        (after, array),
        "hh",
        to="h",
        alias={1: 0},
        room=room,
    )


def rows(queries, keys, values):
    outs = [((QUADS, POS, HD), bf16), ((HEADS, POS, HD), f32), ((2, POS, 128), f32)]
    return call(
        rows_kernel,
        outs,
        (queries, keys, values),
        "hhh",
        to="h",
        scratch=[pltpu.VMEM((POS, QUADS * 4 * HD), bf16)] * 3
        + [pltpu.VMEM(*out) for out in outs]
        + [dma(13)],
        flops=24 * 4 * 128 * 128 * 128,
        moved=5 * mib,
        exps=24 * 128 * 128,
    )


def columns(core, items, other):
    return call(
        column_kernel,
        [((4, 256, HD), bf16)],
        (core, items, other),
        "svv",
        to="h",
        scratch=[
            pltpu.VMEM((4, 256, HD), bf16),
            pltpu.VMEM((1024, HD), bf16),
            pltpu.VMEM((2, 1024, HD), bf16),
            pltpu.VMEM((2, 1024, HD), bf16),
            dma(4),
        ],
        room=46_000_000,
        flops=4 * 1024 * 1280 * 128,
        moved=2 * mib,
        exps=1024 * 1280,
    )


def far_part(pair, heads, summary):
    return call(
        far_kernel,
        [((HEADS, PAY, HD), bf16)],
        (pair, heads, summary),
        "shh",
        to="h",
        scratch=[
            pltpu.VMEM((HEADS, POS, HD), bf16),
            pltpu.VMEM((8, 2, 256, HD), bf16),
            pltpu.VMEM((HEADS, PAY, HD), bf16),
            pltpu.VMEM((2048 // FAR_K, FAR_Q, FAR_K), f32),
            dma(2 + FAR_BLOCKS),
        ],
        flops=8 * 1024 * 2048 * 128,
        moved=3 * mib,
        exps=2 * 1024 * 2048,
    )


def place(column, row_out):
    return call(
        place_kernel,
        [((POS, QUADS * 4 * HD), bf16)],
        (column, row_out),
        "hh",
        to="h",
        scratch=[
            pltpu.VMEM((4, 256, HD), bf16),
            pltpu.VMEM((QUADS, POS, HD), bf16),
            pltpu.VMEM((QUADS, POS, 2 * HD), bf16),
            dma(10),
        ],
        room=46_000_000,
        flops=2 * 8 * 128 * 128 * 128,
        moved=mib,
    )


def merge(placed, far, part, stat):
    return call(
        merge_kernel,
        [((POS, QUADS * 4 * HD), bf16)],
        (placed, far, part, stat),
        "hhhh",
        to="h",
        scratch=[
            pltpu.VMEM((HEADS, PAY, HD), bf16),
            pltpu.VMEM((HEADS, POS, HD), f32),
            pltpu.VMEM((2, POS, 128), f32),
            pltpu.VMEM((QUADS, POS, 2 * HD), bf16),
            dma(14),
        ],
        alias={0: 0},
        room=500_000,
        flops=2 * 8 * 128 * 128 * 128,
        moved=3 * mib,
    )


def body(queries, keys, values):
    heads_at = ("w", "c", "x")
    plane = ("u", "v", "w", "c", "x")
    wide = ("z", "u", "v", "w", "x")
    back = ("x", "z", "u", "v", "w")
    summary = exchange(pack_summary(keys, values), plane)
    summary = summary.reshape(64, 2, ROWS, HD).transpose(1, 0, 2, 3).reshape(1, 2, 256, HD)
    items, heads = pack(queries, keys, values)
    items = ordered(summary, items, room=0)
    summary = lax.all_gather(summary, "z", axis=0, tiled=True)
    items = exchange(items.reshape(768, ROWS, HD), wide).reshape(3072, HD)
    row_out, part, stat = rows(queries, keys, values)
    items = ordered(stat, items)
    heads = exchange(ordered(stat, heads), heads_at)
    other = lax.ppermute(items, "c", [(0, 1), (1, 0)])
    core = lax.axis_index("c").astype(jnp.int32).reshape(1)
    column = columns(core, items, other)
    column = exchange(column.reshape(256, ROWS, HD), back).reshape(4, 256, HD)
    pair = lax.axis_index(("z", "u", "v")).astype(jnp.int32).reshape(1)
    far = exchange(far_part(pair, heads, summary), heads_at)
    return merge(place(column, row_out), far, part, stat)


def solution(mesh):
    fine = Mesh(mesh.devices.reshape(4, 8, 2, 2, 2, 2), ("x", "z", "u", "v", "w", "c"))
    spec = P(("z", "u", "v", "w", "c", "x"), None)
    return jax.shard_map(
        body, mesh=fine, in_specs=(spec, spec, spec), out_specs=spec, check_vma=False
    )
```

```python
import math

import jax
import jax.numpy as jnp
from jax import lax
from jax.experimental import pallas as pl
from jax.experimental.pallas import tpu as pltpu
from jax.sharding import Mesh
from jax.sharding import PartitionSpec as P

HD = 128
STRIDE = 32
QUADS = 8
POS = 128
ROWS = 4
LOW = -1e30
SCALE = math.log2(math.e) / math.sqrt(HD)
SUM_ROWS = 16
PAY = POS + SUM_ROWS
HEADS = 16
PAIR = HEADS * POS

f32 = jnp.float32
bf16 = jnp.bfloat16


def dot_t(a, b):
    return lax.dot_general(a, b, (((1,), (1,)), ((), ())), preferred_element_type=f32)


def dot_tl(a, b):
    return lax.dot_general(a, b, (((0,), (0,)), ((), ())), preferred_element_type=f32)


def dot(a, b):
    return lax.dot_general(a, b, (((1,), (0,)), ((), ())), preferred_element_type=f32)


def iota(shape, dim):
    return lax.broadcasted_iota(jnp.int32, shape, dim)


def one_hot(rows, cols, source):
    row = iota((rows, cols), 0)
    col = iota((rows, cols), 1)
    return jnp.where(source(row) == col, 1.0, 0.0).astype(bf16)


def div12(o):
    return (o * 5462) >> 16


def head(ref, quad, kind):
    start = (quad * 4 + kind) * HD
    return ref[:, start : start + HD]


def pack_summary_kernel(k_ref, v_ref, sum_hbm, buf, sum_ref, sems):
    moves = []
    for a, ref in enumerate((k_ref, v_ref)):
        for r in range(ROWS):
            move = pltpu.make_async_copy(
                ref.at[pl.ds(r * STRIDE + 16, 16), :],
                buf.at[pl.ds((a * ROWS + r) * 16, 16), :],
                sems.at[a * ROWS + r],
            )
            move.start()
            moves.append(move)
    pick = one_hot(8, 128, lambda o: o * 16 + 15)
    for move in moves:
        move.wait()
    for g in range(HEADS):
        rows = dot(pick, head(buf, g // 2, 2 + g % 2)).astype(bf16)
        sum_ref[g] = rows
    moves = []
    for t in range(sum_hbm.shape[0] // HEADS):
        move = pltpu.make_async_copy(
            sum_ref, sum_hbm.at[pl.ds(t * HEADS, HEADS)], sems.at[2 * ROWS + t]
        )
        move.start()
        moves.append(move)
    for move in moves:
        move.wait()


def pack_kernel(q_hbm, k_hbm, v_hbm, item_hbm, query_hbm, qs, ks, vs, items, heads, ins, outs):
    def source(o):
        col = div12(o)
        rest = o - 12 * col
        return (rest >> 2) * POS + (rest & 3) * STRIDE + col

    def fetch(quad):
        at = quad * 4 * HD
        return [
            pltpu.make_async_copy(
                q_hbm.at[:, pl.ds(at + HD, 3 * HD)], qs.at[quad], ins.at[quad * 3]
            ),
            pltpu.make_async_copy(
                k_hbm.at[:, pl.ds(at + HD, HD)], ks.at[quad], ins.at[quad * 3 + 1]
            ),
            pltpu.make_async_copy(
                v_hbm.at[:, pl.ds(at + HD, HD)], vs.at[quad], ins.at[quad * 3 + 2]
            ),
        ]

    for quad in range(QUADS):
        for move in fetch(quad):
            move.start()
    perm = one_hot(384, 384, source)
    moves = []
    for quad in range(QUADS):
        for move in fetch(quad):
            move.wait()
        stack = jnp.concatenate([qs[quad, :, :HD], ks[quad], vs[quad]], axis=0)
        items[quad] = dot(perm, stack).astype(bf16)
        heads[quad * 2] = qs[quad, :, HD : 2 * HD]
        heads[quad * 2 + 1] = qs[quad, :, 2 * HD :]
        two = pl.ds(quad * 2, 2)
        for move in (
            pltpu.make_async_copy(items.at[quad], item_hbm.at[quad], outs.at[quad * 2]),
            pltpu.make_async_copy(heads.at[two], query_hbm.at[two], outs.at[quad * 2 + 1]),
        ):
            move.start()
            moves.append(move)
    for move in moves:
        move.wait()


def order_kernel(after_ref, array_ref, out_ref):
    pass


def rows_kernel(
    q_hbm, k_hbm, v_hbm, row_hbm, part_hbm, stat_hbm,
    q_ref, k_ref, v_ref, row_ref, part_ref, stat_ref, sems,
):
    ins = []
    for a, (hbm, ref) in enumerate(((q_hbm, q_ref), (k_hbm, k_ref), (v_hbm, v_ref))):
        move = pltpu.make_async_copy(hbm, ref, sems.at[a])
        move.start()
        ins.append(move)
    pos = iota((POS, POS), 0)
    key = iota((POS, POS), 1)
    visible = jnp.logical_and((key >> 5) == (pos >> 5), key <= pos)
    tops = jnp.zeros((POS, POS), f32)
    sums = jnp.ones((POS, POS), f32)
    for move in ins:
        move.wait()
    moves = []
    for quad in range(QUADS):
        for kind in (0, 2, 3):
            s = dot_t(head(q_ref, quad, kind), head(k_ref, quad, kind)) * SCALE
            s = jnp.where(visible, s, LOW)
            m = jnp.max(s, axis=1, keepdims=True)
            p = jnp.where(visible, jnp.exp2(s - m), 0.0)
            total = jnp.sum(p, axis=1, keepdims=True)
            acc = dot(p.astype(bf16), head(v_ref, quad, kind))
            if kind == 0:
                row_ref[quad] = (acc / total).astype(bf16)
            else:
                slot = quad * 2 + kind - 2
                part_ref[slot] = acc
                tops = jnp.where(key == slot, m, tops)
                sums = jnp.where(key == slot, total, sums)
        two = pl.ds(quad * 2, 2)
        moves.append(pltpu.make_async_copy(part_ref.at[two], part_hbm.at[two], sems.at[3 + quad]))
        moves[-1].start()
    stat_ref[0] = tops
    stat_ref[1] = sums
    moves.append(pltpu.make_async_copy(row_ref, row_hbm, sems.at[11]))
    moves.append(pltpu.make_async_copy(stat_ref, stat_hbm, sems.at[12]))
    moves[-1].start()
    moves[-2].start()
    for move in moves:
        move.wait()


def column_kernel(
    core_ref, own_ref, other_ref, out_hbm, out_scr, q_scr, k_scr, v_scr, sems
):
    core = core_ref[0]

    def source(o):
        within = o & 31
        return (within >> 2) * 12 + (o >> 5) * 4 + (within & 3)

    split = one_hot(96, 96, source)
    split_kv = one_hot(64, 96, lambda o: source(o + 32))
    by_x = one_hot(POS, POS, lambda o: ((o >> 2) & 7) * 16 + (o >> 5) * 4 + (o & 3))
    for g in range(32):
        at = slice(g * 32, (g + 1) * 32)
        y = dot(split, own_ref[g * 96 : (g + 1) * 96, :]).astype(bf16)
        q_scr[at, :] = y[0:32]
        k_scr[0, at, :] = y[32:64]
        v_scr[0, at, :] = y[64:96]
        y = dot(split_kv, other_ref[g * 96 : (g + 1) * 96, :]).astype(bf16)
        k_scr[1, at, :] = y[0:32]
        v_scr[1, at, :] = y[32:64]

    block = 256
    jq = iota((block, block), 0)
    jk = iota((block, block), 1)
    visible = (jk <= jq, (jk >> 4) < (jq >> 4) + core)
    moves = []
    for qb in range(1024 // block):
        q = q_scr[qb * block : (qb + 1) * block, :]
        pieces = []
        top = None
        for kb in range(qb + 1):
            for c in range(2):
                s = dot_t(q, k_scr[c, kb * block : (kb + 1) * block, :]) * SCALE
                if kb == qb:
                    s = jnp.where(visible[c], s, LOW)
                fold = jnp.maximum(s[:, :128], s[:, 128:])
                top = fold if top is None else jnp.maximum(top, fold)
                pieces.append((kb, c, s))
        m = jnp.max(top, axis=1, keepdims=True)
        total = jnp.zeros((block, 128), f32)
        acc = jnp.zeros((block, HD), f32)
        for kb, c, s in pieces:
            p = jnp.exp2(s - m)
            total = total + (p[:, :128] + p[:, 128:])
            acc = acc + dot(p.astype(bf16), v_scr[c, kb * block : (kb + 1) * block, :])
        total = jnp.sum(total, axis=1, keepdims=True)
        out = (acc / total).astype(bf16)
        for t in range(block // POS):
            y = dot(by_x, out[t * POS : (t + 1) * POS]).astype(bf16)
            at = (qb * block // POS + t) * STRIDE
            for x in range(4):
                out_scr[x, at : at + STRIDE, :] = y[x * STRIDE : (x + 1) * STRIDE]
        at = pl.ds(qb * block // 4, block // 4)
        move = pltpu.make_async_copy(out_scr.at[:, at, :], out_hbm.at[:, at, :], sems.at[qb])
        move.start()
        moves.append(move)
    for move in moves:
        move.wait()


FAR_Q = 1024
FAR_K = 2048
FAR_BLOCKS = PAIR // FAR_Q


def far_kernel(pair_ref, q_hbm, kv_hbm, out_hbm, q_ref, kv_ref, out_ref, s_scr, sems):
    pair = pair_ref[0]
    ins = [
        pltpu.make_async_copy(q_hbm, q_ref, sems.at[0]),
        pltpu.make_async_copy(kv_hbm, kv_ref, sems.at[1]),
    ]
    for move in ins:
        move.start()
    row_ids = PAIR // STRIDE
    last = (pair * row_ids) // FAR_K
    lane = iota((POS, 128), 1)
    eye = one_hot(SUM_ROWS, 128, lambda o: o)
    per = FAR_Q // POS
    planes = FAR_K // 256

    for move in ins:
        move.wait()

    def send(b):
        at = pl.ds(b * per, per)
        return pltpu.make_async_copy(out_ref.at[at], out_hbm.at[at], sems.at[2 + b])

    def piece(i, j):
        return jnp.concatenate([kv_ref[i * planes + t, j] for t in range(planes)], axis=0)

    def fold(x, op):
        r = x[:, :128]
        for t in range(1, FAR_K // 128):
            r = op(r, x[:, t * 128 : (t + 1) * 128])
        return r

    def block(b, unused):
        q = q_ref[pl.ds(b * per, per)].reshape(FAR_Q, HD)

        def score(i, top):
            s = dot_t(q, piece(i, 0)) * SCALE
            s_scr[i] = s
            return jnp.maximum(top, fold(s, jnp.maximum))

        top = lax.fori_loop(0, last, score, jnp.full((FAR_Q, 128), LOW, f32))
        s = dot_t(q, piece(last, 0)) * SCALE
        row_k = last * FAR_K + iota((FAR_Q, FAR_K), 1)
        row_q = pair * row_ids + ((b * FAR_Q + iota((FAR_Q, FAR_K), 0)) >> 5)
        s = jnp.where(row_k < row_q, s, LOW)
        s_scr[last] = s
        top = jnp.maximum(top, fold(s, jnp.maximum))
        m = jnp.max(top, axis=1, keepdims=True)

        def weigh(i, carried):
            total, acc = carried
            p = jnp.exp2(s_scr[i] - m)
            return (
                total + fold(p, jnp.add),
                acc + dot(p.astype(bf16), piece(i, 1)),
            )

        total, acc = lax.fori_loop(
            0,
            last + 1,
            weigh,
            (jnp.zeros((FAR_Q, 128), f32), jnp.zeros((FAR_Q, HD), f32)),
        )
        total = jnp.sum(total, axis=1, keepdims=True)
        out = (acc / total).astype(bf16)
        lse = jnp.where(m > 0.5 * LOW, m + jnp.log2(total), LOW)
        high = lse.astype(bf16).astype(f32)
        left = lse - high
        mid = left.astype(bf16).astype(f32)
        low = left - mid
        for e in range(per):
            at = slice(e * POS, (e + 1) * POS)
            terms = jnp.where(
                lane == 0,
                high[at],
                jnp.where(lane == 1, mid[at], jnp.where(lane == 2, low[at], 0.0)),
            ).astype(bf16)
            out_ref[b * per + e, :POS, :] = out[at]
            out_ref[b * per + e, POS:, :] = dot_t(eye, terms).astype(bf16)
        send(b).start()
        return unused

    lax.fori_loop(0, FAR_BLOCKS, block, 0)
    for b in range(FAR_BLOCKS):
        send(b).wait()


def place_kernel(col_hbm, row_hbm, out_hbm, col_ref, row_ref, out_ref, sems):
    ins = [
        pltpu.make_async_copy(col_hbm, col_ref, sems.at[0]),
        pltpu.make_async_copy(row_hbm, row_ref, sems.at[1]),
    ]
    for move in ins:
        move.start()
    back = one_hot(
        POS, POS, lambda o: (o & 3) * STRIDE + ((o >> 2) & 7) * 4 + (o >> 5)
    )
    for move in ins:
        move.wait()
    moves = []
    for quad in range(QUADS):
        out_ref[quad, :, :HD] = row_ref[quad]
        stack = jnp.concatenate(
            [col_ref[x, quad * STRIDE : (quad + 1) * STRIDE, :] for x in range(4)], axis=0
        )
        out_ref[quad, :, HD:] = dot(back, stack).astype(bf16)
        move = pltpu.make_async_copy(
            out_ref.at[quad], out_hbm.at[:, pl.ds(quad * 4 * HD, 2 * HD)], sems.at[2 + quad]
        )
        move.start()
        moves.append(move)
    for move in moves:
        move.wait()


def merge_kernel(
    placed_hbm, far_hbm, part_hbm, stat_hbm, out_hbm, far_ref, part_ref, stat_ref, out_ref, sems
):
    ins = [
        pltpu.make_async_copy(far_hbm, far_ref, sems.at[0]),
        pltpu.make_async_copy(stat_hbm, stat_ref, sems.at[1]),
    ]
    for g in range(0, HEADS, 4):
        some = pl.ds(g, 4)
        ins.append(
            pltpu.make_async_copy(part_hbm.at[some], part_ref.at[some], sems.at[2 + g // 4])
        )
    for move in ins:
        move.start()
    row = iota((HEADS * SUM_ROWS, 128), 0)
    lane = iota((HEADS * SUM_ROWS, 128), 1)
    pick = jnp.where(
        jnp.logical_and((row >> 4) == lane, (row & 15) < 3), 1.0, 0.0
    ).astype(bf16)
    ins[0].wait()
    ins[1].wait()
    terms = jnp.concatenate([far_ref[g, POS:, :] for g in range(HEADS)], axis=0)
    lse = dot_tl(terms, pick)
    top = jnp.maximum(stat_ref[0], lse)
    own = jnp.exp2(stat_ref[0] - top)
    far = jnp.exp2(lse - top)
    scale = 1.0 / (stat_ref[1] * own + far)
    own = own * scale
    far = far * scale
    moves = []
    for g in range(HEADS):
        if g % 4 == 0:
            ins[2 + g // 4].wait()
        merged = (
            part_ref[g] * own[:, g : g + 1]
            + far_ref[g, :POS, :].astype(f32) * far[:, g : g + 1]
        )
        quad, h = g // 2, g % 2
        out_ref[quad, :, h * HD : (h + 1) * HD] = merged.astype(bf16)
        if h == 1:
            move = pltpu.make_async_copy(
                out_ref.at[quad],
                out_hbm.at[:, pl.ds((quad * 4 + 2) * HD, 2 * HD)],
                sems.at[6 + quad],
            )
            move.start()
            moves.append(move)
    for move in moves:
        move.wait()


VMEM_BYTES = 63_000_000
SPACES = {"v": pltpu.VMEM, "s": pltpu.SMEM, "h": pl.ANY}


def call(kernel, outs, args, ins, to="v", scratch=(), flops=0, moved=0, exps=0, alias=None, room=0):
    def spec(space):
        return pl.BlockSpec(memory_space=SPACES[space])

    shapes = [jax.ShapeDtypeStruct(s, d) for s, d in outs]
    many = len(shapes) > 1
    return pl.pallas_call(
        kernel,
        out_shape=shapes if many else shapes[0],
        in_specs=[spec(space) for space in ins],
        out_specs=[spec(to)] * len(shapes) if many else spec(to),
        scratch_shapes=list(scratch),
        input_output_aliases=alias or {},
        compiler_params=pltpu.CompilerParams(vmem_limit_bytes=VMEM_BYTES - room),
        cost_estimate=pl.CostEstimate(flops=flops, bytes_accessed=moved, transcendentals=exps),
    )(*args)


def exchange(array, axes):
    return lax.all_to_all(array, axes, split_axis=0, concat_axis=0, tiled=True)


def dma(n):
    return pltpu.SemaphoreType.DMA((n,))


mib = 1 << 20


def pack_summary(keys, values):
    return call(
        pack_summary_kernel,
        [((64, 8, HD), bf16)],
        (keys, values),
        "hh",
        to="h",
        scratch=[
            pltpu.VMEM((128, QUADS * 4 * HD), bf16),
            pltpu.VMEM((HEADS, 8, HD), bf16),
            dma(12),
        ],
        flops=2 * 16 * 16 * 128 * 128,
        moved=mib,
    )


def pack(queries, keys, values):
    return call(
        pack_kernel,
        [((QUADS, 384, HD), bf16), ((HEADS, POS, HD), bf16)],
        (queries, keys, values),
        "hhh",
        to="h",
        scratch=[
            pltpu.VMEM((QUADS, POS, 3 * HD), bf16),
            pltpu.VMEM((QUADS, POS, HD), bf16),
            pltpu.VMEM((QUADS, POS, HD), bf16),
            pltpu.VMEM((QUADS, 384, HD), bf16),
            pltpu.VMEM((HEADS, POS, HD), bf16),
            dma(24),
            dma(16),
        ],
        flops=2 * 8 * 384 * 384 * 128,
        moved=4 * mib,
    )


def ordered(after, array, room=46_000_000):
    return call(
        order_kernel,
        [(array.shape, array.dtype)],
        (after, array),
        "hh",
        to="h",
        alias={1: 0},
        room=room,
    )


def rows(queries, keys, values):
    outs = [((QUADS, POS, HD), bf16), ((HEADS, POS, HD), f32), ((2, POS, 128), f32)]
    return call(
        rows_kernel,
        outs,
        (queries, keys, values),
        "hhh",
        to="h",
        scratch=[pltpu.VMEM((POS, QUADS * 4 * HD), bf16)] * 3
        + [pltpu.VMEM(*out) for out in outs]
        + [dma(13)],
        flops=24 * 4 * 128 * 128 * 128,
        moved=5 * mib,
        exps=24 * 128 * 128,
    )


def columns(core, items, other):
    return call(
        column_kernel,
        [((4, 256, HD), bf16)],
        (core, items, other),
        "svv",
        to="h",
        scratch=[
            pltpu.VMEM((4, 256, HD), bf16),
            pltpu.VMEM((1024, HD), bf16),
            pltpu.VMEM((2, 1024, HD), bf16),
            pltpu.VMEM((2, 1024, HD), bf16),
            dma(4),
        ],
        room=46_000_000,
        flops=4 * 1024 * 1280 * 128,
        moved=2 * mib,
        exps=1024 * 1280,
    )


def far_part(pair, heads, summary):
    return call(
        far_kernel,
        [((HEADS, PAY, HD), bf16)],
        (pair, heads, summary),
        "shh",
        to="h",
        scratch=[
            pltpu.VMEM((HEADS, POS, HD), bf16),
            pltpu.VMEM((8, 2, 256, HD), bf16),
            pltpu.VMEM((HEADS, PAY, HD), bf16),
            pltpu.VMEM((2048 // FAR_K, FAR_Q, FAR_K), f32),
            dma(2 + FAR_BLOCKS),
        ],
        flops=8 * 1024 * 2048 * 128,
        moved=3 * mib,
        exps=2 * 1024 * 2048,
    )


def place(column, row_out):
    return call(
        place_kernel,
        [((POS, QUADS * 4 * HD), bf16)],
        (column, row_out),
        "hh",
        to="h",
        scratch=[
            pltpu.VMEM((4, 256, HD), bf16),
            pltpu.VMEM((QUADS, POS, HD), bf16),
            pltpu.VMEM((QUADS, POS, 2 * HD), bf16),
            dma(10),
        ],
        room=46_000_000,
        flops=2 * 8 * 128 * 128 * 128,
        moved=mib,
    )


def merge(placed, far, part, stat):
    return call(
        merge_kernel,
        [((POS, QUADS * 4 * HD), bf16)],
        (placed, far, part, stat),
        "hhhh",
        to="h",
        scratch=[
            pltpu.VMEM((HEADS, PAY, HD), bf16),
            pltpu.VMEM((HEADS, POS, HD), f32),
            pltpu.VMEM((2, POS, 128), f32),
            pltpu.VMEM((QUADS, POS, 2 * HD), bf16),
            dma(14),
        ],
        alias={0: 0},
        room=900_000,
        flops=2 * 8 * 128 * 128 * 128,
        moved=3 * mib,
    )


def body(queries, keys, values):
    heads_at = ("w", "c", "x")
    plane = ("u", "v", "w", "c", "x")
    wide = ("z", "u", "v", "w", "x")
    back = ("x", "z", "u", "v", "w")
    summary = exchange(pack_summary(keys, values), plane)
    items, heads = pack(queries, keys, values)
    items = ordered(summary, items, room=0)
    summary = summary.reshape(64, 2, ROWS, HD).transpose(1, 0, 2, 3).reshape(1, 2, 256, HD)
    summary = lax.all_gather(summary, "z", axis=0, tiled=True)
    items = exchange(items.reshape(768, ROWS, HD), wide).reshape(3072, HD)
    row_out, part, stat = rows(queries, keys, values)
    items = ordered(stat, items)
    heads = exchange(ordered(stat, heads), heads_at)
    other = lax.ppermute(items, "c", [(0, 1), (1, 0)])
    core = lax.axis_index("c").astype(jnp.int32).reshape(1)
    column = columns(core, items, other)
    column = exchange(column.reshape(256, ROWS, HD), back).reshape(4, 256, HD)
    pair = lax.axis_index(("z", "u", "v")).astype(jnp.int32).reshape(1)
    far = exchange(far_part(pair, heads, summary), heads_at)
    return merge(place(column, row_out), far, part, stat)


def solution(mesh):
    fine = Mesh(mesh.devices.reshape(4, 8, 2, 2, 2, 2), ("x", "z", "u", "v", "w", "c"))
    spec = P(("z", "u", "v", "w", "c", "x"), None)
    return jax.shard_map(
        body, mesh=fine, in_specs=(spec, spec, spec), out_specs=spec, check_vma=False
    )
```

```python
import math

import jax
import jax.numpy as jnp
from jax import lax
from jax.experimental import pallas as pl
from jax.experimental.pallas import tpu as pltpu
from jax.sharding import Mesh
from jax.sharding import PartitionSpec as P

HD = 128
STRIDE = 32
QUADS = 8
POS = 128
ROWS = 4
LOW = -1e30
SCALE = math.log2(math.e) / math.sqrt(HD)
SUM_ROWS = 16
PAY = POS + SUM_ROWS
HEADS = 16
PAIR = HEADS * POS

f32 = jnp.float32
bf16 = jnp.bfloat16


def dot_t(a, b):
    return lax.dot_general(a, b, (((1,), (1,)), ((), ())), preferred_element_type=f32)


def dot_tl(a, b):
    return lax.dot_general(a, b, (((0,), (0,)), ((), ())), preferred_element_type=f32)


def dot(a, b):
    return lax.dot_general(a, b, (((1,), (0,)), ((), ())), preferred_element_type=f32)


def iota(shape, dim):
    return lax.broadcasted_iota(jnp.int32, shape, dim)


def one_hot(rows, cols, source):
    row = iota((rows, cols), 0)
    col = iota((rows, cols), 1)
    return jnp.where(source(row) == col, 1.0, 0.0).astype(bf16)


def div12(o):
    return (o * 5462) >> 16


def head(ref, quad, kind):
    start = (quad * 4 + kind) * HD
    return ref[:, start : start + HD]


def pack_summary_kernel(k_ref, v_ref, sum_hbm, buf, sum_ref, sems):
    moves = []
    for a, ref in enumerate((k_ref, v_ref)):
        for r in range(ROWS):
            move = pltpu.make_async_copy(
                ref.at[pl.ds(r * STRIDE + 16, 16), :],
                buf.at[pl.ds((a * ROWS + r) * 16, 16), :],
                sems.at[a * ROWS + r],
            )
            move.start()
            moves.append(move)
    pick = one_hot(8, 128, lambda o: o * 16 + 15)
    for move in moves:
        move.wait()
    for g in range(HEADS):
        rows = dot(pick, head(buf, g // 2, 2 + g % 2)).astype(bf16)
        sum_ref[g] = rows
    moves = []
    for t in range(sum_hbm.shape[0] // HEADS):
        move = pltpu.make_async_copy(
            sum_ref, sum_hbm.at[pl.ds(t * HEADS, HEADS)], sems.at[2 * ROWS + t]
        )
        move.start()
        moves.append(move)
    for move in moves:
        move.wait()


def pack_kernel(q_hbm, k_hbm, v_hbm, item_hbm, query_hbm, qs, ks, vs, items, heads, ins, outs):
    def source(o):
        col = div12(o)
        rest = o - 12 * col
        return (rest >> 2) * POS + (rest & 3) * STRIDE + col

    def fetch(quad):
        at = quad * 4 * HD
        return [
            pltpu.make_async_copy(
                q_hbm.at[:, pl.ds(at + HD, 3 * HD)], qs.at[quad], ins.at[quad * 3]
            ),
            pltpu.make_async_copy(
                k_hbm.at[:, pl.ds(at + HD, HD)], ks.at[quad], ins.at[quad * 3 + 1]
            ),
            pltpu.make_async_copy(
                v_hbm.at[:, pl.ds(at + HD, HD)], vs.at[quad], ins.at[quad * 3 + 2]
            ),
        ]

    for quad in range(QUADS):
        for move in fetch(quad):
            move.start()
    perm = one_hot(384, 384, source)
    moves = []
    for quad in range(QUADS):
        for move in fetch(quad):
            move.wait()
        stack = jnp.concatenate([qs[quad, :, :HD], ks[quad], vs[quad]], axis=0)
        items[quad] = dot(perm, stack).astype(bf16)
        heads[quad * 2] = qs[quad, :, HD : 2 * HD]
        heads[quad * 2 + 1] = qs[quad, :, 2 * HD :]
        two = pl.ds(quad * 2, 2)
        for move in (
            pltpu.make_async_copy(items.at[quad], item_hbm.at[quad], outs.at[quad * 2]),
            pltpu.make_async_copy(heads.at[two], query_hbm.at[two], outs.at[quad * 2 + 1]),
        ):
            move.start()
            moves.append(move)
    for move in moves:
        move.wait()


def order_kernel(after_ref, array_ref, out_ref):
    pass


def rows_kernel(
    q_hbm, k_hbm, v_hbm, row_hbm, part_hbm, stat_hbm,
    q_ref, k_ref, v_ref, row_ref, part_ref, stat_ref, sems,
):
    ins = []
    for a, (hbm, ref) in enumerate(((q_hbm, q_ref), (k_hbm, k_ref), (v_hbm, v_ref))):
        move = pltpu.make_async_copy(hbm, ref, sems.at[a])
        move.start()
        ins.append(move)
    pos = iota((POS, POS), 0)
    key = iota((POS, POS), 1)
    visible = jnp.logical_and((key >> 5) == (pos >> 5), key <= pos)
    tops = jnp.zeros((POS, POS), f32)
    sums = jnp.ones((POS, POS), f32)
    for move in ins:
        move.wait()
    moves = []
    for quad in range(QUADS):
        for kind in (0, 2, 3):
            s = dot_t(head(q_ref, quad, kind), head(k_ref, quad, kind)) * SCALE
            s = jnp.where(visible, s, LOW)
            m = jnp.max(s, axis=1, keepdims=True)
            p = jnp.where(visible, jnp.exp2(s - m), 0.0)
            total = jnp.sum(p, axis=1, keepdims=True)
            acc = dot(p.astype(bf16), head(v_ref, quad, kind))
            if kind == 0:
                row_ref[quad] = (acc / total).astype(bf16)
            else:
                slot = quad * 2 + kind - 2
                part_ref[slot] = acc
                tops = jnp.where(key == slot, m, tops)
                sums = jnp.where(key == slot, total, sums)
        two = pl.ds(quad * 2, 2)
        moves.append(pltpu.make_async_copy(part_ref.at[two], part_hbm.at[two], sems.at[3 + quad]))
        moves[-1].start()
    stat_ref[0] = tops
    stat_ref[1] = sums
    moves.append(pltpu.make_async_copy(row_ref, row_hbm, sems.at[11]))
    moves.append(pltpu.make_async_copy(stat_ref, stat_hbm, sems.at[12]))
    moves[-1].start()
    moves[-2].start()
    for move in moves:
        move.wait()


def column_kernel(
    core_ref, own_ref, other_ref, out_hbm, out_scr, q_scr, k_scr, v_scr, sems
):
    core = core_ref[0]

    def source(o):
        within = o & 31
        return (within >> 2) * 12 + (o >> 5) * 4 + (within & 3)

    split = one_hot(96, 96, source)
    split_kv = one_hot(64, 96, lambda o: source(o + 32))
    by_x = one_hot(POS, POS, lambda o: ((o >> 2) & 7) * 16 + (o >> 5) * 4 + (o & 3))
    for g in range(32):
        at = slice(g * 32, (g + 1) * 32)
        y = dot(split, own_ref[g * 96 : (g + 1) * 96, :]).astype(bf16)
        q_scr[at, :] = y[0:32]
        k_scr[0, at, :] = y[32:64]
        v_scr[0, at, :] = y[64:96]
        y = dot(split_kv, other_ref[g * 96 : (g + 1) * 96, :]).astype(bf16)
        k_scr[1, at, :] = y[0:32]
        v_scr[1, at, :] = y[32:64]

    block = 256
    jq = iota((block, block), 0)
    jk = iota((block, block), 1)
    visible = (jk <= jq, (jk >> 4) < (jq >> 4) + core)
    moves = []
    for qb in range(1024 // block):
        q = q_scr[qb * block : (qb + 1) * block, :]
        pieces = []
        top = None
        for kb in range(qb + 1):
            for c in range(2):
                s = dot_t(q, k_scr[c, kb * block : (kb + 1) * block, :]) * SCALE
                if kb == qb:
                    s = jnp.where(visible[c], s, LOW)
                fold = jnp.maximum(s[:, :128], s[:, 128:])
                top = fold if top is None else jnp.maximum(top, fold)
                pieces.append((kb, c, s))
        m = jnp.max(top, axis=1, keepdims=True)
        total = jnp.zeros((block, 128), f32)
        acc = jnp.zeros((block, HD), f32)
        for kb, c, s in pieces:
            p = jnp.exp2(s - m)
            total = total + (p[:, :128] + p[:, 128:])
            acc = acc + dot(p.astype(bf16), v_scr[c, kb * block : (kb + 1) * block, :])
        total = jnp.sum(total, axis=1, keepdims=True)
        out = (acc / total).astype(bf16)
        for t in range(block // POS):
            y = dot(by_x, out[t * POS : (t + 1) * POS]).astype(bf16)
            at = (qb * block // POS + t) * STRIDE
            for x in range(4):
                out_scr[x, at : at + STRIDE, :] = y[x * STRIDE : (x + 1) * STRIDE]
        at = pl.ds(qb * block // 4, block // 4)
        move = pltpu.make_async_copy(out_scr.at[:, at, :], out_hbm.at[:, at, :], sems.at[qb])
        move.start()
        moves.append(move)
    for move in moves:
        move.wait()


FAR_Q = 1024
FAR_K = 2048
FAR_BLOCKS = PAIR // FAR_Q


def far_kernel(pair_ref, q_hbm, kv_hbm, out_hbm, q_ref, kv_ref, out_ref, s_scr, sems):
    pair = pair_ref[0]
    ins = [
        pltpu.make_async_copy(q_hbm, q_ref, sems.at[0]),
        pltpu.make_async_copy(kv_hbm, kv_ref, sems.at[1]),
    ]
    for move in ins:
        move.start()
    row_ids = PAIR // STRIDE
    last = (pair * row_ids) // FAR_K
    lane = iota((POS, 128), 1)
    eye = one_hot(SUM_ROWS, 128, lambda o: o)
    per = FAR_Q // POS
    planes = FAR_K // 256

    for move in ins:
        move.wait()

    def send(b):
        at = pl.ds(b * per, per)
        return pltpu.make_async_copy(out_ref.at[at], out_hbm.at[at], sems.at[2 + b])

    def piece(i, j):
        return jnp.concatenate([kv_ref[i * planes + t, j] for t in range(planes)], axis=0)

    def fold(x, op):
        r = x[:, :128]
        for t in range(1, FAR_K // 128):
            r = op(r, x[:, t * 128 : (t + 1) * 128])
        return r

    def block(b, unused):
        q = q_ref[pl.ds(b * per, per)].reshape(FAR_Q, HD)

        def score(i, top):
            s = dot_t(q, piece(i, 0)) * SCALE
            s_scr[i] = s
            return jnp.maximum(top, fold(s, jnp.maximum))

        top = lax.fori_loop(0, last, score, jnp.full((FAR_Q, 128), LOW, f32))
        s = dot_t(q, piece(last, 0)) * SCALE
        row_k = last * FAR_K + iota((FAR_Q, FAR_K), 1)
        row_q = pair * row_ids + ((b * FAR_Q + iota((FAR_Q, FAR_K), 0)) >> 5)
        s = jnp.where(row_k < row_q, s, LOW)
        s_scr[last] = s
        top = jnp.maximum(top, fold(s, jnp.maximum))
        m = jnp.max(top, axis=1, keepdims=True)

        def weigh(i, carried):
            total, acc = carried
            p = jnp.exp2(s_scr[i] - m)
            return (
                total + fold(p, jnp.add),
                acc + dot(p.astype(bf16), piece(i, 1)),
            )

        total, acc = lax.fori_loop(
            0,
            last + 1,
            weigh,
            (jnp.zeros((FAR_Q, 128), f32), jnp.zeros((FAR_Q, HD), f32)),
        )
        total = jnp.sum(total, axis=1, keepdims=True)
        out = (acc / total).astype(bf16)
        lse = jnp.where(m > 0.5 * LOW, m + jnp.log2(total), LOW)
        high = lse.astype(bf16).astype(f32)
        left = lse - high
        mid = left.astype(bf16).astype(f32)
        low = left - mid
        for e in range(per):
            at = slice(e * POS, (e + 1) * POS)
            terms = jnp.where(
                lane == 0,
                high[at],
                jnp.where(lane == 1, mid[at], jnp.where(lane == 2, low[at], 0.0)),
            ).astype(bf16)
            out_ref[b * per + e, :POS, :] = out[at]
            out_ref[b * per + e, POS:, :] = dot_t(eye, terms).astype(bf16)
        send(b).start()
        return unused

    lax.fori_loop(0, FAR_BLOCKS, block, 0)
    for b in range(FAR_BLOCKS):
        send(b).wait()


def place_kernel(col_hbm, row_hbm, out_hbm, col_ref, row_ref, out_ref, sems):
    ins = [
        pltpu.make_async_copy(col_hbm, col_ref, sems.at[0]),
        pltpu.make_async_copy(row_hbm, row_ref, sems.at[1]),
    ]
    for move in ins:
        move.start()
    back = one_hot(
        POS, POS, lambda o: (o & 3) * STRIDE + ((o >> 2) & 7) * 4 + (o >> 5)
    )
    for move in ins:
        move.wait()
    moves = []
    for quad in range(QUADS):
        out_ref[quad, :, :HD] = row_ref[quad]
        stack = jnp.concatenate(
            [col_ref[x, quad * STRIDE : (quad + 1) * STRIDE, :] for x in range(4)], axis=0
        )
        out_ref[quad, :, HD:] = dot(back, stack).astype(bf16)
        move = pltpu.make_async_copy(
            out_ref.at[quad], out_hbm.at[:, pl.ds(quad * 4 * HD, 2 * HD)], sems.at[2 + quad]
        )
        move.start()
        moves.append(move)
    for move in moves:
        move.wait()


def merge_kernel(
    placed_hbm, far_hbm, part_hbm, stat_hbm, out_hbm, far_ref, part_ref, stat_ref, out_ref, sems
):
    ins = [
        pltpu.make_async_copy(far_hbm, far_ref, sems.at[0]),
        pltpu.make_async_copy(stat_hbm, stat_ref, sems.at[1]),
    ]
    for g in range(0, HEADS, 4):
        some = pl.ds(g, 4)
        ins.append(
            pltpu.make_async_copy(part_hbm.at[some], part_ref.at[some], sems.at[2 + g // 4])
        )
    for move in ins:
        move.start()
    row = iota((HEADS * SUM_ROWS, 128), 0)
    lane = iota((HEADS * SUM_ROWS, 128), 1)
    pick = jnp.where(
        jnp.logical_and((row >> 4) == lane, (row & 15) < 3), 1.0, 0.0
    ).astype(bf16)
    ins[0].wait()
    ins[1].wait()
    terms = jnp.concatenate([far_ref[g, POS:, :] for g in range(HEADS)], axis=0)
    lse = dot_tl(terms, pick)
    top = jnp.maximum(stat_ref[0], lse)
    own = jnp.exp2(stat_ref[0] - top)
    far = jnp.exp2(lse - top)
    scale = 1.0 / (stat_ref[1] * own + far)
    own = own * scale
    far = far * scale
    moves = []
    for g in range(HEADS):
        if g % 4 == 0:
            ins[2 + g // 4].wait()
        merged = (
            part_ref[g] * own[:, g : g + 1]
            + far_ref[g, :POS, :].astype(f32) * far[:, g : g + 1]
        )
        quad, h = g // 2, g % 2
        out_ref[quad, :, h * HD : (h + 1) * HD] = merged.astype(bf16)
        if h == 1:
            move = pltpu.make_async_copy(
                out_ref.at[quad],
                out_hbm.at[:, pl.ds((quad * 4 + 2) * HD, 2 * HD)],
                sems.at[6 + quad],
            )
            move.start()
            moves.append(move)
    for move in moves:
        move.wait()


VMEM_BYTES = 63_000_000
SPACES = {"v": pltpu.VMEM, "s": pltpu.SMEM, "h": pl.ANY}


def call(kernel, outs, args, ins, to="v", scratch=(), flops=0, moved=0, exps=0, alias=None, room=0):
    def spec(space):
        return pl.BlockSpec(memory_space=SPACES[space])

    shapes = [jax.ShapeDtypeStruct(s, d) for s, d in outs]
    many = len(shapes) > 1
    return pl.pallas_call(
        kernel,
        out_shape=shapes if many else shapes[0],
        in_specs=[spec(space) for space in ins],
        out_specs=[spec(to)] * len(shapes) if many else spec(to),
        scratch_shapes=list(scratch),
        input_output_aliases=alias or {},
        compiler_params=pltpu.CompilerParams(vmem_limit_bytes=VMEM_BYTES - room),
        cost_estimate=pl.CostEstimate(flops=flops, bytes_accessed=moved, transcendentals=exps),
    )(*args)


def exchange(array, axes):
    return lax.all_to_all(array, axes, split_axis=0, concat_axis=0, tiled=True)


def dma(n):
    return pltpu.SemaphoreType.DMA((n,))


mib = 1 << 20


def pack_summary(keys, values):
    return call(
        pack_summary_kernel,
        [((64, 8, HD), bf16)],
        (keys, values),
        "hh",
        to="h",
        scratch=[
            pltpu.VMEM((128, QUADS * 4 * HD), bf16),
            pltpu.VMEM((HEADS, 8, HD), bf16),
            dma(12),
        ],
        flops=2 * 16 * 16 * 128 * 128,
        moved=mib,
    )


def pack(queries, keys, values):
    return call(
        pack_kernel,
        [((QUADS, 384, HD), bf16), ((HEADS, POS, HD), bf16)],
        (queries, keys, values),
        "hhh",
        to="h",
        scratch=[
            pltpu.VMEM((QUADS, POS, 3 * HD), bf16),
            pltpu.VMEM((QUADS, POS, HD), bf16),
            pltpu.VMEM((QUADS, POS, HD), bf16),
            pltpu.VMEM((QUADS, 384, HD), bf16),
            pltpu.VMEM((HEADS, POS, HD), bf16),
            dma(24),
            dma(16),
        ],
        flops=2 * 8 * 384 * 384 * 128,
        moved=4 * mib,
    )


def ordered(after, array, room=46_000_000):
    return call(
        order_kernel,
        [(array.shape, array.dtype)],
        (after, array),
        "hh",
        to="h",
        alias={1: 0},
        room=room,
    )


def rows(queries, keys, values):
    outs = [((QUADS, POS, HD), bf16), ((HEADS, POS, HD), f32), ((2, POS, 128), f32)]
    return call(
        rows_kernel,
        outs,
        (queries, keys, values),
        "hhh",
        to="h",
        scratch=[pltpu.VMEM((POS, QUADS * 4 * HD), bf16)] * 3
        + [pltpu.VMEM(*out) for out in outs]
        + [dma(13)],
        flops=24 * 4 * 128 * 128 * 128,
        moved=5 * mib,
        exps=24 * 128 * 128,
    )


def columns(core, items, other):
    return call(
        column_kernel,
        [((4, 256, HD), bf16)],
        (core, items, other),
        "svv",
        to="h",
        scratch=[
            pltpu.VMEM((4, 256, HD), bf16),
            pltpu.VMEM((1024, HD), bf16),
            pltpu.VMEM((2, 1024, HD), bf16),
            pltpu.VMEM((2, 1024, HD), bf16),
            dma(4),
        ],
        room=46_000_000,
        flops=4 * 1024 * 1280 * 128,
        moved=2 * mib,
        exps=1024 * 1280,
    )


def far_part(pair, heads, summary):
    return call(
        far_kernel,
        [((HEADS, PAY, HD), bf16)],
        (pair, heads, summary),
        "shh",
        to="h",
        scratch=[
            pltpu.VMEM((HEADS, POS, HD), bf16),
            pltpu.VMEM((8, 2, 256, HD), bf16),
            pltpu.VMEM((HEADS, PAY, HD), bf16),
            pltpu.VMEM((2048 // FAR_K, FAR_Q, FAR_K), f32),
            dma(2 + FAR_BLOCKS),
        ],
        flops=8 * 1024 * 2048 * 128,
        moved=3 * mib,
        exps=2 * 1024 * 2048,
    )


def place(column, row_out):
    return call(
        place_kernel,
        [((POS, QUADS * 4 * HD), bf16)],
        (column, row_out),
        "hh",
        to="h",
        scratch=[
            pltpu.VMEM((4, 256, HD), bf16),
            pltpu.VMEM((QUADS, POS, HD), bf16),
            pltpu.VMEM((QUADS, POS, 2 * HD), bf16),
            dma(10),
        ],
        room=46_000_000,
        flops=2 * 8 * 128 * 128 * 128,
        moved=mib,
    )


def merge(placed, far, part, stat):
    return call(
        merge_kernel,
        [((POS, QUADS * 4 * HD), bf16)],
        (placed, far, part, stat),
        "hhhh",
        to="h",
        scratch=[
            pltpu.VMEM((HEADS, PAY, HD), bf16),
            pltpu.VMEM((HEADS, POS, HD), f32),
            pltpu.VMEM((2, POS, 128), f32),
            pltpu.VMEM((QUADS, POS, 2 * HD), bf16),
            dma(14),
        ],
        alias={0: 0},
        room=2_300_000,
        flops=2 * 8 * 128 * 128 * 128,
        moved=3 * mib,
    )


def body(queries, keys, values):
    heads_at = ("w", "c", "x")
    plane = ("u", "v", "w", "c", "x")
    wide = ("z", "u", "v", "w", "x")
    back = ("x", "z", "u", "v", "w")
    summary = exchange(pack_summary(keys, values), plane)
    items, heads = pack(queries, keys, values)
    items = ordered(summary, items, room=1_700_000)
    summary = summary.reshape(64, 2, ROWS, HD).transpose(1, 0, 2, 3).reshape(1, 2, 256, HD)
    summary = lax.all_gather(summary, "z", axis=0, tiled=True)
    items = exchange(items.reshape(768, ROWS, HD), wide).reshape(3072, HD)
    row_out, part, stat = rows(queries, keys, values)
    items = ordered(stat, items)
    heads = exchange(ordered(stat, heads), heads_at)
    other = lax.ppermute(items, "c", [(0, 1), (1, 0)])
    core = lax.axis_index("c").astype(jnp.int32).reshape(1)
    column = columns(core, items, other)
    column = exchange(column.reshape(256, ROWS, HD), back).reshape(4, 256, HD)
    pair = lax.axis_index(("z", "u", "v")).astype(jnp.int32).reshape(1)
    far = exchange(far_part(pair, heads, summary), heads_at)
    return merge(place(column, row_out), far, part, stat)


def solution(mesh):
    fine = Mesh(mesh.devices.reshape(4, 8, 2, 2, 2, 2), ("x", "z", "u", "v", "w", "c"))
    spec = P(("z", "u", "v", "w", "c", "x"), None)
    return jax.shard_map(
        body, mesh=fine, in_specs=(spec, spec, spec), out_specs=spec, check_vma=False
    )
```

```python
import math

import jax
import jax.numpy as jnp
from jax import lax
from jax.experimental import pallas as pl
from jax.experimental.pallas import tpu as pltpu
from jax.sharding import Mesh
from jax.sharding import PartitionSpec as P

HD = 128
STRIDE = 32
QUADS = 8
POS = 128
ROWS = 4
LOW = -1e30
SCALE = math.log2(math.e) / math.sqrt(HD)
SUM_ROWS = 16
PAY = POS + SUM_ROWS
HEADS = 16
PAIR = HEADS * POS

f32 = jnp.float32
bf16 = jnp.bfloat16


def dot_t(a, b):
    return lax.dot_general(a, b, (((1,), (1,)), ((), ())), preferred_element_type=f32)


def dot_tl(a, b):
    return lax.dot_general(a, b, (((0,), (0,)), ((), ())), preferred_element_type=f32)


def dot(a, b):
    return lax.dot_general(a, b, (((1,), (0,)), ((), ())), preferred_element_type=f32)


def iota(shape, dim):
    return lax.broadcasted_iota(jnp.int32, shape, dim)


def one_hot(rows, cols, source):
    row = iota((rows, cols), 0)
    col = iota((rows, cols), 1)
    return jnp.where(source(row) == col, 1.0, 0.0).astype(bf16)


def div12(o):
    return (o * 5462) >> 16


def head(ref, quad, kind):
    start = (quad * 4 + kind) * HD
    return ref[:, start : start + HD]


def pack_summary_kernel(k_ref, v_ref, sum_hbm, buf, sum_ref, sems):
    moves = []
    for a, ref in enumerate((k_ref, v_ref)):
        for r in range(ROWS):
            move = pltpu.make_async_copy(
                ref.at[pl.ds(r * STRIDE + 16, 16), :],
                buf.at[pl.ds((a * ROWS + r) * 16, 16), :],
                sems.at[a * ROWS + r],
            )
            move.start()
            moves.append(move)
    pick = one_hot(8, 128, lambda o: o * 16 + 15)
    for move in moves:
        move.wait()
    for g in range(HEADS):
        rows = dot(pick, head(buf, g // 2, 2 + g % 2)).astype(bf16)
        sum_ref[g] = rows
    moves = []
    for t in range(sum_hbm.shape[0] // HEADS):
        move = pltpu.make_async_copy(
            sum_ref, sum_hbm.at[pl.ds(t * HEADS, HEADS)], sems.at[2 * ROWS + t]
        )
        move.start()
        moves.append(move)
    for move in moves:
        move.wait()


def pack_kernel(q_hbm, k_hbm, v_hbm, item_hbm, query_hbm, qs, ks, vs, items, heads, ins, outs):
    def source(o):
        col = div12(o)
        rest = o - 12 * col
        return (rest >> 2) * POS + (rest & 3) * STRIDE + col

    def fetch(quad):
        at = quad * 4 * HD
        return [
            pltpu.make_async_copy(
                q_hbm.at[:, pl.ds(at + HD, 3 * HD)], qs.at[quad], ins.at[quad * 3]
            ),
            pltpu.make_async_copy(
                k_hbm.at[:, pl.ds(at + HD, HD)], ks.at[quad], ins.at[quad * 3 + 1]
            ),
            pltpu.make_async_copy(
                v_hbm.at[:, pl.ds(at + HD, HD)], vs.at[quad], ins.at[quad * 3 + 2]
            ),
        ]

    for quad in range(QUADS):
        for move in fetch(quad):
            move.start()
    perm = one_hot(384, 384, source)
    moves = []
    for quad in range(QUADS):
        for move in fetch(quad):
            move.wait()
        stack = jnp.concatenate([qs[quad, :, :HD], ks[quad], vs[quad]], axis=0)
        items[quad] = dot(perm, stack).astype(bf16)
        heads[quad * 2] = qs[quad, :, HD : 2 * HD]
        heads[quad * 2 + 1] = qs[quad, :, 2 * HD :]
        two = pl.ds(quad * 2, 2)
        for move in (
            pltpu.make_async_copy(items.at[quad], item_hbm.at[quad], outs.at[quad * 2]),
            pltpu.make_async_copy(heads.at[two], query_hbm.at[two], outs.at[quad * 2 + 1]),
        ):
            move.start()
            moves.append(move)
    for move in moves:
        move.wait()


def order_kernel(after_ref, array_ref, out_ref):
    pass


def rows_kernel(
    q_hbm, k_hbm, v_hbm, row_hbm, part_hbm, stat_hbm,
    q_ref, k_ref, v_ref, row_ref, part_ref, stat_ref, sems,
):
    ins = []
    for a, (hbm, ref) in enumerate(((q_hbm, q_ref), (k_hbm, k_ref), (v_hbm, v_ref))):
        move = pltpu.make_async_copy(hbm, ref, sems.at[a])
        move.start()
        ins.append(move)
    pos = iota((POS, POS), 0)
    key = iota((POS, POS), 1)
    visible = jnp.logical_and((key >> 5) == (pos >> 5), key <= pos)
    tops = jnp.zeros((POS, POS), f32)
    sums = jnp.ones((POS, POS), f32)
    for move in ins:
        move.wait()
    moves = []
    for quad in range(QUADS):
        for kind in (0, 2, 3):
            s = dot_t(head(q_ref, quad, kind), head(k_ref, quad, kind)) * SCALE
            s = jnp.where(visible, s, LOW)
            m = jnp.max(s, axis=1, keepdims=True)
            p = jnp.where(visible, jnp.exp2(s - m), 0.0)
            total = jnp.sum(p, axis=1, keepdims=True)
            acc = dot(p.astype(bf16), head(v_ref, quad, kind))
            if kind == 0:
                row_ref[quad] = (acc / total).astype(bf16)
            else:
                slot = quad * 2 + kind - 2
                part_ref[slot] = acc
                tops = jnp.where(key == slot, m, tops)
                sums = jnp.where(key == slot, total, sums)
        two = pl.ds(quad * 2, 2)
        moves.append(pltpu.make_async_copy(part_ref.at[two], part_hbm.at[two], sems.at[3 + quad]))
        moves[-1].start()
    stat_ref[0] = tops
    stat_ref[1] = sums
    moves.append(pltpu.make_async_copy(row_ref, row_hbm, sems.at[11]))
    moves.append(pltpu.make_async_copy(stat_ref, stat_hbm, sems.at[12]))
    moves[-1].start()
    moves[-2].start()
    for move in moves:
        move.wait()


def column_kernel(
    core_ref, own_ref, other_ref, out_hbm, out_scr, q_scr, k_scr, v_scr, sems
):
    core = core_ref[0]

    def source(o):
        within = o & 31
        return (within >> 2) * 12 + (o >> 5) * 4 + (within & 3)

    split = one_hot(96, 96, source)
    split_kv = one_hot(64, 96, lambda o: source(o + 32))
    by_x = one_hot(POS, POS, lambda o: ((o >> 2) & 7) * 16 + (o >> 5) * 4 + (o & 3))
    for g in range(32):
        at = slice(g * 32, (g + 1) * 32)
        y = dot(split, own_ref[g * 96 : (g + 1) * 96, :]).astype(bf16)
        q_scr[at, :] = y[0:32]
        k_scr[0, at, :] = y[32:64]
        v_scr[0, at, :] = y[64:96]
        y = dot(split_kv, other_ref[g * 96 : (g + 1) * 96, :]).astype(bf16)
        k_scr[1, at, :] = y[0:32]
        v_scr[1, at, :] = y[32:64]

    block = 256
    jq = iota((block, block), 0)
    jk = iota((block, block), 1)
    visible = (jk <= jq, (jk >> 4) < (jq >> 4) + core)
    moves = []
    for qb in range(1024 // block):
        q = q_scr[qb * block : (qb + 1) * block, :]
        pieces = []
        top = None
        for kb in range(qb + 1):
            for c in range(2):
                s = dot_t(q, k_scr[c, kb * block : (kb + 1) * block, :]) * SCALE
                if kb == qb:
                    s = jnp.where(visible[c], s, LOW)
                fold = jnp.maximum(s[:, :128], s[:, 128:])
                top = fold if top is None else jnp.maximum(top, fold)
                pieces.append((kb, c, s))
        m = jnp.max(top, axis=1, keepdims=True)
        total = jnp.zeros((block, 128), f32)
        acc = jnp.zeros((block, HD), f32)
        for kb, c, s in pieces:
            p = jnp.exp2(s - m)
            total = total + (p[:, :128] + p[:, 128:])
            acc = acc + dot(p.astype(bf16), v_scr[c, kb * block : (kb + 1) * block, :])
        total = jnp.sum(total, axis=1, keepdims=True)
        out = (acc / total).astype(bf16)
        for t in range(block // POS):
            y = dot(by_x, out[t * POS : (t + 1) * POS]).astype(bf16)
            at = (qb * block // POS + t) * STRIDE
            for x in range(4):
                out_scr[x, at : at + STRIDE, :] = y[x * STRIDE : (x + 1) * STRIDE]
        at = pl.ds(qb * block // 4, block // 4)
        move = pltpu.make_async_copy(out_scr.at[:, at, :], out_hbm.at[:, at, :], sems.at[qb])
        move.start()
        moves.append(move)
    for move in moves:
        move.wait()


FAR_Q = 1024
FAR_K = 2048
FAR_BLOCKS = PAIR // FAR_Q


def far_kernel(pair_ref, q_hbm, kv_hbm, out_hbm, q_ref, kv_ref, out_ref, s_scr, sems):
    pair = pair_ref[0]
    ins = [
        pltpu.make_async_copy(q_hbm, q_ref, sems.at[0]),
        pltpu.make_async_copy(kv_hbm, kv_ref, sems.at[1]),
    ]
    for move in ins:
        move.start()
    row_ids = PAIR // STRIDE
    last = (pair * row_ids) // FAR_K
    lane = iota((POS, 128), 1)
    eye = one_hot(SUM_ROWS, 128, lambda o: o)
    per = FAR_Q // POS
    planes = FAR_K // 256

    for move in ins:
        move.wait()

    def send(b):
        at = pl.ds(b * per, per)
        return pltpu.make_async_copy(out_ref.at[at], out_hbm.at[at], sems.at[2 + b])

    def piece(i, j):
        return jnp.concatenate([kv_ref[i * planes + t, j] for t in range(planes)], axis=0)

    def fold(x, op):
        r = x[:, :128]
        for t in range(1, FAR_K // 128):
            r = op(r, x[:, t * 128 : (t + 1) * 128])
        return r

    def block(b, unused):
        q = q_ref[pl.ds(b * per, per)].reshape(FAR_Q, HD)

        def score(i, top):
            s = dot_t(q, piece(i, 0)) * SCALE
            s_scr[i] = s
            return jnp.maximum(top, fold(s, jnp.maximum))

        top = lax.fori_loop(0, last, score, jnp.full((FAR_Q, 128), LOW, f32))
        s = dot_t(q, piece(last, 0)) * SCALE
        row_k = last * FAR_K + iota((FAR_Q, FAR_K), 1)
        row_q = pair * row_ids + ((b * FAR_Q + iota((FAR_Q, FAR_K), 0)) >> 5)
        s = jnp.where(row_k < row_q, s, LOW)
        s_scr[last] = s
        top = jnp.maximum(top, fold(s, jnp.maximum))
        m = jnp.max(top, axis=1, keepdims=True)

        def weigh(i, carried):
            total, acc = carried
            p = jnp.exp2(s_scr[i] - m)
            return (
                total + fold(p, jnp.add),
                acc + dot(p.astype(bf16), piece(i, 1)),
            )

        total, acc = lax.fori_loop(
            0,
            last + 1,
            weigh,
            (jnp.zeros((FAR_Q, 128), f32), jnp.zeros((FAR_Q, HD), f32)),
        )
        total = jnp.sum(total, axis=1, keepdims=True)
        out = (acc / total).astype(bf16)
        lse = jnp.where(m > 0.5 * LOW, m + jnp.log2(total), LOW)
        high = lse.astype(bf16).astype(f32)
        left = lse - high
        mid = left.astype(bf16).astype(f32)
        low = left - mid
        for e in range(per):
            at = slice(e * POS, (e + 1) * POS)
            terms = jnp.where(
                lane == 0,
                high[at],
                jnp.where(lane == 1, mid[at], jnp.where(lane == 2, low[at], 0.0)),
            ).astype(bf16)
            out_ref[b * per + e, :POS, :] = out[at]
            out_ref[b * per + e, POS:, :] = dot_t(eye, terms).astype(bf16)
        send(b).start()
        return unused

    lax.fori_loop(0, FAR_BLOCKS, block, 0)
    for b in range(FAR_BLOCKS):
        send(b).wait()


def place_kernel(col_hbm, row_hbm, out_hbm, col_ref, row_ref, out_ref, sems):
    ins = [
        pltpu.make_async_copy(col_hbm, col_ref, sems.at[0]),
        pltpu.make_async_copy(row_hbm, row_ref, sems.at[1]),
    ]
    for move in ins:
        move.start()
    back = one_hot(
        POS, POS, lambda o: (o & 3) * STRIDE + ((o >> 2) & 7) * 4 + (o >> 5)
    )
    for move in ins:
        move.wait()
    moves = []
    for quad in range(QUADS):
        out_ref[quad, :, :HD] = row_ref[quad]
        stack = jnp.concatenate(
            [col_ref[x, quad * STRIDE : (quad + 1) * STRIDE, :] for x in range(4)], axis=0
        )
        out_ref[quad, :, HD:] = dot(back, stack).astype(bf16)
        move = pltpu.make_async_copy(
            out_ref.at[quad], out_hbm.at[:, pl.ds(quad * 4 * HD, 2 * HD)], sems.at[2 + quad]
        )
        move.start()
        moves.append(move)
    for move in moves:
        move.wait()


def merge_kernel(
    placed_hbm, far_hbm, part_hbm, stat_hbm, out_hbm, far_ref, part_ref, stat_ref, out_ref, sems
):
    ins = [
        pltpu.make_async_copy(far_hbm, far_ref, sems.at[0]),
        pltpu.make_async_copy(stat_hbm, stat_ref, sems.at[1]),
    ]
    for g in range(0, HEADS, 4):
        some = pl.ds(g, 4)
        ins.append(
            pltpu.make_async_copy(part_hbm.at[some], part_ref.at[some], sems.at[2 + g // 4])
        )
    for move in ins:
        move.start()
    row = iota((HEADS * SUM_ROWS, 128), 0)
    lane = iota((HEADS * SUM_ROWS, 128), 1)
    pick = jnp.where(
        jnp.logical_and((row >> 4) == lane, (row & 15) < 3), 1.0, 0.0
    ).astype(bf16)
    ins[0].wait()
    ins[1].wait()
    terms = jnp.concatenate([far_ref[g, POS:, :] for g in range(HEADS)], axis=0)
    lse = dot_tl(terms, pick)
    top = jnp.maximum(stat_ref[0], lse)
    own = jnp.exp2(stat_ref[0] - top)
    far = jnp.exp2(lse - top)
    scale = 1.0 / (stat_ref[1] * own + far)
    own = own * scale
    far = far * scale
    moves = []
    for g in range(HEADS):
        if g % 4 == 0:
            ins[2 + g // 4].wait()
        merged = (
            part_ref[g] * own[:, g : g + 1]
            + far_ref[g, :POS, :].astype(f32) * far[:, g : g + 1]
        )
        quad, h = g // 2, g % 2
        out_ref[quad, :, h * HD : (h + 1) * HD] = merged.astype(bf16)
        if h == 1:
            move = pltpu.make_async_copy(
                out_ref.at[quad],
                out_hbm.at[:, pl.ds((quad * 4 + 2) * HD, 2 * HD)],
                sems.at[6 + quad],
            )
            move.start()
            moves.append(move)
    for move in moves:
        move.wait()


VMEM_BYTES = 63_000_000
SPACES = {"v": pltpu.VMEM, "s": pltpu.SMEM, "h": pl.ANY}


def call(kernel, outs, args, ins, to="v", scratch=(), flops=0, moved=0, exps=0, alias=None, room=0):
    def spec(space):
        return pl.BlockSpec(memory_space=SPACES[space])

    shapes = [jax.ShapeDtypeStruct(s, d) for s, d in outs]
    many = len(shapes) > 1
    return pl.pallas_call(
        kernel,
        out_shape=shapes if many else shapes[0],
        in_specs=[spec(space) for space in ins],
        out_specs=[spec(to)] * len(shapes) if many else spec(to),
        scratch_shapes=list(scratch),
        input_output_aliases=alias or {},
        compiler_params=pltpu.CompilerParams(vmem_limit_bytes=VMEM_BYTES - room),
        cost_estimate=pl.CostEstimate(flops=flops, bytes_accessed=moved, transcendentals=exps),
    )(*args)


def exchange(array, axes):
    return lax.all_to_all(array, axes, split_axis=0, concat_axis=0, tiled=True)


def dma(n):
    return pltpu.SemaphoreType.DMA((n,))


mib = 1 << 20


def pack_summary(keys, values):
    return call(
        pack_summary_kernel,
        [((64, 8, HD), bf16)],
        (keys, values),
        "hh",
        to="h",
        scratch=[
            pltpu.VMEM((128, QUADS * 4 * HD), bf16),
            pltpu.VMEM((HEADS, 8, HD), bf16),
            dma(12),
        ],
        flops=2 * 16 * 16 * 128 * 128,
        moved=mib,
    )


def pack(queries, keys, values):
    return call(
        pack_kernel,
        [((QUADS, 384, HD), bf16), ((HEADS, POS, HD), bf16)],
        (queries, keys, values),
        "hhh",
        to="h",
        scratch=[
            pltpu.VMEM((QUADS, POS, 3 * HD), bf16),
            pltpu.VMEM((QUADS, POS, HD), bf16),
            pltpu.VMEM((QUADS, POS, HD), bf16),
            pltpu.VMEM((QUADS, 384, HD), bf16),
            pltpu.VMEM((HEADS, POS, HD), bf16),
            dma(24),
            dma(16),
        ],
        flops=2 * 8 * 384 * 384 * 128,
        moved=4 * mib,
    )


def ordered(after, array, room=46_000_000):
    return call(
        order_kernel,
        [(array.shape, array.dtype)],
        (after, array),
        "hh",
        to="h",
        alias={1: 0},
        room=room,
    )


def rows(queries, keys, values):
    outs = [((QUADS, POS, HD), bf16), ((HEADS, POS, HD), f32), ((2, POS, 128), f32)]
    return call(
        rows_kernel,
        outs,
        (queries, keys, values),
        "hhh",
        to="h",
        scratch=[pltpu.VMEM((POS, QUADS * 4 * HD), bf16)] * 3
        + [pltpu.VMEM(*out) for out in outs]
        + [dma(13)],
        flops=24 * 4 * 128 * 128 * 128,
        moved=5 * mib,
        exps=24 * 128 * 128,
    )


def columns(core, items, other):
    return call(
        column_kernel,
        [((4, 256, HD), bf16)],
        (core, items, other),
        "svv",
        to="h",
        scratch=[
            pltpu.VMEM((4, 256, HD), bf16),
            pltpu.VMEM((1024, HD), bf16),
            pltpu.VMEM((2, 1024, HD), bf16),
            pltpu.VMEM((2, 1024, HD), bf16),
            dma(4),
        ],
        room=46_000_000,
        flops=4 * 1024 * 1280 * 128,
        moved=2 * mib,
        exps=1024 * 1280,
    )


def far_part(pair, heads, summary):
    return call(
        far_kernel,
        [((HEADS, PAY, HD), bf16)],
        (pair, heads, summary),
        "shh",
        to="h",
        scratch=[
            pltpu.VMEM((HEADS, POS, HD), bf16),
            pltpu.VMEM((8, 2, 256, HD), bf16),
            pltpu.VMEM((HEADS, PAY, HD), bf16),
            pltpu.VMEM((2048 // FAR_K, FAR_Q, FAR_K), f32),
            dma(2 + FAR_BLOCKS),
        ],
        flops=8 * 1024 * 2048 * 128,
        moved=3 * mib,
        exps=2 * 1024 * 2048,
    )


def place(column, row_out):
    return call(
        place_kernel,
        [((POS, QUADS * 4 * HD), bf16)],
        (column, row_out),
        "hh",
        to="h",
        scratch=[
            pltpu.VMEM((4, 256, HD), bf16),
            pltpu.VMEM((QUADS, POS, HD), bf16),
            pltpu.VMEM((QUADS, POS, 2 * HD), bf16),
            dma(10),
        ],
        room=46_000_000,
        flops=2 * 8 * 128 * 128 * 128,
        moved=mib,
    )


def merge(placed, far, part, stat):
    return call(
        merge_kernel,
        [((POS, QUADS * 4 * HD), bf16)],
        (placed, far, part, stat),
        "hhhh",
        to="h",
        scratch=[
            pltpu.VMEM((HEADS, PAY, HD), bf16),
            pltpu.VMEM((HEADS, POS, HD), f32),
            pltpu.VMEM((2, POS, 128), f32),
            pltpu.VMEM((QUADS, POS, 2 * HD), bf16),
            dma(14),
        ],
        alias={0: 0},
        room=46_000_000,
        flops=2 * 8 * 128 * 128 * 128,
        moved=3 * mib,
    )


def body(queries, keys, values):
    heads_at = ("w", "c", "x")
    plane = ("u", "v", "w", "c", "x")
    wide = ("z", "u", "v", "w", "x")
    back = ("x", "z", "u", "v", "w")
    summary = exchange(pack_summary(keys, values), plane)
    items, heads = pack(queries, keys, values)
    items = ordered(summary, items, room=0)
    summary = summary.reshape(64, 2, ROWS, HD).transpose(1, 0, 2, 3).reshape(1, 2, 256, HD)
    summary = lax.all_gather(summary, "z", axis=0, tiled=True)
    items = exchange(items.reshape(768, ROWS, HD), wide).reshape(3072, HD)
    row_out, part, stat = rows(queries, keys, values)
    items = ordered(stat, items)
    heads = exchange(ordered(stat, heads), heads_at)
    other = lax.ppermute(items, "c", [(0, 1), (1, 0)])
    core = lax.axis_index("c").astype(jnp.int32).reshape(1)
    column = columns(core, items, other)
    column = exchange(column.reshape(256, ROWS, HD), back).reshape(4, 256, HD)
    pair = lax.axis_index(("z", "u", "v")).astype(jnp.int32).reshape(1)
    far = exchange(far_part(pair, heads, summary), heads_at)
    return merge(place(column, row_out), far, part, stat)


def solution(mesh):
    fine = Mesh(mesh.devices.reshape(4, 8, 2, 2, 2, 2), ("x", "z", "u", "v", "w", "c"))
    spec = P(("z", "u", "v", "w", "c", "x"), None)
    return jax.shard_map(
        body, mesh=fine, in_specs=(spec, spec, spec), out_specs=spec, check_vma=False
    )
```
